128 devices in a mesh: dev: 128 (over x, z, y, core).
Axes of the slice: x: 4, y: 4, z: 4, core: 2. Of those that a mesh axis runs over, the one named last changes fastest.
Arguments:
- gauss_params: float32 [59, 1048576], P(None, 'dev'), may hold values from -8 to 8, as said below
- adam_first: float32 [59, 1048576], P(None, 'dev'), may hold values from -6 to 6
- adam_second: float32 [59, 1048576], P(None, 'dev'), may hold values from 0.0001 to 100
- camera: float32 [2, 6], replicated, may hold values from -0.004 to 0.004
- send_first: int32 [128, 4096], P('dev'), may hold values from -1 to 8191, as said below
- send_second: int32 [128, 4096], P('dev'), may hold values from -1 to 8191, as said below
- lists_first: int32 [4096, 128], P('dev'), may hold values from -1 to 4095, as said below
- lists_second: int32 [4096, 128], P('dev'), may hold values from -1 to 4095, as said below
- tiles_first: int32 [4096], P('dev'), may hold values from 0 to 4095, as said below
- tiles_second: int32 [4096], P('dev'), may hold values from 0 to 4095, as said below
- targets: float32 [4096, 3, 256], P('dev'), may hold values from 0 to 1
Outputs:
- new_params: float32 [59, 1048576], P(None, 'dev')
- new_first: float32 [59, 1048576], P(None, 'dev')
- new_second: float32 [59, 1048576], P(None, 'dev')
- rendered_next: float32 [4096, 3, 256], P('dev')
The draws below stay inside these ranges and needn't reach their ends.
Inputs may be any that keep to these rules, and one draw needn't show every extreme that they name: `gauss_params`: rows 0 to 2 hold a position, 3 to 5 log scales, 6 to 9 a quaternion (w, x, y, z) with w at least 1, 10 an opacity logit, 11 + 16 c + k the spherical-harmonic coefficient k of colour c. Every Gaussian lies at depth 1.4 or more in front of both cameras. `send_first`: row s holds, for each destination d in turn, 32 slots: local column indices of Gaussians of device s, the used ones first, then -1. Entries other than -1 in a row are distinct. Some destination gets 32 used slots from every device. `send_second`: same form as send_first, but unused slots (-1) may stand anywhere in a destination's run. Some destination gets 32 used slots from every device. `lists_first`: row r, rendered by device r // 32, lists in compositing order (front first) received slots s * 32 + k of that device (slot k from device s), only used slots, then -1 to the end. Every used slot of a device appears exactly once among its rows. Some rows have no -1. `lists_second`: same form as lists_first, for the next view and its send array. `tiles_first`: A permutation of the image's tiles. `tiles_second`: A permutation of the image's tiles.
All inputs are finite; a program needn't handle non-finite values.
Results may differ from the reference program's by a relative error of at most 0.0003.
Values sent between devices are 32-bit elements; how exact they have to be, the bound alone decides.
A program may use at most 128 MiB of HBM per device.

```python
import math
import jax
import jax.numpy as jnp
import numpy as np
from jax import lax

PARAMS = 59
LIST_LEN = 128
TILE_PIXELS = 256
TILES_X = 128
TILE_DEV = 32
G_DEV = 8192
CAP = 32
TILES = 4096
GAUSS = 1048576
N_DEV = 128


def routing_tables(key):
    base = jax.random.fold_in(key, 911)
    key_list = jax.random.split(base, 7)
    half_cap = CAP // 2
    received = N_DEV * CAP
    device_ids = jnp.arange(N_DEV, dtype=jnp.int32)
    level_table = jnp.array([1, 1, 1, 1, 1, 2, 2, 4], jnp.int32)
    load_level = level_table[jax.random.randint(key_list[0], (N_DEV,), 0, 8)]
    ranking = jax.random.permutation(key_list[1], N_DEV).astype(jnp.int32)
    hot_first = ranking[0]
    hot_second = ranking[1]
    is_hot = (device_ids == hot_first) | (device_ids == hot_second)
    ceiling = CAP * load_level // 4
    drops = jax.random.randint(key_list[2], (N_DEV, N_DEV), 0, CAP + 1) % (ceiling // 8 + 1)[None, :]
    counts = jnp.where(is_hot[None, :], CAP, ceiling[None, :] - drops).astype(jnp.int32)
    source_keys = jax.random.split(key_list[3], N_DEV)
    local_ids = jax.vmap(lambda one_key: jax.random.permutation(one_key, G_DEV)[:received])(source_keys).astype(jnp.int32)
    run_slot = jnp.arange(received, dtype=jnp.int32) % CAP
    run_dest = jnp.arange(received, dtype=jnp.int32) // CAP
    used = run_slot[None, :] < counts[:, run_dest]
    send_first = jnp.where(used, local_ids, -1).astype(jnp.int32)
    tiles_first = jax.random.permutation(key_list[4], TILES).astype(jnp.int32)

    def device_lists(device_key, count_column):
        slot_ids = jnp.arange(received, dtype=jnp.int32)
        source_of = slot_ids // CAP
        slot_of = slot_ids % CAP
        half_of = slot_of // half_cap
        within = source_of * half_cap + slot_of - half_of * half_cap
        half_size = N_DEV * half_cap
        order_low = jax.random.permutation(jax.random.fold_in(device_key, 1), half_size).astype(jnp.int32)
        order_high = jax.random.permutation(jax.random.fold_in(device_key, 2), half_size).astype(jnp.int32)
        place = jnp.where(half_of == 0, order_low[within], half_size + order_high[within]).astype(jnp.int32)
        live = (slot_of < count_column[source_of]).astype(jnp.int32)
        entries = jnp.zeros((received,), jnp.int32).at[place].set(slot_ids).reshape(TILE_DEV, LIST_LEN)
        live_at = jnp.zeros((received,), jnp.int32).at[place].set(live).reshape(TILE_DEV, LIST_LEN)
        sort_key = (1 - live_at) * LIST_LEN + jnp.arange(LIST_LEN, dtype=jnp.int32)[None, :]
        order = jnp.argsort(sort_key, axis=1)
        entries = jnp.take_along_axis(entries, order, axis=1)
        live_at = jnp.take_along_axis(live_at, order, axis=1)
        return (jnp.where(live_at == 1, entries, -1).astype(jnp.int32), place)
    lists_all, places = jax.vmap(device_lists)(jax.random.split(key_list[5], N_DEV), counts.T)
    lists_first = lists_all.reshape(TILES, LIST_LEN)
    tile_rows = device_ids[:, None] * TILE_DEV + places // LIST_LEN
    tile_of_slot = tiles_first[tile_rows]
    by_source = jnp.transpose(tile_of_slot.reshape(N_DEV, N_DEV, CAP), (1, 0, 2)).reshape(N_DEV, received)
    home = jax.random.randint(key_list[6], (N_DEV, G_DEV), 0, TILES).astype(jnp.int32)
    home = home.at[device_ids[:, None], local_ids].set(by_source)
    loads = jnp.sum(counts, axis=0)
    score = loads + is_hot.astype(jnp.int32) * (N_DEV * CAP) + (device_ids == hot_first).astype(jnp.int32) * (N_DEV * CAP)
    descending = jnp.argsort(-(score * N_DEV + device_ids)).astype(jnp.int32)
    ascending = descending[::-1]
    previous = ascending[0]
    pair_high = ascending.at[0].set(descending[1]).at[N_DEV - 2].set(previous)
    pair_low = descending
    source_dest = jnp.where(run_slot < half_cap, pair_low[run_dest], pair_high[run_dest])
    send_second = send_first[:, source_dest * CAP + run_slot].astype(jnp.int32)
    row_ids = jnp.arange(TILES, dtype=jnp.int32)
    row_owner = row_ids // TILE_DEV
    row_within = row_ids % TILE_DEV
    from_device = jnp.where(row_within < TILE_DEV // 2, pair_low[row_owner], pair_high[row_owner])
    source_rows = from_device * TILE_DEV + row_within
    tiles_second = tiles_first[source_rows].astype(jnp.int32)
    lists_second = lists_first[source_rows].astype(jnp.int32)
    return (send_first, send_second, lists_first, lists_second, tiles_first, tiles_second, home.reshape(-1))


def draw_send_first(key, part):
    return routing_tables(key)[0]


def draw_send_second(key, part):
    return routing_tables(key)[1]


def draw_lists_first(key, part):
    return routing_tables(key)[2]


def draw_lists_second(key, part):
    return routing_tables(key)[3]


def draw_tiles_first(key, part):
    return routing_tables(key)[4]


def draw_tiles_second(key, part):
    return routing_tables(key)[5]


def draw_gauss_params(key, part):
    home = routing_tables(key)[6]
    float_keys = jax.random.split(jax.random.fold_in(key, 4242), 9)
    number = N_DEV * G_DEV
    image_width = TILES_X * 16.0
    image_height = TILES // TILES_X * 16.0
    across = (home % TILES_X).astype(jnp.float32) * 16.0 + jax.random.uniform(float_keys[0], (number,), jnp.float32, 0.0, 16.0)
    downward = (home // TILES_X).astype(jnp.float32) * 16.0 + jax.random.uniform(float_keys[1], (number,), jnp.float32, 0.0, 16.0)
    distance = jax.random.uniform(float_keys[2], (number,), jnp.float32, 2.0, 4.0)
    log_scales = jax.random.uniform(float_keys[3], (3, number), jnp.float32, -5.3, -4.3)
    logits = jax.random.uniform(float_keys[5], (1, number), jnp.float32, -4.0, 0.0)
    base_terms = jnp.clip(1.2 * jax.random.normal(float_keys[6], (3, 1, number), jnp.float32), -3.0, 3.0)
    high_terms = jnp.clip(0.25 * jax.random.normal(float_keys[7], (3, 15, number), jnp.float32), -1.0, 1.0)
    position_x = (across - 0.5 * image_width) * distance / 1000.0
    position_y = (downward - 0.5 * image_height) * distance / 1000.0
    versor = jnp.concatenate([jax.random.uniform(float_keys[4], (1, number), jnp.float32, 1.0, 2.0), jax.random.uniform(float_keys[8], (3, number), jnp.float32, -1.0, 1.0)])
    harmonics = jnp.concatenate([base_terms, high_terms], axis=1).reshape(48, number)
    return jnp.concatenate([jnp.stack([position_x, position_y, distance]), log_scales, versor, logits, harmonics]).astype(jnp.float32)


def levels(own_key, extent, cuts, smallest, largest):
    loudness = 1.0
    for axis_at, blocks in cuts:
        heights = jax.random.uniform(jax.random.fold_in(jax.random.fold_in(own_key, 6), axis_at), (blocks,), jnp.float32, smallest / len(cuts), largest / len(cuts))
        loudness = loudness * jnp.repeat(jnp.exp(heights), extent[axis_at] // blocks).reshape((-1,) + (1,) * (len(extent) - 1 - axis_at))
    return loudness


def bell_draw(stream_key, extent, scale, most, pieces=(), kind=jnp.bfloat16):
    gain = levels(stream_key, extent, pieces, -0.22, 0.18) if pieces else 1.0
    values = jax.random.normal(stream_key, extent, jnp.float32) * scale * gain
    return jnp.minimum(jnp.maximum(values, -most), most).astype(kind)


def setup_inputs(seed: int = 0) -> dict:
    streams_of = jax.random.split(jax.random.key(seed), 12)
    gauss_params = draw_gauss_params(jax.random.fold_in(streams_of[11], 71), 0)
    adam_first = bell_draw(streams_of[1], (PARAMS, GAUSS), 1.0, 6.0, ((1, 128),), jnp.float32)
    adam_second = jnp.clip(jnp.exp(math.log(100.0) - 13.815511 * jax.random.uniform(streams_of[2], (PARAMS, GAUSS), jnp.float32) ** levels(streams_of[2], (PARAMS, GAUSS), ((1, 128),), -0.2, 0.2)), 0.0001, 100.0)
    camera = jnp.clip(jax.random.uniform(streams_of[3], (2, 6), jnp.float32, -0.004, 0.004), -0.004, 0.004)
    send_first = draw_send_first(jax.random.fold_in(streams_of[11], 71), 0)
    send_second = draw_send_second(jax.random.fold_in(streams_of[11], 71), 0)
    lists_first = draw_lists_first(jax.random.fold_in(streams_of[11], 71), 0)
    lists_second = draw_lists_second(jax.random.fold_in(streams_of[11], 71), 0)
    tiles_first = draw_tiles_first(jax.random.fold_in(streams_of[11], 71), 0)
    tiles_second = draw_tiles_second(jax.random.fold_in(streams_of[11], 71), 0)
    targets = jnp.clip(1.0 * jax.random.uniform(streams_of[10], (TILES, 3, TILE_PIXELS), jnp.float32) ** levels(streams_of[10], (TILES, 3, TILE_PIXELS), ((0, 128),), -0.2, 0.2), 0.0, 1.0)
    return {"gauss_params": gauss_params, "adam_first": adam_first, "adam_second": adam_second, "camera": camera, "send_first": send_first, "send_second": send_second, "lists_first": lists_first, "lists_second": lists_second, "tiles_first": tiles_first, "tiles_second": tiles_second, "targets": targets}


tile_edge = 16
focal_length = 1000.0
blur_floor = 0.3
adam_epsilon = 1e-08
bias_first = 1.0 - 0.9 ** 20
bias_second = 1.0 - 0.999 ** 20
sh_first = 0.28209479177387814
sh_second = 0.4886025119029199
sh_third = (1.0925484305920792, -1.0925484305920792, 0.31539156525252005, -1.0925484305920792, 0.5462742152960396)
sh_fourth = (-0.5900435899266435, 2.890611442640554, -0.4570457994644658, 0.3731763325901154, -0.4570457994644658, 1.445305721320277, -0.5900435899266435)

def rate_values():
    values = np.full((59,), 0.000125)
    values[0:3] = 0.00016
    values[3:6] = 0.005
    values[6:10] = 0.001
    values[10] = 0.05
    values[11] = 0.0025
    values[27] = 0.0025
    values[43] = 0.0025
    return values

def camera_frame(camera_row):
    cosine_a, sine_a = (jnp.cos(camera_row[0]), jnp.sin(camera_row[0]))
    cosine_b, sine_b = (jnp.cos(camera_row[1]), jnp.sin(camera_row[1]))
    cosine_c, sine_c = (jnp.cos(camera_row[2]), jnp.sin(camera_row[2]))
    filler_zero = jnp.zeros_like(cosine_a)
    filler_one = jnp.ones_like(cosine_a)
    turn_x = jnp.stack([jnp.stack([filler_one, filler_zero, filler_zero]), jnp.stack([filler_zero, cosine_a, -sine_a]), jnp.stack([filler_zero, sine_a, cosine_a])])
    turn_y = jnp.stack([jnp.stack([cosine_b, filler_zero, sine_b]), jnp.stack([filler_zero, filler_one, filler_zero]), jnp.stack([-sine_b, filler_zero, cosine_b])])
    turn_z = jnp.stack([jnp.stack([cosine_c, -sine_c, filler_zero]), jnp.stack([sine_c, cosine_c, filler_zero]), jnp.stack([filler_zero, filler_zero, filler_one])])
    highest = lax.Precision.HIGHEST
    rotation = jnp.dot(turn_z, jnp.dot(turn_y, turn_x, precision=highest), precision=highest)
    return (rotation, camera_row[3:6])

def sh_terms(along_x, along_y, along_z):
    square_x, square_y, square_z = (along_x * along_x, along_y * along_y, along_z * along_z)
    return [-sh_second * along_y, sh_second * along_z, -sh_second * along_x, sh_third[0] * along_x * along_y, sh_third[1] * along_y * along_z, sh_third[2] * (2.0 * square_z - square_x - square_y), sh_third[3] * along_x * along_z, sh_third[4] * (square_x - square_y), sh_fourth[0] * along_y * (3.0 * square_x - square_y), sh_fourth[1] * along_x * along_y * along_z, sh_fourth[2] * along_y * (4.0 * square_z - square_x - square_y), sh_fourth[3] * along_z * (2.0 * square_z - 3.0 * square_x - 3.0 * square_y), sh_fourth[4] * along_x * (4.0 * square_z - square_x - square_y), sh_fourth[5] * along_z * (square_x - square_y), sh_fourth[6] * along_x * (square_x - 3.0 * square_y)]

def project(params, camera_row, image_width, image_height):
    rotation, offset = camera_frame(camera_row)
    centres = params[0:3]
    viewed = [rotation[row_index, 0] * centres[0] + rotation[row_index, 1] * centres[1] + rotation[row_index, 2] * centres[2] + offset[row_index] for row_index in range(3)]
    inverse_depth = 1.0 / viewed[2]
    screen_u = focal_length * viewed[0] * inverse_depth + 0.5 * image_width
    screen_v = focal_length * viewed[1] * inverse_depth + 0.5 * image_height
    scales = jnp.exp(params[3:6])
    versor = params[6:10] / jnp.sqrt(lax.optimization_barrier(jnp.sum(params[6:10] * params[6:10], axis=0)))
    part_w, part_x, part_y, part_z = (versor[0], versor[1], versor[2], versor[3])
    turn_rows = [[1.0 - 2.0 * (part_y * part_y + part_z * part_z), 2.0 * (part_x * part_y - part_w * part_z), 2.0 * (part_x * part_z + part_w * part_y)], [2.0 * (part_x * part_y + part_w * part_z), 1.0 - 2.0 * (part_x * part_x + part_z * part_z), 2.0 * (part_y * part_z - part_w * part_x)], [2.0 * (part_x * part_z - part_w * part_y), 2.0 * (part_y * part_z + part_w * part_x), 1.0 - 2.0 * (part_x * part_x + part_y * part_y)]]
    factor = [[turn_rows[row_index][col_index] * scales[col_index] for col_index in range(3)] for row_index in range(3)]
    spread = [[factor[row_index][0] * factor[col_index][0] + factor[row_index][1] * factor[col_index][1] + factor[row_index][2] * factor[col_index][2] for col_index in range(3)] for row_index in range(3)]
    jacobian = [[focal_length * inverse_depth, 0.0, -focal_length * viewed[0] * inverse_depth * inverse_depth], [0.0, focal_length * inverse_depth, -focal_length * viewed[1] * inverse_depth * inverse_depth]]
    mapping = [[jacobian[row_index][0] * rotation[0, col_index] + jacobian[row_index][1] * rotation[1, col_index] + jacobian[row_index][2] * rotation[2, col_index] for col_index in range(3)] for row_index in range(2)]

    def mapped(first_index, second_index):
        running = 0.0
        for inner_a in range(3):
            for inner_b in range(3):
                running = running + mapping[first_index][inner_a] * spread[inner_a][inner_b] * mapping[second_index][inner_b]
        return running
    cover_a = mapped(0, 0) + blur_floor
    cover_b = mapped(0, 1)
    cover_c = mapped(1, 1) + blur_floor
    determinant = cover_a * cover_c - cover_b * cover_b
    opacity = jax.nn.sigmoid(params[10])
    centre_cam = [-(rotation[0, col_index] * offset[0] + rotation[1, col_index] * offset[1] + rotation[2, col_index] * offset[2]) for col_index in range(3)]
    towards = [centres[col_index] - centre_cam[col_index] for col_index in range(3)]
    length = jnp.sqrt(towards[0] * towards[0] + towards[1] * towards[1] + towards[2] * towards[2])
    harmonics = sh_terms(towards[0] / length, towards[1] / length, towards[2] / length)
    colours = []
    for channel in range(3):
        running = 0.5 + sh_first * params[11 + 16 * channel]
        for term_index in range(1, 16):
            running = running + harmonics[term_index - 1] * params[11 + 16 * channel + term_index]
        colours.append(jnp.maximum(running, 0.0))
    return jnp.stack([screen_u, screen_v, cover_c / determinant, -cover_b / determinant, cover_a / determinant, opacity] + colours)

def composite(gathered, live_mask, tile_numbers):
    pixel_ids = jnp.arange(TILE_PIXELS, dtype=jnp.int32)
    pixel_col = (tile_numbers % TILES_X)[:, None] * tile_edge + pixel_ids[None, :] % tile_edge
    pixel_row = (tile_numbers // TILES_X)[:, None] * tile_edge + pixel_ids[None, :] // tile_edge
    offset_x = gathered[0][:, None, :] - (pixel_col.astype(gathered.dtype) + 0.5)[:, :, None]
    offset_y = gathered[1][:, None, :] - (pixel_row.astype(gathered.dtype) + 0.5)[:, :, None]
    exponent = -0.5 * (gathered[2][:, None, :] * offset_x * offset_x + gathered[4][:, None, :] * offset_y * offset_y) - gathered[3][:, None, :] * offset_x * offset_y
    coverage = gathered[5][:, None, :] * jnp.exp(exponent) * live_mask[:, None, :]
    log_clear = jnp.log1p(-coverage)
    before = jnp.cumsum(log_clear, axis=2) - log_clear
    weight = coverage * jnp.exp(before)
    return jnp.einsum('bpi,cbi->bcp', weight, gathered[6:9], precision=lax.Precision.HIGHEST)

def gathered_splats(splats, send, tile_lists):
    slot_table = jnp.maximum(send, 0).reshape(N_DEV, N_DEV, CAP) + (jnp.arange(N_DEV, dtype=jnp.int32) * G_DEV)[:, None, None]
    slot_table = jnp.transpose(slot_table, (1, 0, 2)).reshape(N_DEV, N_DEV * CAP)
    safe_ids = jnp.maximum(tile_lists, 0).reshape(N_DEV, TILE_DEV * LIST_LEN)
    global_ids = jnp.take_along_axis(slot_table, safe_ids, axis=1).reshape(TILES * LIST_LEN)
    return jnp.take(splats, global_ids, axis=1).reshape(9, TILES, LIST_LEN)

def render_all(gathered, live_mask, tile_numbers):
    group_size = 32
    block_count = TILES // group_size
    stacked = jnp.transpose(gathered.reshape(9, block_count, group_size, LIST_LEN), (1, 0, 2, 3))
    masks = live_mask.reshape(block_count, group_size, LIST_LEN)
    numbers = tile_numbers.reshape(block_count, group_size)
    rendered = lax.map(jax.checkpoint(lambda items: composite(items[0], items[1], items[2])), (stacked, masks, numbers))
    return rendered.reshape(TILES, 3, TILE_PIXELS)

def reference(gauss_params, adam_first, adam_second, camera, send_first, send_second, lists_first, lists_second, tiles_first, tiles_second, targets):
    image_width = TILES_X * tile_edge * 1.0
    image_height = TILES // TILES_X * tile_edge * 1.0
    live_first = (lists_first >= 0).astype(gauss_params.dtype)
    live_second = (lists_second >= 0).astype(gauss_params.dtype)

    def loss_of(params):
        splats = project(params, camera[0], image_width, image_height)
        rendered = render_all(gathered_splats(splats, send_first, lists_first), live_first, tiles_first)
        return 0.5 * jnp.sum((rendered - targets) ** 2)
    gradient = jax.grad(loss_of)(gauss_params)
    new_first = 0.9 * adam_first + 0.1 * gradient
    new_second = 0.999 * adam_second + 0.001 * gradient * gradient
    step_sizes = jnp.asarray(rate_values(), gauss_params.dtype)[:, None]
    new_params = gauss_params - step_sizes * (new_first / bias_first) / (jnp.sqrt(new_second / bias_second) + adam_epsilon)
    splats_next = project(new_params, camera[1], image_width, image_height)
    rendered_next = render_all(gathered_splats(splats_next, send_second, lists_second), live_second, tiles_second)
    return (new_params, new_first, new_second, rendered_next)
```

```python
import functools

import jax
import jax.numpy as jnp
import numpy as np
from jax import lax
from jax.experimental import pallas as pl
from jax.experimental.pallas import tpu as pltpu
from jax.sharding import PartitionSpec as P

LANES = 128
TILES_X = 128
TILE_DEV = 32
LIST_LEN = 128
CHUNK = 1024
LOG2E = 1.4426950408889634

focal_length = 1000.0
blur_floor = 0.3
adam_epsilon = 1e-08
bias_first = 1.0 - 0.9**20
bias_second = 1.0 - 0.999**20
sh_first = 0.28209479177387814
sh_second = 0.4886025119029199
sh_third = (
    1.0925484305920792,
    -1.0925484305920792,
    0.31539156525252005,
    -1.0925484305920792,
    0.5462742152960396,
)
sh_fourth = (
    -0.5900435899266435,
    2.890611442640554,
    -0.4570457994644658,
    0.3731763325901154,
    -0.4570457994644658,
    1.445305721320277,
    -0.5900435899266435,
)


def rate_values():
    values = np.full((64,), 0.000125)
    values[0:3] = 0.00016
    values[3:6] = 0.005
    values[6:10] = 0.001
    values[10] = 0.05
    values[11] = 0.0025
    values[27] = 0.0025
    values[43] = 0.0025
    return np.broadcast_to(values[:, None], (64, LANES)).astype(np.float32)


def camera_frame(camera_ref, view):
    def full(k):
        return jnp.full((8, LANES), camera_ref[view, k], jnp.float32)

    ca, sa = jnp.cos(full(0)), jnp.sin(full(0))
    cb, sb = jnp.cos(full(1)), jnp.sin(full(1))
    cc, sc = jnp.cos(full(2)), jnp.sin(full(2))
    rot = [
        [cc * cb, cc * (sb * sa) - sc * ca, cc * (sb * ca) + sc * sa],
        [sc * cb, sc * (sb * sa) + cc * ca, sc * (sb * ca) - cc * sa],
        [-sb, cb * sa, cb * ca],
    ]
    shift = [full(3), full(4), full(5)]
    back = [rot[0][k] * shift[0] + rot[1][k] * shift[1] + rot[2][k] * shift[2] for k in range(3)]
    return [rot[0][0], rot[0][1], rot[0][2], rot[1][0], rot[1][1], rot[1][2],
            rot[2][0], rot[2][1], rot[2][2]] + shift + back


def sh_terms(along_x, along_y, along_z):
    square_x, square_y, square_z = (along_x * along_x, along_y * along_y, along_z * along_z)
    return [
        -sh_second * along_y,
        sh_second * along_z,
        -sh_second * along_x,
        sh_third[0] * along_x * along_y,
        sh_third[1] * along_y * along_z,
        sh_third[2] * (2.0 * square_z - square_x - square_y),
        sh_third[3] * along_x * along_z,
        sh_third[4] * (square_x - square_y),
        sh_fourth[0] * along_y * (3.0 * square_x - square_y),
        sh_fourth[1] * along_x * along_y * along_z,
        sh_fourth[2] * along_y * (4.0 * square_z - square_x - square_y),
        sh_fourth[3] * along_z * (2.0 * square_z - 3.0 * square_x - 3.0 * square_y),
        sh_fourth[4] * along_x * (4.0 * square_z - square_x - square_y),
        sh_fourth[5] * along_z * (square_x - square_y),
        sh_fourth[6] * along_x * (square_x - 3.0 * square_y),
    ]


def footprint(params, frame, half_width, half_height):
    rot = [frame[0:3], frame[3:6], frame[6:9]]
    shift, back = frame[9:12], frame[12:15]
    x, y, z = params[0], params[1], params[2]
    viewed = [rot[k][0] * x + rot[k][1] * y + rot[k][2] * z + shift[k] for k in range(3)]
    inverse_depth = 1.0 / viewed[2]
    screen_u = focal_length * viewed[0] * inverse_depth + half_width
    screen_v = focal_length * viewed[1] * inverse_depth + half_height
    scales = [jnp.exp(params[3 + k]) for k in range(3)]
    size = params[6] * params[6] + params[7] * params[7] + params[8] * params[8] + params[9] * params[9]
    unit = 1.0 / jnp.sqrt(size)
    w, i, j, k = [params[6 + n] * unit for n in range(4)]
    turn = [
        [1.0 - 2.0 * (j * j + k * k), 2.0 * (i * j - w * k), 2.0 * (i * k + w * j)],
        [2.0 * (i * j + w * k), 1.0 - 2.0 * (i * i + k * k), 2.0 * (j * k - w * i)],
        [2.0 * (i * k - w * j), 2.0 * (j * k + w * i), 1.0 - 2.0 * (i * i + j * j)],
    ]
    near = focal_length * inverse_depth
    slant_x = -near * viewed[0] * inverse_depth
    slant_y = -near * viewed[1] * inverse_depth
    mapping = [
        [near * rot[0][n] + slant_x * rot[2][n] for n in range(3)],
        [near * rot[1][n] + slant_y * rot[2][n] for n in range(3)],
    ]
    half = [
        [
            (mapping[m][0] * turn[0][n] + mapping[m][1] * turn[1][n] + mapping[m][2] * turn[2][n])
            * scales[n]
            for n in range(3)
        ]
        for m in range(2)
    ]

    def inner(p, q):
        return p[0] * q[0] + p[1] * q[1] + p[2] * q[2]

    cover_a = inner(half[0], half[0]) + blur_floor
    cover_b = inner(half[0], half[1])
    cover_c = inner(half[1], half[1]) + blur_floor
    towards = [x + back[0], y + back[1], z + back[2]]
    inverse_length = 1.0 / jnp.sqrt(inner(towards, towards))
    harmonics = sh_terms(*[t * inverse_length for t in towards])
    colours = []
    for channel in range(3):
        running = 0.5 + sh_first * params[11 + 16 * channel]
        for term in range(1, 16):
            running = running + harmonics[term - 1] * params[11 + 16 * channel + term]
        colours.append(jnp.maximum(running, 0.0))
    return (screen_u, screen_v, cover_a, cover_b, cover_c, *colours)


def conic_of(cover_a, cover_b, cover_c):
    inverse = 1.0 / (cover_a * cover_c - cover_b * cover_b)
    return cover_c * inverse, -cover_b * inverse, cover_a * inverse


def project(params, frame, half_width, half_height):
    u, w, cover_a, cover_b, cover_c, *colours = footprint(params, frame, half_width, half_height)
    return [u, w, *conic_of(cover_a, cover_b, cover_c), jax.nn.sigmoid(params[10]), *colours]


def turned(tiles):
    swapped = jnp.swapaxes(jnp.stack(tiles, axis=0), 0, 1)
    return [swapped[n] for n in range(8)]


def lane_pick(values, lanes):
    numbers = lax.GatherDimensionNumbers(
        offset_dims=(),
        collapsed_slice_dims=(1,),
        start_index_map=(1,),
        operand_batching_dims=(0,),
        start_indices_batching_dims=(0,),
    )
    return lax.gather(
        values, lanes[:, :, None], numbers, (1, 1), mode=lax.GatherScatterMode.PROMISE_IN_BOUNDS
    )


def pick(source_ref, blocks, wanted, unroll):
    count = source_ref.shape[0]
    high = [w >> 7 for w in wanted]
    low = [w & 127 for w in wanted]

    def body(block, held):
        hit = [h == block for h in high]
        out = []
        for row in range(count):
            source = jnp.broadcast_to(source_ref[row, pl.ds(block, 1), :], (8, LANES))
            for n in range(len(wanted)):
                out.append(
                    jnp.where(hit[n], lane_pick(source, low[n]), held[row * len(wanted) + n])
                )
        return tuple(out)

    start = tuple(jnp.zeros((8, LANES), jnp.float32) for _ in range(count * len(wanted)))
    flat = lax.fori_loop(0, blocks, body, start, unroll=unroll)
    return [list(flat[r * len(wanted) : (r + 1) * len(wanted)]) for r in range(count)]


def lane_block():
    return lax.broadcasted_iota(jnp.int32, (8, LANES), 1) >> 5


def block_turn(vectors):
    block = lane_block()
    out = []
    for j in range(4):
        made = None
        for i in range(4):
            shift = ((i - j) * 32) % LANES
            moved = pltpu.roll(vectors[i], shift, 1) if shift else vectors[i]
            made = moved if made is None else jnp.where(block == i, moved, made)
        out.append(made)
    return out


def pack(values, message_ref):
    nothing = jnp.zeros((8, LANES), jnp.float32)
    for g in range(4):
        for a in range(3):
            rows = [values[4 * a + b][g] if 4 * a + b < 9 else nothing for b in range(4)]
            for d, made in enumerate(block_turn(rows)):
                message_ref[8 * g : 8 * g + 8, d, a, :] = made
        for d in range(4):
            message_ref[8 * g : 8 * g + 8, d, 3, :] = nothing


def unpack(message_ref, buffer_ref):
    for g in range(4):
        for a in range(3):
            rows = [message_ref[8 * g : 8 * g + 8, d, a, :] for d in range(4)]
            for b, made in enumerate(block_turn(rows)):
                if 4 * a + b < 9:
                    buffer_ref[4 * a + b, 8 * g : 8 * g + 8, :] = made


def eight(ref, g):
    return ref[8 * g : 8 * g + 8, :]


def send_splats(splats_ref, send_ref, message_ref):
    picked = pick(splats_ref, splats_ref.shape[1], [eight(send_ref, g) for g in range(4)], 2)
    pack(picked, message_ref)


def first_kernel(camera_ref, params_ref, send_ref, message_ref, splats_ref, frame_ref, *, half):
    step = pl.program_id(0)

    @pl.when(step == 0)
    def _():
        for n, entry in enumerate(camera_frame(camera_ref, 0)):
            frame_ref[n] = entry

    rows = []
    for g in range(8):
        rows += turned([params_ref[8 * g : 8 * g + 8, LANES * c : LANES * (c + 1)] for c in range(8)])
    splats = project(rows, [frame_ref[n] for n in range(15)], *half)
    at = pl.ds(pl.multiple_of(step * 8, 8), 8)
    for n in range(9):
        splats_ref[n, at, :] = splats[n]

    @pl.when(step == pl.num_programs(0) - 1)
    def _():
        send_splats(splats_ref, send_ref, message_ref)


def inverse_of(ids_ref, blocks):
    lane = lax.broadcasted_iota(jnp.int32, (blocks, LANES), 1)
    row_id = lax.broadcasted_iota(jnp.int32, (blocks, LANES), 0)
    low_id = lax.broadcasted_iota(jnp.int32, (LANES, LANES), 0)
    lane_digit = (lane + 1).astype(jnp.float32)

    def body(j, total):
        ids = ids_ref[pl.ds(j, 1), :]
        hit = row_id == (ids >> 7)
        digit = jnp.full((blocks, LANES), j, jnp.int32).astype(jnp.float32)
        left = jnp.concatenate(
            [jnp.where(hit, lane_digit, 0.0), jnp.where(hit, digit, 0.0)], axis=0
        ).astype(jnp.bfloat16)
        right = jnp.where(low_id == (ids & 127), 1.0, 0.0).astype(jnp.bfloat16)
        return total + lax.dot_general(
            left, right, (((1,), (1,)), ((), ())), preferred_element_type=jnp.float32
        )

    total = lax.fori_loop(0, ids_ref.shape[0], body, jnp.zeros((2 * blocks, LANES), jnp.float32), unroll=4)
    return (total[blocks:] * 128.0 + total[:blocks]).astype(jnp.int32) - 1


def inverse_kernel(lists_ref, send_ref, from_list_ref, from_send_ref):
    from_list_ref[...] = inverse_of(lists_ref, from_list_ref.shape[0])
    from_send_ref[...] = inverse_of(send_ref, from_send_ref.shape[0])


def entry_rows(picked, rows_ref):
    block = lane_block()
    scale = {2: -0.5 * LOG2E, 3: -LOG2E, 4: -0.5 * LOG2E}
    for row in range(9):
        for g in range(4):
            value = picked[row][g]
            if row in scale:
                value = value * scale[row]
            moved = [value] + [pltpu.roll(value, 32 * k, 1) for k in range(1, 4)]
            for part in range(4):
                made = moved[(0 - part) % 4]
                for b in range(1, 4):
                    made = jnp.where(block == b, moved[(b - part) % 4], made)
                rows_ref[4 * row + part, 8 * g : 8 * g + 8, :] = made


def pixel_places(tiles_ref):
    lane = lax.broadcasted_iota(jnp.int32, (8, LANES), 1)
    sub = lax.broadcasted_iota(jnp.int32, (8, LANES), 0)
    tiles = jnp.broadcast_to(tiles_ref[0:1, :], (8, LANES))
    column = (tiles & (TILES_X - 1)) * 16 + sub
    row = (tiles >> 7) * 16 + (lane >> 5) * 4
    across = [column.astype(jnp.float32) + (0.5 + 8 * p) for p in range(2)]
    down = [row.astype(jnp.float32) + (0.5 + q) for q in range(4)]
    return across, down


def splat_at(rows_ref, j, part):
    return [
        jnp.broadcast_to(rows_ref[4 * row + part, pl.ds(j, 1), :], (8, LANES)) for row in range(9)
    ]


def composite(rows_ref, across, down, keep):
    def body(j, carry):
        clear, light = list(carry[:8]), [list(carry[8 + 8 * c : 16 + 8 * c]) for c in range(3)]
        for part in range(4):
            u, w, a, b, c2, o, *colour = splat_at(rows_ref, j, part)
            dx = [u - x for x in across]
            dy = [w - y for y in down]
            ax = [a * d for d in dx]
            by = [b * d for d in dy]
            cy = [c2 * d * d for d in dy]
            for v in range(8):
                q, p = v // 2, v % 2
                alpha = o * jnp.exp2((ax[p] + by[q]) * dx[p] + cy[q])
                weight = clear[v] * alpha
                if keep is not None:
                    keep[0][j, part * 8 + v] = alpha
                    keep[1][j, part * 8 + v] = weight
                clear[v] = clear[v] - weight
                for c in range(3):
                    light[c][v] = light[c][v] + colour[c] * weight
        return (*clear, *light[0], *light[1], *light[2])

    start = tuple([jnp.ones((8, LANES), jnp.float32)] * 8 + [jnp.zeros((8, LANES), jnp.float32)] * 24)
    done = lax.fori_loop(0, LIST_LEN // 4, body, start)
    return [done[8 + 8 * c : 16 + 8 * c] for c in range(3)]


def train_kernel(
    message_ref, lists_ref, inverse_ref, tiles_ref, targets_ref, back_ref,
    buffer_ref, rows_ref, alpha_ref, weight_ref, sums_ref, miss_ref,
):
    unpack(message_ref, buffer_ref)
    picked = pick(buffer_ref, 32, [eight(lists_ref, g) for g in range(4)], 2)
    entry_rows(picked, rows_ref)
    across, down = pixel_places(tiles_ref)
    light = composite(rows_ref, across, down, (alpha_ref, weight_ref))
    for c in range(3):
        for v in range(8):
            miss_ref[8 * c + v] = light[c][v] - targets_ref[c, 8 * v : 8 * v + 8, :]

    def body(step, behind):
        j = LIST_LEN // 4 - 1 - step
        behind = list(behind)
        for part in (3, 2, 1, 0):
            u, w, _, _, _, _, *colour = splat_at(rows_ref, j, part)
            dx = [u - x for x in across]
            dy = [w - y for y in down]
            pull = []
            tint = [None] * 3
            for v in range(8):
                alpha = alpha_ref[j, part * 8 + v]
                weight = weight_ref[j, part * 8 + v]
                miss = [miss_ref[8 * c + v] for c in range(3)]
                ahead = colour[0] * miss[0] + colour[1] * miss[1] + colour[2] * miss[2] - behind[v]
                pull.append(weight * ahead)
                behind[v] = behind[v] + alpha * ahead
                for c in range(3):
                    term = weight * miss[c]
                    tint[c] = term if tint[c] is None else tint[c] + term
            row_pull = [pull[2 * q] + pull[2 * q + 1] for q in range(4)]
            row_down = [row_pull[q] * dy[q] for q in range(4)]
            col_pull = [pull[p] + pull[2 + p] + pull[4 + p] + pull[6 + p] for p in range(2)]
            col_down = [
                pull[p] * dy[0] + pull[2 + p] * dy[1] + pull[4 + p] * dy[2] + pull[6 + p] * dy[3]
                for p in range(2)
            ]
            col_across = [col_pull[p] * dx[p] for p in range(2)]
            sums = [
                col_across[0] + col_across[1],
                row_down[0] + row_down[1] + row_down[2] + row_down[3],
                col_across[0] * dx[0] + col_across[1] * dx[1],
                col_down[0] * dx[0] + col_down[1] * dx[1],
                row_down[0] * dy[0] + row_down[1] * dy[1] + row_down[2] * dy[2] + row_down[3] * dy[3],
                col_pull[0] + col_pull[1],
                *tint,
            ]
            for n in range(9):
                sums_ref[4 * n + part, pl.ds(j, 1), :] = jnp.sum(sums[n], axis=0, keepdims=True)
        return tuple(behind)

    lax.fori_loop(0, LIST_LEN // 4, body, tuple([jnp.zeros((8, LANES), jnp.float32)] * 8))

    block = lane_block()
    for g in range(4):
        moment = []
        for n in range(9):
            made = None
            for part in range(4):
                value = sums_ref[4 * n + part, 8 * g : 8 * g + 8, :]
                value = value + pltpu.roll(value, 64, 1)
                value = value + pltpu.roll(value, 32, 1)
                made = value if made is None else jnp.where(block == part, value, made)
            moment.append(made)
        a, b, c2 = picked[2][g], picked[3][g], picked[4][g]
        grads = [
            -(a * moment[0] + b * moment[1]),
            -(c2 * moment[1] + b * moment[0]),
            -0.5 * moment[2],
            -moment[3],
            -0.5 * moment[4],
            *moment[5:],
        ]
        for n in range(9):
            buffer_ref[n, 8 * g : 8 * g + 8, :] = grads[n]
    returned = pick(buffer_ref, 32, [eight(inverse_ref, g) for g in range(4)], 2)
    pack(returned, back_ref)


def update_kernel(
    camera_ref, rates_ref, back_ref, inverse_ref, send_ref, params_ref, first_ref, second_ref,
    new_params_ref, new_first_ref, new_second_ref, message_ref,
    buffer_ref, splats_ref, frame_ref, *, half,
):
    step = pl.program_id(0)

    @pl.when(step == 0)
    def _():
        unpack(back_ref, buffer_ref)
        for view in range(2):
            for n, entry in enumerate(camera_frame(camera_ref, view)):
                frame_ref[view, n] = entry

    slot_grads = [g[0] for g in pick(buffer_ref, 32, [inverse_ref[...]], 4)]
    rows = []
    for g in range(8):
        rows += turned([params_ref[8 * g : 8 * g + 8, LANES * c : LANES * (c + 1)] for c in range(8)])
    frame = [frame_ref[0, n] for n in range(15)]
    used = rows[:10] + [None] + rows[11:59]

    def view_first(*leaves):
        return footprint(list(leaves[:10]) + [None] + list(leaves[10:]), frame, *half)

    made, pullback = jax.vjp(view_first, *(used[:10] + used[11:]))
    ka, kb, kc = conic_of(*made[2:5])
    ga, gb, gc = slot_grads[2], 0.5 * slot_grads[3], slot_grads[4]
    left = [[ka * ga + kb * gb, ka * gb + kb * gc], [kb * ga + kc * gb, kb * gb + kc * gc]]
    cover_grads = (
        -(left[0][0] * ka + left[0][1] * kb),
        -2.0 * (left[0][0] * kb + left[0][1] * kc),
        -(left[1][0] * kb + left[1][1] * kc),
    )
    grads = list(pullback((slot_grads[0], slot_grads[1], *cover_grads, *slot_grads[6:])))
    opacity_grad = slot_grads[5] * (1.0 - jax.nn.sigmoid(rows[10]))
    grads = grads[:10] + [opacity_grad] + grads[10:] + [jnp.zeros((8, LANES), jnp.float32)] * 5
    new_rows = []
    for g in range(8):
        columns = turned(grads[8 * g : 8 * g + 8])
        rate = rates_ref[8 * g : 8 * g + 8, :]
        fresh = []
        for c in range(8):
            at = (slice(8 * g, 8 * g + 8), slice(LANES * c, LANES * (c + 1)))
            gradient = columns[c]
            first = 0.9 * first_ref[at] + 0.1 * gradient
            second = 0.999 * second_ref[at] + 0.001 * gradient * gradient
            value = params_ref[at] - rate * (first * (1.0 / bias_first)) / (
                jnp.sqrt(second * (1.0 / bias_second)) + adam_epsilon
            )
            new_first_ref[at] = first
            new_second_ref[at] = second
            new_params_ref[at] = value
            fresh.append(value)
        new_rows += turned(fresh)
    splats = project(new_rows, [frame_ref[1, n] for n in range(15)], *half)
    at = pl.ds(pl.multiple_of(step * 8, 8), 8)
    for n in range(9):
        splats_ref[n, at, :] = splats[n]

    @pl.when(step == pl.num_programs(0) - 1)
    def _():
        send_splats(splats_ref, send_ref, message_ref)


def render_kernel(message_ref, lists_ref, tiles_ref, image_ref, buffer_ref, rows_ref):
    unpack(message_ref, buffer_ref)
    picked = pick(buffer_ref, 32, [eight(lists_ref, g) for g in range(4)], 2)
    entry_rows(picked, rows_ref)
    across, down = pixel_places(tiles_ref)
    light = composite(rows_ref, across, down, None)
    for c in range(3):
        flat = jnp.concatenate(list(light[c]), axis=0)
        upright = jnp.transpose(jnp.concatenate([flat, flat], axis=0))
        pieces = [upright[32 * b : 32 * b + 32, :] for b in range(4)]
        low = lax.broadcasted_iota(jnp.int32, (32, LANES), 1) < 64
        image_ref[:, c, 0:128] = jnp.where(low, pieces[0], pieces[1])
        image_ref[:, c, 128:256] = jnp.where(low, pieces[2], pieces[3])


def vmem(shape):
    return pltpu.VMEM(shape, jnp.float32)


def whole():
    return pl.BlockSpec(memory_space=pltpu.VMEM)


def scalars():
    return pl.BlockSpec(memory_space=pltpu.SMEM)


def f32(*shape):
    return jax.ShapeDtypeStruct(shape, jnp.float32)


def exchange(message, axis):
    flat = message.reshape(-1, 4, LANES)
    return lax.all_to_all(flat, axis, 0, 0, tiled=True).reshape(message.shape)


def shards(
    gauss_params, adam_first, adam_second, camera, send_first, send_second,
    lists_first, lists_second, tiles_first, tiles_second, targets,
):
    local = gauss_params.shape[1]
    steps = local // CHUNK
    half = (TILES_X * 8.0, lists_first.shape[0] * lax.axis_size("dev") // TILES_X * 8.0)
    limit = pltpu.CompilerParams(vmem_limit_bytes=48 * 1024 * 1024)
    slots_first, slots_second = send_first.reshape(32, LANES), send_second.reshape(32, LANES)
    order_first = lists_first.T.reshape(32, LANES)
    order_second = lists_second.T.reshape(32, LANES)
    places_first = jnp.tile(tiles_first, 4)[None]
    places_second = jnp.tile(tiles_second, 4)[None]
    goals = jnp.transpose(targets.reshape(TILE_DEV, 3, 4, 64), (1, 3, 2, 0)).reshape(3, 64, LANES)
    block = pl.BlockSpec((64, CHUNK), lambda i: (0, i))
    fixed = pl.BlockSpec((32, LANES), lambda i: (0, 0))
    packet = pl.BlockSpec((32, 4, 4, LANES), lambda i: (0, 0, 0, 0))


    message = pl.pallas_call(
        functools.partial(first_kernel, half=half),
        grid=(steps,),
        out_shape=f32(32, 4, 4, LANES),
        in_specs=[scalars(), block, fixed],
        out_specs=packet,
        scratch_shapes=[vmem((9, local // LANES, LANES)), vmem((15, 8, LANES))],
        compiler_params=limit,
        name="project_first",
    )(camera, gauss_params, slots_first)
    received = exchange(message, "dev")
    from_list, from_send = pl.pallas_call(
        inverse_kernel,
        out_shape=(
            jax.ShapeDtypeStruct((32, LANES), jnp.int32),
            jax.ShapeDtypeStruct((local // LANES, LANES), jnp.int32),
        ),
        in_specs=[whole(), whole()],
        out_specs=(whole(), whole()),
        compiler_params=limit,
        name="inverses",
    )(order_first, slots_first)
    back = pl.pallas_call(
        train_kernel,
        out_shape=f32(32, 4, 4, LANES),
        in_specs=[whole()] * 5,
        out_specs=whole(),
        scratch_shapes=[
            vmem((9, 32, LANES)), vmem((36, 32, LANES)), vmem((32, 32, 8, LANES)),
            vmem((32, 32, 8, LANES)), vmem((36, 32, LANES)), vmem((24, 8, LANES)),
        ],
        compiler_params=limit,
        name="train",
    )(received, order_first, from_list, places_first, goals)
    returned = exchange(back, "dev")
    new_params, new_first, new_second, message_next = pl.pallas_call(
        functools.partial(update_kernel, half=half),
        grid=(steps,),
        out_shape=(f32(59, local), f32(59, local), f32(59, local), f32(32, 4, 4, LANES)),
        in_specs=[
            scalars(),
            pl.BlockSpec((64, LANES), lambda i: (0, 0)),
            packet,
            pl.BlockSpec((8, LANES), lambda i: (i, 0)),
            fixed,
            block, block, block,
        ],
        out_specs=(block, block, block, packet),
        scratch_shapes=[vmem((9, 32, LANES)), vmem((9, local // LANES, LANES)), vmem((2, 15, 8, LANES))],
        compiler_params=limit,
        name="update",
    )(camera, jnp.asarray(rate_values()), returned, from_send, slots_second, gauss_params, adam_first, adam_second)
    received_next = exchange(message_next, "dev")
    image = pl.pallas_call(
        render_kernel,
        out_shape=f32(TILE_DEV, 3, 256),
        in_specs=[whole()] * 3,
        out_specs=whole(),
        scratch_shapes=[vmem((9, 32, LANES)), vmem((36, 32, LANES))],
        compiler_params=limit,
        name="render",
    )(received_next, order_second, places_second)
    return (new_params, new_first, new_second, image)


def solution(mesh):
    split = P(None, "dev")
    rows = P("dev", None)
    return jax.shard_map(
        shards,
        mesh=mesh,
        in_specs=(split, split, split, P(), rows, rows, rows, rows, P("dev"), P("dev"), P("dev", None, None)),
        out_specs=(split, split, split, P("dev", None, None)),
        check_vma=False,
    )
```

```python
import functools

import jax
import jax.numpy as jnp
import numpy as np
from jax import lax
from jax.experimental import pallas as pl
from jax.experimental.pallas import tpu as pltpu
from jax.sharding import PartitionSpec as P

LANES = 128
TILES_X = 128
TILE_DEV = 32
LIST_LEN = 128
CHUNK = 1024
LOG2E = 1.4426950408889634

focal_length = 1000.0
blur_floor = 0.3
adam_epsilon = 1e-08
bias_first = 1.0 - 0.9**20
bias_second = 1.0 - 0.999**20
sh_first = 0.28209479177387814
sh_second = 0.4886025119029199
sh_third = (
    1.0925484305920792,
    -1.0925484305920792,
    0.31539156525252005,
    -1.0925484305920792,
    0.5462742152960396,
)
sh_fourth = (
    -0.5900435899266435,
    2.890611442640554,
    -0.4570457994644658,
    0.3731763325901154,
    -0.4570457994644658,
    1.445305721320277,
    -0.5900435899266435,
)


def rate_values():
    values = np.full((64,), 0.000125)
    values[0:3] = 0.00016
    values[3:6] = 0.005
    values[6:10] = 0.001
    values[10] = 0.05
    values[11] = 0.0025
    values[27] = 0.0025
    values[43] = 0.0025
    return np.broadcast_to(values[:, None], (64, LANES)).astype(np.float32)


def camera_frame(camera_ref, view):
    def full(k):
        return jnp.full((8, LANES), camera_ref[view, k], jnp.float32)

    ca, sa = jnp.cos(full(0)), jnp.sin(full(0))
    cb, sb = jnp.cos(full(1)), jnp.sin(full(1))
    cc, sc = jnp.cos(full(2)), jnp.sin(full(2))
    rot = [
        [cc * cb, cc * (sb * sa) - sc * ca, cc * (sb * ca) + sc * sa],
        [sc * cb, sc * (sb * sa) + cc * ca, sc * (sb * ca) - cc * sa],
        [-sb, cb * sa, cb * ca],
    ]
    shift = [full(3), full(4), full(5)]
    back = [rot[0][k] * shift[0] + rot[1][k] * shift[1] + rot[2][k] * shift[2] for k in range(3)]
    return [rot[0][0], rot[0][1], rot[0][2], rot[1][0], rot[1][1], rot[1][2],
            rot[2][0], rot[2][1], rot[2][2]] + shift + back


def sh_terms(along_x, along_y, along_z):
    square_x, square_y, square_z = (along_x * along_x, along_y * along_y, along_z * along_z)
    return [
        -sh_second * along_y,
        sh_second * along_z,
        -sh_second * along_x,
        sh_third[0] * along_x * along_y,
        sh_third[1] * along_y * along_z,
        sh_third[2] * (2.0 * square_z - square_x - square_y),
        sh_third[3] * along_x * along_z,
        sh_third[4] * (square_x - square_y),
        sh_fourth[0] * along_y * (3.0 * square_x - square_y),
        sh_fourth[1] * along_x * along_y * along_z,
        sh_fourth[2] * along_y * (4.0 * square_z - square_x - square_y),
        sh_fourth[3] * along_z * (2.0 * square_z - 3.0 * square_x - 3.0 * square_y),
        sh_fourth[4] * along_x * (4.0 * square_z - square_x - square_y),
        sh_fourth[5] * along_z * (square_x - square_y),
        sh_fourth[6] * along_x * (square_x - 3.0 * square_y),
    ]


def footprint(params, frame, half_width, half_height):
    rot = [frame[0:3], frame[3:6], frame[6:9]]
    shift, back = frame[9:12], frame[12:15]
    x, y, z = params[0], params[1], params[2]
    viewed = [rot[k][0] * x + rot[k][1] * y + rot[k][2] * z + shift[k] for k in range(3)]
    inverse_depth = 1.0 / viewed[2]
    screen_u = focal_length * viewed[0] * inverse_depth + half_width
    screen_v = focal_length * viewed[1] * inverse_depth + half_height
    scales = [jnp.exp(params[3 + k]) for k in range(3)]
    size = params[6] * params[6] + params[7] * params[7] + params[8] * params[8] + params[9] * params[9]
    unit = 1.0 / jnp.sqrt(size)
    w, i, j, k = [params[6 + n] * unit for n in range(4)]
    turn = [
        [1.0 - 2.0 * (j * j + k * k), 2.0 * (i * j - w * k), 2.0 * (i * k + w * j)],
        [2.0 * (i * j + w * k), 1.0 - 2.0 * (i * i + k * k), 2.0 * (j * k - w * i)],
        [2.0 * (i * k - w * j), 2.0 * (j * k + w * i), 1.0 - 2.0 * (i * i + j * j)],
    ]
    near = focal_length * inverse_depth
    slant_x = -near * viewed[0] * inverse_depth
    slant_y = -near * viewed[1] * inverse_depth
    mapping = [
        [near * rot[0][n] + slant_x * rot[2][n] for n in range(3)],
        [near * rot[1][n] + slant_y * rot[2][n] for n in range(3)],
    ]
    half = [
        [
            (mapping[m][0] * turn[0][n] + mapping[m][1] * turn[1][n] + mapping[m][2] * turn[2][n])
            * scales[n]
            for n in range(3)
        ]
        for m in range(2)
    ]

    def inner(p, q):
        return p[0] * q[0] + p[1] * q[1] + p[2] * q[2]

    cover_a = inner(half[0], half[0]) + blur_floor
    cover_b = inner(half[0], half[1])
    cover_c = inner(half[1], half[1]) + blur_floor
    towards = [x + back[0], y + back[1], z + back[2]]
    inverse_length = 1.0 / jnp.sqrt(inner(towards, towards))
    harmonics = sh_terms(*[t * inverse_length for t in towards])
    colours = []
    for channel in range(3):
        running = 0.5 + sh_first * params[11 + 16 * channel]
        for term in range(1, 16):
            running = running + harmonics[term - 1] * params[11 + 16 * channel + term]
        colours.append(jnp.maximum(running, 0.0))
    return (screen_u, screen_v, cover_a, cover_b, cover_c, *colours)


def conic_of(cover_a, cover_b, cover_c):
    inverse = 1.0 / (cover_a * cover_c - cover_b * cover_b)
    return cover_c * inverse, -cover_b * inverse, cover_a * inverse


def project(params, frame, half_width, half_height):
    u, w, cover_a, cover_b, cover_c, *colours = footprint(params, frame, half_width, half_height)
    return [u, w, *conic_of(cover_a, cover_b, cover_c), jax.nn.sigmoid(params[10]), *colours]


def turned(tiles):
    swapped = jnp.swapaxes(jnp.stack(tiles, axis=0), 0, 1)
    return [swapped[n] for n in range(8)]


def lane_pick(values, lanes):
    numbers = lax.GatherDimensionNumbers(
        offset_dims=(),
        collapsed_slice_dims=(1,),
        start_index_map=(1,),
        operand_batching_dims=(0,),
        start_indices_batching_dims=(0,),
    )
    return lax.gather(
        values, lanes[:, :, None], numbers, (1, 1), mode=lax.GatherScatterMode.PROMISE_IN_BOUNDS
    )


def pick_eight(source_ref, wanted):
    count, blocks = source_ref.shape[:2]
    high, low = wanted >> 7, wanted & 127
    held = [jnp.zeros((8, LANES), jnp.float32)] * count
    for block in range(blocks):
        hit = high == block
        for row in range(count):
            source = jnp.broadcast_to(source_ref[row, block : block + 1, :], (8, LANES))
            held[row] = jnp.where(hit, lane_pick(source, low), held[row])
    return held


def pick(source_ref, wanted_ref, picked_ref):
    def body(g, _):
        at = pl.ds(pl.multiple_of(g * 8, 8), 8)
        for row, value in enumerate(pick_eight(source_ref, wanted_ref[at, :])):
            picked_ref[row, at, :] = value
        return 0

    lax.fori_loop(0, wanted_ref.shape[0] // 8, body, 0)


def lane_block():
    return lax.broadcasted_iota(jnp.int32, (8, LANES), 1) >> 5


def block_turn(vectors):
    block = lane_block()
    out = []
    for j in range(4):
        made = None
        for i in range(4):
            shift = ((i - j) * 32) % LANES
            moved = pltpu.roll(vectors[i], shift, 1) if shift else vectors[i]
            made = moved if made is None else jnp.where(block == i, moved, made)
        out.append(made)
    return out


def pack(picked_ref, message_ref):
    nothing = jnp.zeros((8, LANES), jnp.float32)
    for g in range(4):
        for a in range(3):
            rows = [
                picked_ref[4 * a + b, 8 * g : 8 * g + 8, :] if 4 * a + b < 9 else nothing
                for b in range(4)
            ]
            for d, made in enumerate(block_turn(rows)):
                message_ref[8 * g : 8 * g + 8, d, a, :] = made
        for d in range(4):
            message_ref[8 * g : 8 * g + 8, d, 3, :] = nothing


def unpack(message_ref, buffer_ref):
    for g in range(4):
        for a in range(3):
            rows = [message_ref[8 * g : 8 * g + 8, d, a, :] for d in range(4)]
            for b, made in enumerate(block_turn(rows)):
                if 4 * a + b < 9:
                    buffer_ref[4 * a + b, 8 * g : 8 * g + 8, :] = made


def send_splats(splats_ref, send_ref, picked_ref, message_ref):
    pick(splats_ref, send_ref, picked_ref)
    pack(picked_ref, message_ref)


def first_kernel(
    camera_ref, params_ref, send_ref, message_ref, splats_ref, picked_ref, frame_ref, *, half
):
    step = pl.program_id(0)

    @pl.when(step == 0)
    def _():
        for n, entry in enumerate(camera_frame(camera_ref, 0)):
            frame_ref[n] = entry

    rows = []
    for g in range(8):
        rows += turned([params_ref[8 * g : 8 * g + 8, LANES * c : LANES * (c + 1)] for c in range(8)])
    splats = project(rows, [frame_ref[n] for n in range(15)], *half)
    at = pl.ds(pl.multiple_of(step * 8, 8), 8)
    for n in range(9):
        splats_ref[n, at, :] = splats[n]

    @pl.when(step == pl.num_programs(0) - 1)
    def _():
        send_splats(splats_ref, send_ref, picked_ref, message_ref)


def inverse_of(ids_ref, blocks):
    lane = lax.broadcasted_iota(jnp.int32, (blocks, LANES), 1)
    row_id = lax.broadcasted_iota(jnp.int32, (blocks, LANES), 0)
    low_id = lax.broadcasted_iota(jnp.int32, (LANES, LANES), 0)
    lane_digit = (lane + 1).astype(jnp.float32)

    def body(j, total):
        ids = ids_ref[pl.ds(j, 1), :]
        hit = row_id == (ids >> 7)
        digit = jnp.full((blocks, LANES), j, jnp.int32).astype(jnp.float32)
        left = jnp.concatenate(
            [jnp.where(hit, lane_digit, 0.0), jnp.where(hit, digit, 0.0)], axis=0
        ).astype(jnp.bfloat16)
        right = jnp.where(low_id == (ids & 127), 1.0, 0.0).astype(jnp.bfloat16)
        return total + lax.dot_general(
            left, right, (((1,), (1,)), ((), ())), preferred_element_type=jnp.float32
        )

    total = lax.fori_loop(0, ids_ref.shape[0], body, jnp.zeros((2 * blocks, LANES), jnp.float32), unroll=4)
    return (total[blocks:] * 128.0 + total[:blocks]).astype(jnp.int32) - 1


def inverse_kernel(lists_ref, send_ref, from_list_ref, from_send_ref):
    from_list_ref[...] = inverse_of(lists_ref, from_list_ref.shape[0])
    from_send_ref[...] = inverse_of(send_ref, from_send_ref.shape[0])


def entry_rows(picked_ref, rows_ref):
    block = lane_block()
    scale = {2: -0.5 * LOG2E, 3: -LOG2E, 4: -0.5 * LOG2E}
    for row in range(9):
        for g in range(4):
            value = picked_ref[row, 8 * g : 8 * g + 8, :]
            if row in scale:
                value = value * scale[row]
            moved = [value] + [pltpu.roll(value, 32 * k, 1) for k in range(1, 4)]
            for part in range(4):
                made = moved[(0 - part) % 4]
                for b in range(1, 4):
                    made = jnp.where(block == b, moved[(b - part) % 4], made)
                rows_ref[4 * row + part, 8 * g : 8 * g + 8, :] = made


def pixel_places(tiles_ref):
    lane = lax.broadcasted_iota(jnp.int32, (8, LANES), 1)
    sub = lax.broadcasted_iota(jnp.int32, (8, LANES), 0)
    tiles = jnp.broadcast_to(tiles_ref[0:1, :], (8, LANES))
    column = (tiles & (TILES_X - 1)) * 16 + sub
    row = (tiles >> 7) * 16 + (lane >> 5) * 4
    across = [column.astype(jnp.float32) + (0.5 + 8 * p) for p in range(2)]
    down = [row.astype(jnp.float32) + (0.5 + q) for q in range(4)]
    return across, down


def splat_at(rows_ref, j, part):
    return [
        jnp.broadcast_to(rows_ref[4 * row + part, pl.ds(j, 1), :], (8, LANES)) for row in range(9)
    ]


def composite(rows_ref, across, down, keep):
    def body(j, carry):
        clear, light = list(carry[:8]), [list(carry[8 + 8 * c : 16 + 8 * c]) for c in range(3)]
        for part in range(4):
            u, w, a, b, c2, o, *colour = splat_at(rows_ref, j, part)
            dx = [u - x for x in across]
            dy = [w - y for y in down]
            ax = [a * d for d in dx]
            by = [b * d for d in dy]
            cy = [c2 * d * d for d in dy]
            for v in range(8):
                q, p = v // 2, v % 2
                alpha = o * jnp.exp2((ax[p] + by[q]) * dx[p] + cy[q])
                weight = clear[v] * alpha
                if keep is not None:
                    keep[0][j, part * 8 + v] = alpha
                    keep[1][j, part * 8 + v] = weight
                clear[v] = clear[v] - weight
                for c in range(3):
                    light[c][v] = light[c][v] + colour[c] * weight
        return (*clear, *light[0], *light[1], *light[2])

    start = tuple([jnp.ones((8, LANES), jnp.float32)] * 8 + [jnp.zeros((8, LANES), jnp.float32)] * 24)
    done = lax.fori_loop(0, LIST_LEN // 4, body, start)
    return [done[8 + 8 * c : 16 + 8 * c] for c in range(3)]


def train_kernel(
    message_ref, lists_ref, inverse_ref, tiles_ref, targets_ref, back_ref,
    buffer_ref, picked_ref, rows_ref, alpha_ref, weight_ref, sums_ref, miss_ref,
):
    unpack(message_ref, buffer_ref)
    pick(buffer_ref, lists_ref, picked_ref)
    entry_rows(picked_ref, rows_ref)
    across, down = pixel_places(tiles_ref)
    light = composite(rows_ref, across, down, (alpha_ref, weight_ref))
    for c in range(3):
        for v in range(8):
            miss_ref[8 * c + v] = light[c][v] - targets_ref[c, 8 * v : 8 * v + 8, :]

    def body(step, behind):
        j = LIST_LEN // 4 - 1 - step
        behind = list(behind)
        for part in (3, 2, 1, 0):
            u, w, _, _, _, _, *colour = splat_at(rows_ref, j, part)
            dx = [u - x for x in across]
            dy = [w - y for y in down]
            pull = []
            tint = [None] * 3
            for v in range(8):
                alpha = alpha_ref[j, part * 8 + v]
                weight = weight_ref[j, part * 8 + v]
                miss = [miss_ref[8 * c + v] for c in range(3)]
                ahead = colour[0] * miss[0] + colour[1] * miss[1] + colour[2] * miss[2] - behind[v]
                pull.append(weight * ahead)
                behind[v] = behind[v] + alpha * ahead
                for c in range(3):
                    term = weight * miss[c]
                    tint[c] = term if tint[c] is None else tint[c] + term
            row_pull = [pull[2 * q] + pull[2 * q + 1] for q in range(4)]
            row_down = [row_pull[q] * dy[q] for q in range(4)]
            col_pull = [pull[p] + pull[2 + p] + pull[4 + p] + pull[6 + p] for p in range(2)]
            col_down = [
                pull[p] * dy[0] + pull[2 + p] * dy[1] + pull[4 + p] * dy[2] + pull[6 + p] * dy[3]
                for p in range(2)
            ]
            col_across = [col_pull[p] * dx[p] for p in range(2)]
            sums = [
                col_across[0] + col_across[1],
                row_down[0] + row_down[1] + row_down[2] + row_down[3],
                col_across[0] * dx[0] + col_across[1] * dx[1],
                col_down[0] * dx[0] + col_down[1] * dx[1],
                row_down[0] * dy[0] + row_down[1] * dy[1] + row_down[2] * dy[2] + row_down[3] * dy[3],
                col_pull[0] + col_pull[1],
                *tint,
            ]
            for n in range(9):
                sums_ref[4 * n + part, pl.ds(j, 1), :] = jnp.sum(sums[n], axis=0, keepdims=True)
        return tuple(behind)

    lax.fori_loop(0, LIST_LEN // 4, body, tuple([jnp.zeros((8, LANES), jnp.float32)] * 8))

    block = lane_block()
    for g in range(4):
        moment = []
        for n in range(9):
            made = None
            for part in range(4):
                value = sums_ref[4 * n + part, 8 * g : 8 * g + 8, :]
                value = value + pltpu.roll(value, 64, 1)
                value = value + pltpu.roll(value, 32, 1)
                made = value if made is None else jnp.where(block == part, value, made)
            moment.append(made)
        a, b, c2 = [picked_ref[n, 8 * g : 8 * g + 8, :] for n in (2, 3, 4)]
        grads = [
            -(a * moment[0] + b * moment[1]),
            -(c2 * moment[1] + b * moment[0]),
            -0.5 * moment[2],
            -moment[3],
            -0.5 * moment[4],
            *moment[5:],
        ]
        for n in range(9):
            buffer_ref[n, 8 * g : 8 * g + 8, :] = grads[n]
    pick(buffer_ref, inverse_ref, picked_ref)
    pack(picked_ref, back_ref)


def update_kernel(
    camera_ref, rates_ref, back_ref, inverse_ref, send_ref, params_ref, first_ref, second_ref,
    new_params_ref, new_first_ref, new_second_ref, message_ref,
    buffer_ref, splats_ref, picked_ref, frame_ref, *, half,
):
    step = pl.program_id(0)

    @pl.when(step == 0)
    def _():
        unpack(back_ref, buffer_ref)
        for view in range(2):
            for n, entry in enumerate(camera_frame(camera_ref, view)):
                frame_ref[view, n] = entry

    slot_grads = pick_eight(buffer_ref, inverse_ref[...])
    rows = []
    for g in range(8):
        rows += turned([params_ref[8 * g : 8 * g + 8, LANES * c : LANES * (c + 1)] for c in range(8)])
    frame = [frame_ref[0, n] for n in range(15)]
    used = rows[:10] + [None] + rows[11:59]

    def view_first(*leaves):
        return footprint(list(leaves[:10]) + [None] + list(leaves[10:]), frame, *half)

    made, pullback = jax.vjp(view_first, *(used[:10] + used[11:]))
    ka, kb, kc = conic_of(*made[2:5])
    ga, gb, gc = slot_grads[2], 0.5 * slot_grads[3], slot_grads[4]
    left = [[ka * ga + kb * gb, ka * gb + kb * gc], [kb * ga + kc * gb, kb * gb + kc * gc]]
    cover_grads = (
        -(left[0][0] * ka + left[0][1] * kb),
        -2.0 * (left[0][0] * kb + left[0][1] * kc),
        -(left[1][0] * kb + left[1][1] * kc),
    )
    grads = list(pullback((slot_grads[0], slot_grads[1], *cover_grads, *slot_grads[6:])))
    opacity_grad = slot_grads[5] * (1.0 - jax.nn.sigmoid(rows[10]))
    grads = grads[:10] + [opacity_grad] + grads[10:] + [jnp.zeros((8, LANES), jnp.float32)] * 5
    new_rows = []
    for g in range(8):
        columns = turned(grads[8 * g : 8 * g + 8])
        rate = rates_ref[8 * g : 8 * g + 8, :]
        fresh = []
        for c in range(8):
            at = (slice(8 * g, 8 * g + 8), slice(LANES * c, LANES * (c + 1)))
            gradient = columns[c]
            first = 0.9 * first_ref[at] + 0.1 * gradient
            second = 0.999 * second_ref[at] + 0.001 * gradient * gradient
            value = params_ref[at] - rate * (first * (1.0 / bias_first)) / (
                jnp.sqrt(second * (1.0 / bias_second)) + adam_epsilon
            )
            new_first_ref[at] = first
            new_second_ref[at] = second
            new_params_ref[at] = value
            fresh.append(value)
        new_rows += turned(fresh)
    splats = project(new_rows, [frame_ref[1, n] for n in range(15)], *half)
    at = pl.ds(pl.multiple_of(step * 8, 8), 8)
    for n in range(9):
        splats_ref[n, at, :] = splats[n]

    @pl.when(step == pl.num_programs(0) - 1)
    def _():
        send_splats(splats_ref, send_ref, picked_ref, message_ref)


def render_kernel(message_ref, lists_ref, tiles_ref, image_ref, buffer_ref, picked_ref, rows_ref):
    unpack(message_ref, buffer_ref)
    pick(buffer_ref, lists_ref, picked_ref)
    entry_rows(picked_ref, rows_ref)
    across, down = pixel_places(tiles_ref)
    light = composite(rows_ref, across, down, None)
    for c in range(3):
        flat = jnp.concatenate(list(light[c]), axis=0)
        upright = jnp.transpose(jnp.concatenate([flat, flat], axis=0))
        pieces = [upright[32 * b : 32 * b + 32, :] for b in range(4)]
        low = lax.broadcasted_iota(jnp.int32, (32, LANES), 1) < 64
        image_ref[c, :, 0:128] = jnp.where(low, pieces[0], pieces[1])
        image_ref[c, :, 128:256] = jnp.where(low, pieces[2], pieces[3])


def vmem(shape):
    return pltpu.VMEM(shape, jnp.float32)


def whole():
    return pl.BlockSpec(memory_space=pltpu.VMEM)


def scalars():
    return pl.BlockSpec(memory_space=pltpu.SMEM)


def f32(*shape):
    return jax.ShapeDtypeStruct(shape, jnp.float32)


def exchange(message, axis):
    flat = message.reshape(-1, 4, LANES)
    return lax.all_to_all(flat, axis, 0, 0, tiled=True).reshape(message.shape)


def shards(
    gauss_params, adam_first, adam_second, camera, send_first, send_second,
    lists_first, lists_second, tiles_first, tiles_second, targets,
):
    local = gauss_params.shape[1]
    steps = local // CHUNK
    half = (TILES_X * 8.0, lists_first.shape[0] * lax.axis_size("dev") // TILES_X * 8.0)
    limit = pltpu.CompilerParams(vmem_limit_bytes=48 * 1024 * 1024)
    streamed = pltpu.CompilerParams(vmem_limit_bytes=62 * 1024 * 1024)
    slots_first, slots_second = send_first.reshape(32, LANES), send_second.reshape(32, LANES)
    order_first = lists_first.T.reshape(32, LANES)
    order_second = lists_second.T.reshape(32, LANES)
    places_first = jnp.tile(tiles_first, 4)[None]
    places_second = jnp.tile(tiles_second, 4)[None]
    goals = jnp.transpose(targets.reshape(TILE_DEV, 3, 4, 64), (1, 3, 2, 0)).reshape(3, 64, LANES)
    block = pl.BlockSpec((64, CHUNK), lambda i: (0, i))
    fixed = pl.BlockSpec((32, LANES), lambda i: (0, 0))
    packet = pl.BlockSpec((32, 4, 4, LANES), lambda i: (0, 0, 0, 0))


    message = pl.pallas_call(
        functools.partial(first_kernel, half=half),
        grid=(steps,),
        out_shape=f32(32, 4, 4, LANES),
        in_specs=[scalars(), block, fixed],
        out_specs=packet,
        scratch_shapes=[vmem((9, local // LANES, LANES)), vmem((9, 32, LANES)), vmem((15, 8, LANES))],
        compiler_params=streamed,
        name="project_first",
    )(camera, gauss_params, slots_first)
    received = exchange(message, "dev")
    from_list, from_send = pl.pallas_call(
        inverse_kernel,
        out_shape=(
            jax.ShapeDtypeStruct((32, LANES), jnp.int32),
            jax.ShapeDtypeStruct((local // LANES, LANES), jnp.int32),
        ),
        in_specs=[whole(), whole()],
        out_specs=(whole(), whole()),
        compiler_params=limit,
        name="inverses",
    )(order_first, slots_first)
    back = pl.pallas_call(
        train_kernel,
        out_shape=f32(32, 4, 4, LANES),
        in_specs=[whole()] * 5,
        out_specs=whole(),
        scratch_shapes=[
            vmem((9, 32, LANES)), vmem((9, 32, LANES)), vmem((36, 32, LANES)), vmem((32, 32, 8, LANES)),
            vmem((32, 32, 8, LANES)), vmem((36, 32, LANES)), vmem((24, 8, LANES)),
        ],
        compiler_params=limit,
        name="train",
    )(received, order_first, from_list, places_first, goals)
    returned = exchange(back, "dev")
    new_params, new_first, new_second, message_next = pl.pallas_call(
        functools.partial(update_kernel, half=half),
        grid=(steps,),
        out_shape=(f32(59, local), f32(59, local), f32(59, local), f32(32, 4, 4, LANES)),
        in_specs=[
            scalars(),
            pl.BlockSpec((64, LANES), lambda i: (0, 0)),
            packet,
            pl.BlockSpec((8, LANES), lambda i: (i, 0)),
            fixed,
            block, block, block,
        ],
        out_specs=(block, block, block, packet),
        scratch_shapes=[vmem((9, 32, LANES)), vmem((9, local // LANES, LANES)), vmem((9, 32, LANES)), vmem((2, 15, 8, LANES))],
        compiler_params=streamed,
        name="update",
    )(camera, jnp.asarray(rate_values()), returned, from_send, slots_second, gauss_params, adam_first, adam_second)
    received_next = exchange(message_next, "dev")
    image = pl.pallas_call(
        render_kernel,
        out_shape=f32(3, TILE_DEV, 256),
        in_specs=[whole()] * 3,
        out_specs=whole(),
        scratch_shapes=[vmem((9, 32, LANES)), vmem((9, 32, LANES)), vmem((36, 32, LANES))],
        compiler_params=limit,
        name="render",
    )(received_next, order_second, places_second)
    return (new_params, new_first, new_second, jnp.transpose(image, (1, 0, 2)))


def solution(mesh):
    split = P(None, "dev")
    rows = P("dev", None)
    return jax.shard_map(
        shards,
        mesh=mesh,
        in_specs=(split, split, split, P(), rows, rows, rows, rows, P("dev"), P("dev"), P("dev", None, None)),
        out_specs=(split, split, split, P("dev", None, None)),
        check_vma=False,
    )
```

```python
import functools

import jax
import jax.numpy as jnp
import numpy as np
from jax import lax
from jax.experimental import pallas as pl
from jax.experimental.pallas import tpu as pltpu
from jax.sharding import PartitionSpec as P

LANES = 128
TILES_X = 128
TILE_DEV = 32
LIST_LEN = 128
CHUNK = 1024
LOG2E = 1.4426950408889634

focal_length = 1000.0
blur_floor = 0.3
adam_epsilon = 1e-08
bias_first = 1.0 - 0.9**20
bias_second = 1.0 - 0.999**20
sh_first = 0.28209479177387814
sh_second = 0.4886025119029199
sh_third = (
    1.0925484305920792,
    -1.0925484305920792,
    0.31539156525252005,
    -1.0925484305920792,
    0.5462742152960396,
)
sh_fourth = (
    -0.5900435899266435,
    2.890611442640554,
    -0.4570457994644658,
    0.3731763325901154,
    -0.4570457994644658,
    1.445305721320277,
    -0.5900435899266435,
)


def rate_values():
    values = np.full((64,), 0.000125)
    values[0:3] = 0.00016
    values[3:6] = 0.005
    values[6:10] = 0.001
    values[10] = 0.05
    values[11] = 0.0025
    values[27] = 0.0025
    values[43] = 0.0025
    return np.broadcast_to(values[:, None], (64, LANES)).astype(np.float32)


def camera_frame(camera_ref, view):
    def full(k):
        return jnp.full((8, LANES), camera_ref[view, k], jnp.float32)

    ca, sa = jnp.cos(full(0)), jnp.sin(full(0))
    cb, sb = jnp.cos(full(1)), jnp.sin(full(1))
    cc, sc = jnp.cos(full(2)), jnp.sin(full(2))
    rot = [
        [cc * cb, cc * (sb * sa) - sc * ca, cc * (sb * ca) + sc * sa],
        [sc * cb, sc * (sb * sa) + cc * ca, sc * (sb * ca) - cc * sa],
        [-sb, cb * sa, cb * ca],
    ]
    shift = [full(3), full(4), full(5)]
    back = [rot[0][k] * shift[0] + rot[1][k] * shift[1] + rot[2][k] * shift[2] for k in range(3)]
    return [rot[0][0], rot[0][1], rot[0][2], rot[1][0], rot[1][1], rot[1][2],
            rot[2][0], rot[2][1], rot[2][2]] + shift + back


def sh_terms(along_x, along_y, along_z):
    square_x, square_y, square_z = (along_x * along_x, along_y * along_y, along_z * along_z)
    return [
        -sh_second * along_y,
        sh_second * along_z,
        -sh_second * along_x,
        sh_third[0] * along_x * along_y,
        sh_third[1] * along_y * along_z,
        sh_third[2] * (2.0 * square_z - square_x - square_y),
        sh_third[3] * along_x * along_z,
        sh_third[4] * (square_x - square_y),
        sh_fourth[0] * along_y * (3.0 * square_x - square_y),
        sh_fourth[1] * along_x * along_y * along_z,
        sh_fourth[2] * along_y * (4.0 * square_z - square_x - square_y),
        sh_fourth[3] * along_z * (2.0 * square_z - 3.0 * square_x - 3.0 * square_y),
        sh_fourth[4] * along_x * (4.0 * square_z - square_x - square_y),
        sh_fourth[5] * along_z * (square_x - square_y),
        sh_fourth[6] * along_x * (square_x - 3.0 * square_y),
    ]


def footprint(params, frame, half_width, half_height):
    rot = [frame[0:3], frame[3:6], frame[6:9]]
    shift, back = frame[9:12], frame[12:15]
    x, y, z = params[0], params[1], params[2]
    viewed = [rot[k][0] * x + rot[k][1] * y + rot[k][2] * z + shift[k] for k in range(3)]
    inverse_depth = 1.0 / viewed[2]
    screen_u = focal_length * viewed[0] * inverse_depth + half_width
    screen_v = focal_length * viewed[1] * inverse_depth + half_height
    scales = [jnp.exp(params[3 + k]) for k in range(3)]
    size = params[6] * params[6] + params[7] * params[7] + params[8] * params[8] + params[9] * params[9]
    unit = 1.0 / jnp.sqrt(size)
    w, i, j, k = [params[6 + n] * unit for n in range(4)]
    turn = [
        [1.0 - 2.0 * (j * j + k * k), 2.0 * (i * j - w * k), 2.0 * (i * k + w * j)],
        [2.0 * (i * j + w * k), 1.0 - 2.0 * (i * i + k * k), 2.0 * (j * k - w * i)],
        [2.0 * (i * k - w * j), 2.0 * (j * k + w * i), 1.0 - 2.0 * (i * i + j * j)],
    ]
    near = focal_length * inverse_depth
    slant_x = -near * viewed[0] * inverse_depth
    slant_y = -near * viewed[1] * inverse_depth
    mapping = [
        [near * rot[0][n] + slant_x * rot[2][n] for n in range(3)],
        [near * rot[1][n] + slant_y * rot[2][n] for n in range(3)],
    ]
    half = [
        [
            (mapping[m][0] * turn[0][n] + mapping[m][1] * turn[1][n] + mapping[m][2] * turn[2][n])
            * scales[n]
            for n in range(3)
        ]
        for m in range(2)
    ]

    def inner(p, q):
        return p[0] * q[0] + p[1] * q[1] + p[2] * q[2]

    cover_a = inner(half[0], half[0]) + blur_floor
    cover_b = inner(half[0], half[1])
    cover_c = inner(half[1], half[1]) + blur_floor
    towards = [x + back[0], y + back[1], z + back[2]]
    inverse_length = 1.0 / jnp.sqrt(inner(towards, towards))
    harmonics = sh_terms(*[t * inverse_length for t in towards])
    colours = []
    for channel in range(3):
        running = 0.5 + sh_first * params[11 + 16 * channel]
        for term in range(1, 16):
            running = running + harmonics[term - 1] * params[11 + 16 * channel + term]
        colours.append(jnp.maximum(running, 0.0))
    return (screen_u, screen_v, cover_a, cover_b, cover_c, *colours)


def conic_of(cover_a, cover_b, cover_c):
    inverse = 1.0 / (cover_a * cover_c - cover_b * cover_b)
    return cover_c * inverse, -cover_b * inverse, cover_a * inverse


def project(params, frame, half_width, half_height):
    u, w, cover_a, cover_b, cover_c, *colours = footprint(params, frame, half_width, half_height)
    return [u, w, *conic_of(cover_a, cover_b, cover_c), jax.nn.sigmoid(params[10]), *colours]


def turned(tiles):
    swapped = jnp.swapaxes(jnp.stack(tiles, axis=0), 0, 1)
    return [swapped[n] for n in range(8)]


def lane_pick(values, lanes):
    numbers = lax.GatherDimensionNumbers(
        offset_dims=(),
        collapsed_slice_dims=(1,),
        start_index_map=(1,),
        operand_batching_dims=(0,),
        start_indices_batching_dims=(0,),
    )
    return lax.gather(
        values, lanes[:, :, None], numbers, (1, 1), mode=lax.GatherScatterMode.PROMISE_IN_BOUNDS
    )


def pick_eight(source_ref, wanted):
    count, blocks = source_ref.shape[:2]
    high, low = wanted >> 7, wanted & 127
    held = [jnp.zeros((8, LANES), jnp.float32)] * count
    for block in range(blocks):
        hit = high == block
        for row in range(count):
            source = jnp.broadcast_to(source_ref[row, block : block + 1, :], (8, LANES))
            held[row] = jnp.where(hit, lane_pick(source, low), held[row])
    return held


def pick(source_ref, wanted_ref, picked_ref):
    def body(g, _):
        at = pl.ds(pl.multiple_of(g * 8, 8), 8)
        for row, value in enumerate(pick_eight(source_ref, wanted_ref[at, :])):
            picked_ref[row, at, :] = value
        return 0

    lax.fori_loop(0, wanted_ref.shape[0] // 8, body, 0)


def lane_block():
    return lax.broadcasted_iota(jnp.int32, (8, LANES), 1) >> 5


def block_turn(vectors):
    block = lane_block()
    out = []
    for j in range(4):
        made = None
        for i in range(4):
            shift = ((i - j) * 32) % LANES
            moved = pltpu.roll(vectors[i], shift, 1) if shift else vectors[i]
            made = moved if made is None else jnp.where(block == i, moved, made)
        out.append(made)
    return out


def device_rows(g, d):
    return pl.ds(32 * g + d, 8, stride=4)


def pack(picked_ref, message_ref):
    nothing = jnp.zeros((8, LANES), jnp.float32)
    for g in range(4):
        for a in range(3):
            rows = [
                picked_ref[4 * a + b, 8 * g : 8 * g + 8, :] if 4 * a + b < 9 else nothing
                for b in range(4)
            ]
            for d, made in enumerate(block_turn(rows)):
                message_ref[device_rows(g, d), a, :] = made


def unpack(message_ref, buffer_ref):
    for g in range(4):
        for a in range(3):
            rows = [message_ref[device_rows(g, d), a, :] for d in range(4)]
            for b, made in enumerate(block_turn(rows)):
                if 4 * a + b < 9:
                    buffer_ref[4 * a + b, 8 * g : 8 * g + 8, :] = made


def greet():
    me, devices = lax.axis_index("dev"), lax.axis_size("dev")
    barrier = pltpu.get_barrier_semaphore()

    def body(j, _):
        pl.semaphore_signal(
            barrier, inc=1, device_id=(lax.rem(me + j, devices),), device_id_type=pl.DeviceIdType.MESH
        )
        return 0

    lax.fori_loop(1, devices, body, 0)


def deliver(message_ref, landing_ref, sent, landed, meanwhile=None):
    me, devices = lax.axis_index("dev"), lax.axis_size("dev")
    pl.semaphore_wait(pltpu.get_barrier_semaphore(), devices - 1)

    def remote(source, target, device):
        return pltpu.make_async_remote_copy(
            src_ref=source,
            dst_ref=target,
            send_sem=sent.at[0],
            recv_sem=landed.at[0],
            device_id=(device,),
            device_id_type=pl.DeviceIdType.MESH,
        )

    def body(j, _):
        other = lax.rem(me + j, devices)
        remote(message_ref.at[other], landing_ref.at[me], other).start()
        return 0

    lax.fori_loop(1, devices, body, 0)
    own = pltpu.make_async_copy(message_ref.at[me], landing_ref.at[me], sent.at[1])
    own.start()
    if meanwhile is not None:
        meanwhile()
    own.wait()
    several = pl.ds(0, devices - 1)
    remote(message_ref.at[several], landing_ref.at[several], lax.rem(me + 1, devices)).wait()


def first_kernel(
    camera_ref, params_ref, send_ref, lists_ref, landing_ref, from_list_ref, from_send_ref,
    params_held, splats_ref, picked_ref, message_ref, loaded, sent, landed, *, half
):
    chunks = params_ref.shape[1] // CHUNK
    loads = [
        pltpu.make_async_copy(
            params_ref.at[:, CHUNK * k : CHUNK * (k + 1)], params_held.at[k], loaded.at[k]
        )
        for k in range(chunks)
    ]
    for load in loads:
        load.start()
    greet()
    frame = camera_frame(camera_ref, 0)
    for k in range(chunks):
        loads[k].wait()
        rows = []
        for g in range(8):
            rows += turned([param_tile(params_held, k, g, c) for c in range(8)])
        splats = project(rows, frame, *half)
        for n in range(9):
            splats_ref[n, 8 * k : 8 * k + 8, :] = splats[n]
    pick(splats_ref, send_ref, picked_ref)
    pack(picked_ref, message_ref)

    def meanwhile():
        from_list_ref[...] = inverse_of(lists_ref, from_list_ref.shape[0])
        from_send_ref[...] = inverse_of(send_ref, from_send_ref.shape[0])

    deliver(message_ref, landing_ref, sent, landed, meanwhile)


def param_tile(params_held, k, g, c):
    at = slice(LANES * c, LANES * (c + 1))
    if g < 7:
        return params_held[k, 8 * g : 8 * g + 8, at]
    return jnp.concatenate([params_held[k, 56:59, at], jnp.zeros((5, LANES), jnp.float32)], axis=0)


def last_kernel(splats_ref, send_ref, landing_ref, picked_ref, message_ref, sent, landed):
    greet()
    pick(splats_ref, send_ref, picked_ref)
    pack(picked_ref, message_ref)
    deliver(message_ref, landing_ref, sent, landed)


def inverse_of(ids_ref, blocks):
    lane = lax.broadcasted_iota(jnp.int32, (blocks, LANES), 1)
    row_id = lax.broadcasted_iota(jnp.int32, (blocks, LANES), 0)
    low_id = lax.broadcasted_iota(jnp.int32, (LANES, LANES), 0)
    lane_digit = (lane + 1).astype(jnp.float32)

    def body(j, total):
        ids = ids_ref[pl.ds(j, 1), :]
        hit = row_id == (ids >> 7)
        digit = jnp.full((blocks, LANES), j, jnp.int32).astype(jnp.float32)
        left = jnp.concatenate(
            [jnp.where(hit, lane_digit, 0.0), jnp.where(hit, digit, 0.0)], axis=0
        ).astype(jnp.bfloat16)
        right = jnp.where(low_id == (ids & 127), 1.0, 0.0).astype(jnp.bfloat16)
        return total + lax.dot_general(
            left, right, (((1,), (1,)), ((), ())), preferred_element_type=jnp.float32
        )

    total = lax.fori_loop(0, ids_ref.shape[0], body, jnp.zeros((2 * blocks, LANES), jnp.float32), unroll=4)
    return (total[blocks:] * 128.0 + total[:blocks]).astype(jnp.int32) - 1


def entry_rows(picked_ref, rows_ref):
    block = lane_block()
    scale = {2: -0.5 * LOG2E, 3: -LOG2E, 4: -0.5 * LOG2E}
    for row in range(9):
        for g in range(4):
            value = picked_ref[row, 8 * g : 8 * g + 8, :]
            if row in scale:
                value = value * scale[row]
            moved = [value] + [pltpu.roll(value, 32 * k, 1) for k in range(1, 4)]
            for part in range(4):
                made = moved[(0 - part) % 4]
                for b in range(1, 4):
                    made = jnp.where(block == b, moved[(b - part) % 4], made)
                rows_ref[4 * row + part, 8 * g : 8 * g + 8, :] = made


def pixel_places(tiles_ref):
    lane = lax.broadcasted_iota(jnp.int32, (8, LANES), 1)
    sub = lax.broadcasted_iota(jnp.int32, (8, LANES), 0)
    tiles = jnp.broadcast_to(tiles_ref[0:1, :], (8, LANES))
    column = (tiles & (TILES_X - 1)) * 16 + sub
    row = (tiles >> 7) * 16 + (lane >> 5) * 4
    across = [column.astype(jnp.float32) + (0.5 + 8 * p) for p in range(2)]
    down = [row.astype(jnp.float32) + (0.5 + q) for q in range(4)]
    return across, down


def splat_at(rows_ref, j, part):
    return [
        jnp.broadcast_to(rows_ref[4 * row + part, pl.ds(j, 1), :], (8, LANES)) for row in range(9)
    ]


def composite(rows_ref, across, down, keep):
    def body(j, carry):
        clear, light = list(carry[:8]), [list(carry[8 + 8 * c : 16 + 8 * c]) for c in range(3)]
        for part in range(4):
            u, w, a, b, c2, o, *colour = splat_at(rows_ref, j, part)
            dx = [u - x for x in across]
            dy = [w - y for y in down]
            ax = [a * d for d in dx]
            by = [b * d for d in dy]
            cy = [c2 * d * d for d in dy]
            for v in range(8):
                q, p = v // 2, v % 2
                alpha = o * jnp.exp2((ax[p] + by[q]) * dx[p] + cy[q])
                weight = clear[v] * alpha
                if keep is not None:
                    keep[0][j, part * 8 + v] = alpha
                    keep[1][j, part * 8 + v] = weight
                clear[v] = clear[v] - weight
                for c in range(3):
                    light[c][v] = light[c][v] + colour[c] * weight
        return (*clear, *light[0], *light[1], *light[2])

    start = tuple([jnp.ones((8, LANES), jnp.float32)] * 8 + [jnp.zeros((8, LANES), jnp.float32)] * 24)
    done = lax.fori_loop(0, LIST_LEN // 4, body, start)
    return [done[8 + 8 * c : 16 + 8 * c] for c in range(3)]


def train_kernel(
    received_ref, lists_ref, inverse_ref, tiles_ref, targets_ref, landing_ref,
    buffer_ref, picked_ref, rows_ref, alpha_ref, weight_ref, sums_ref, miss_ref, message_ref,
    sent, landed,
):
    greet()
    unpack(received_ref, buffer_ref)
    pick(buffer_ref, lists_ref, picked_ref)
    entry_rows(picked_ref, rows_ref)
    across, down = pixel_places(tiles_ref)
    light = composite(rows_ref, across, down, (alpha_ref, weight_ref))
    for c in range(3):
        for v in range(8):
            miss_ref[8 * c + v] = light[c][v] - targets_ref[c, 8 * v : 8 * v + 8, :]

    def body(step, behind):
        j = LIST_LEN // 4 - 1 - step
        behind = list(behind)
        for part in (3, 2, 1, 0):
            u, w, _, _, _, _, *colour = splat_at(rows_ref, j, part)
            dx = [u - x for x in across]
            dy = [w - y for y in down]
            pull = []
            tint = [None] * 3
            for v in range(8):
                alpha = alpha_ref[j, part * 8 + v]
                weight = weight_ref[j, part * 8 + v]
                miss = [miss_ref[8 * c + v] for c in range(3)]
                ahead = colour[0] * miss[0] + colour[1] * miss[1] + colour[2] * miss[2] - behind[v]
                pull.append(weight * ahead)
                behind[v] = behind[v] + alpha * ahead
                for c in range(3):
                    term = weight * miss[c]
                    tint[c] = term if tint[c] is None else tint[c] + term
            row_pull = [pull[2 * q] + pull[2 * q + 1] for q in range(4)]
            row_down = [row_pull[q] * dy[q] for q in range(4)]
            col_pull = [pull[p] + pull[2 + p] + pull[4 + p] + pull[6 + p] for p in range(2)]
            col_down = [
                pull[p] * dy[0] + pull[2 + p] * dy[1] + pull[4 + p] * dy[2] + pull[6 + p] * dy[3]
                for p in range(2)
            ]
            col_across = [col_pull[p] * dx[p] for p in range(2)]
            sums = [
                col_across[0] + col_across[1],
                row_down[0] + row_down[1] + row_down[2] + row_down[3],
                col_across[0] * dx[0] + col_across[1] * dx[1],
                col_down[0] * dx[0] + col_down[1] * dx[1],
                row_down[0] * dy[0] + row_down[1] * dy[1] + row_down[2] * dy[2] + row_down[3] * dy[3],
                col_pull[0] + col_pull[1],
                *tint,
            ]
            for n in range(9):
                sums_ref[4 * n + part, pl.ds(j, 1), :] = jnp.sum(sums[n], axis=0, keepdims=True)
        return tuple(behind)

    lax.fori_loop(0, LIST_LEN // 4, body, tuple([jnp.zeros((8, LANES), jnp.float32)] * 8))

    block = lane_block()
    for g in range(4):
        moment = []
        for n in range(9):
            made = None
            for part in range(4):
                value = sums_ref[4 * n + part, 8 * g : 8 * g + 8, :]
                value = value + pltpu.roll(value, 64, 1)
                value = value + pltpu.roll(value, 32, 1)
                made = value if made is None else jnp.where(block == part, value, made)
            moment.append(made)
        a, b, c2 = [picked_ref[n, 8 * g : 8 * g + 8, :] for n in (2, 3, 4)]
        grads = [
            -(a * moment[0] + b * moment[1]),
            -(c2 * moment[1] + b * moment[0]),
            -0.5 * moment[2],
            -moment[3],
            -0.5 * moment[4],
            *moment[5:],
        ]
        for n in range(9):
            buffer_ref[n, 8 * g : 8 * g + 8, :] = grads[n]
    pick(buffer_ref, inverse_ref, picked_ref)
    pack(picked_ref, message_ref)
    deliver(message_ref, landing_ref, sent, landed)


def update_kernel(
    camera_ref, rates_ref, back_ref, inverse_ref, params_ref, first_ref, second_ref,
    new_params_ref, new_first_ref, new_second_ref, splats_ref,
    buffer_ref, frame_ref, *, half,
):
    step = pl.program_id(0)

    @pl.when(step == 0)
    def _():
        unpack(back_ref, buffer_ref)
        for view in range(2):
            for n, entry in enumerate(camera_frame(camera_ref, view)):
                frame_ref[view, n] = entry

    slot_grads = pick_eight(buffer_ref, inverse_ref[...])
    rows = []
    for g in range(8):
        rows += turned([params_ref[8 * g : 8 * g + 8, LANES * c : LANES * (c + 1)] for c in range(8)])
    frame = [frame_ref[0, n] for n in range(15)]
    used = rows[:10] + [None] + rows[11:59]

    def view_first(*leaves):
        return footprint(list(leaves[:10]) + [None] + list(leaves[10:]), frame, *half)

    made, pullback = jax.vjp(view_first, *(used[:10] + used[11:]))
    ka, kb, kc = conic_of(*made[2:5])
    ga, gb, gc = slot_grads[2], 0.5 * slot_grads[3], slot_grads[4]
    left = [[ka * ga + kb * gb, ka * gb + kb * gc], [kb * ga + kc * gb, kb * gb + kc * gc]]
    cover_grads = (
        -(left[0][0] * ka + left[0][1] * kb),
        -2.0 * (left[0][0] * kb + left[0][1] * kc),
        -(left[1][0] * kb + left[1][1] * kc),
    )
    grads = list(pullback((slot_grads[0], slot_grads[1], *cover_grads, *slot_grads[6:])))
    opacity_grad = slot_grads[5] * (1.0 - jax.nn.sigmoid(rows[10]))
    grads = grads[:10] + [opacity_grad] + grads[10:] + [jnp.zeros((8, LANES), jnp.float32)] * 5
    new_rows = []
    for g in range(8):
        columns = turned(grads[8 * g : 8 * g + 8])
        rate = rates_ref[8 * g : 8 * g + 8, :]
        fresh = []
        for c in range(8):
            at = (slice(8 * g, 8 * g + 8), slice(LANES * c, LANES * (c + 1)))
            gradient = columns[c]
            first = 0.9 * first_ref[at] + 0.1 * gradient
            second = 0.999 * second_ref[at] + 0.001 * gradient * gradient
            value = params_ref[at] - rate * (first * (1.0 / bias_first)) / (
                jnp.sqrt(second * (1.0 / bias_second)) + adam_epsilon
            )
            new_first_ref[at] = first
            new_second_ref[at] = second
            new_params_ref[at] = value
            fresh.append(value)
        new_rows += turned(fresh)
    splats = project(new_rows, [frame_ref[1, n] for n in range(15)], *half)
    for n in range(9):
        splats_ref[n] = splats[n]


def render_kernel(message_ref, lists_ref, tiles_ref, image_ref, buffer_ref, picked_ref, rows_ref):
    unpack(message_ref, buffer_ref)
    pick(buffer_ref, lists_ref, picked_ref)
    entry_rows(picked_ref, rows_ref)
    across, down = pixel_places(tiles_ref)
    light = composite(rows_ref, across, down, None)
    for c in range(3):
        flat = jnp.concatenate(list(light[c]), axis=0)
        upright = jnp.transpose(jnp.concatenate([flat, flat], axis=0))
        pieces = [upright[32 * b : 32 * b + 32, :] for b in range(4)]
        low = lax.broadcasted_iota(jnp.int32, (32, LANES), 1) < 64
        image_ref[c, :, 0:128] = jnp.where(low, pieces[0], pieces[1])
        image_ref[c, :, 128:256] = jnp.where(low, pieces[2], pieces[3])


def vmem(shape):
    return pltpu.VMEM(shape, jnp.float32)


def whole():
    return pl.BlockSpec(memory_space=pltpu.VMEM)


def scalars():
    return pl.BlockSpec(memory_space=pltpu.SMEM)


def f32(*shape):
    return jax.ShapeDtypeStruct(shape, jnp.float32)


def shards(
    gauss_params, adam_first, adam_second, camera, send_first, send_second,
    lists_first, lists_second, tiles_first, tiles_second, targets,
):
    local = gauss_params.shape[1]
    steps, blocks = local // CHUNK, local // LANES
    devices = lax.axis_size("dev")
    half = (TILES_X * 8.0, lists_first.shape[0] * devices // TILES_X * 8.0)
    megabyte = 1024 * 1024
    limit = pltpu.CompilerParams(vmem_limit_bytes=48 * megabyte)
    streamed = pltpu.CompilerParams(vmem_limit_bytes=62 * megabyte)

    def linked(number):
        return pltpu.CompilerParams(
            vmem_limit_bytes=60 * megabyte, collective_id=number, has_side_effects=True
        )

    slots_first, slots_second = send_first.reshape(32, LANES), send_second.reshape(32, LANES)
    order_first = lists_first.T.reshape(32, LANES)
    order_second = lists_second.T.reshape(32, LANES)
    places_first = jnp.tile(tiles_first, 4)[None]
    places_second = jnp.tile(tiles_second, 4)[None]
    goals = jnp.transpose(targets.reshape(TILE_DEV, 3, 4, 64), (1, 3, 2, 0)).reshape(3, 64, LANES)
    packet = (devices, 3, LANES)
    links = [pltpu.SemaphoreType.DMA((2,)), pltpu.SemaphoreType.DMA((1,))]
    received, from_list, from_send = pl.pallas_call(
        functools.partial(first_kernel, half=half),
        out_shape=(
            f32(*packet),
            jax.ShapeDtypeStruct((32, LANES), jnp.int32),
            jax.ShapeDtypeStruct((blocks, LANES), jnp.int32),
        ),
        in_specs=[scalars(), pl.BlockSpec(memory_space=pl.ANY), whole(), whole()],
        out_specs=(whole(), whole(), whole()),
        scratch_shapes=[
            vmem((steps, 59, CHUNK)), vmem((9, blocks, LANES)), vmem((9, 32, LANES)), vmem(packet),
            pltpu.SemaphoreType.DMA((steps,)), *links,
        ],
        compiler_params=linked(1),
        name="project_first",
    )(camera, gauss_params, slots_first, order_first)
    returned = pl.pallas_call(
        train_kernel,
        out_shape=f32(*packet),
        in_specs=[whole()] * 5,
        out_specs=whole(),
        scratch_shapes=[
            vmem((9, 32, LANES)), vmem((9, 32, LANES)), vmem((36, 32, LANES)), vmem((32, 32, 8, LANES)),
            vmem((32, 32, 8, LANES)), vmem((36, 32, LANES)), vmem((24, 8, LANES)), vmem(packet), *links,
        ],
        compiler_params=linked(2),
        name="train",
    )(received, order_first, from_list, places_first, goals)
    block = pl.BlockSpec((64, CHUNK), lambda i: (0, i))
    new_params, new_first, new_second, splats_next = pl.pallas_call(
        functools.partial(update_kernel, half=half),
        grid=(steps,),
        out_shape=(f32(59, local), f32(59, local), f32(59, local), f32(9, blocks, LANES)),
        in_specs=[
            scalars(),
            pl.BlockSpec((64, LANES), lambda i: (0, 0)),
            pl.BlockSpec(packet, lambda i: (0, 0, 0)),
            pl.BlockSpec((8, LANES), lambda i: (i, 0)),
            block, block, block,
        ],
        out_specs=(block, block, block, pl.BlockSpec((9, 8, LANES), lambda i: (0, i, 0))),
        scratch_shapes=[vmem((9, 32, LANES)), vmem((2, 15, 8, LANES))],
        compiler_params=streamed,
        name="update",
    )(camera, jnp.asarray(rate_values()), returned, from_send, gauss_params, adam_first, adam_second)
    received_next = pl.pallas_call(
        last_kernel,
        out_shape=f32(*packet),
        in_specs=[whole()] * 2,
        out_specs=whole(),
        scratch_shapes=[vmem((9, 32, LANES)), vmem(packet), *links],
        compiler_params=linked(3),
        name="send_next",
    )(splats_next, slots_second)
    image = pl.pallas_call(
        render_kernel,
        out_shape=f32(3, TILE_DEV, 256),
        in_specs=[whole()] * 3,
        out_specs=whole(),
        scratch_shapes=[vmem((9, 32, LANES)), vmem((9, 32, LANES)), vmem((36, 32, LANES))],
        compiler_params=limit,
        name="render",
    )(received_next, order_second, places_second)
    return (new_params, new_first, new_second, jnp.transpose(image, (1, 0, 2)))


def solution(mesh):
    split = P(None, "dev")
    rows = P("dev", None)
    return jax.shard_map(
        shards,
        mesh=mesh,
        in_specs=(split, split, split, P(), rows, rows, rows, rows, P("dev"), P("dev"), P("dev", None, None)),
        out_specs=(split, split, split, P("dev", None, None)),
        check_vma=False,
    )
```

```python
import functools

import jax
import jax.numpy as jnp
import numpy as np
from jax import lax
from jax.experimental import pallas as pl
from jax.experimental.pallas import tpu as pltpu
from jax.sharding import PartitionSpec as P

LANES = 128
TILES_X = 128
TILE_DEV = 32
LIST_LEN = 128
CHUNK = 1024
LOG2E = 1.4426950408889634

focal_length = 1000.0
blur_floor = 0.3
adam_epsilon = 1e-08
bias_first = 1.0 - 0.9**20
bias_second = 1.0 - 0.999**20
sh_first = 0.28209479177387814
sh_second = 0.4886025119029199
sh_third = (
    1.0925484305920792,
    -1.0925484305920792,
    0.31539156525252005,
    -1.0925484305920792,
    0.5462742152960396,
)
sh_fourth = (
    -0.5900435899266435,
    2.890611442640554,
    -0.4570457994644658,
    0.3731763325901154,
    -0.4570457994644658,
    1.445305721320277,
    -0.5900435899266435,
)


def rate_values():
    values = np.full((64,), 0.000125)
    values[0:3] = 0.00016
    values[3:6] = 0.005
    values[6:10] = 0.001
    values[10] = 0.05
    values[11] = 0.0025
    values[27] = 0.0025
    values[43] = 0.0025
    return np.broadcast_to(values[:, None], (64, LANES)).astype(np.float32)


def small_turn(angle):
    square = angle * angle
    cosine = 1.0 + square * (
        -1 / 2 + square * (1 / 24 + square * (-1 / 720 + square * (1 / 40320 - square / 3628800)))
    )
    sine = angle * (
        1.0 + square * (-1 / 6 + square * (1 / 120 + square * (-1 / 5040 + square / 362880)))
    )
    return cosine, sine


def camera_frame(camera_ref, view):
    def full(k):
        return jnp.full((8, LANES), camera_ref[view, k], jnp.float32)

    (ca, sa), (cb, sb), (cc, sc) = [small_turn(full(k)) for k in range(3)]
    rot = [
        [cc * cb, cc * (sb * sa) - sc * ca, cc * (sb * ca) + sc * sa],
        [sc * cb, sc * (sb * sa) + cc * ca, sc * (sb * ca) - cc * sa],
        [-sb, cb * sa, cb * ca],
    ]
    shift = [full(3), full(4), full(5)]
    back = [rot[0][k] * shift[0] + rot[1][k] * shift[1] + rot[2][k] * shift[2] for k in range(3)]
    return [rot[0][0], rot[0][1], rot[0][2], rot[1][0], rot[1][1], rot[1][2],
            rot[2][0], rot[2][1], rot[2][2]] + shift + back


def sh_terms(along_x, along_y, along_z):
    square_x, square_y, square_z = (along_x * along_x, along_y * along_y, along_z * along_z)
    return [
        -sh_second * along_y,
        sh_second * along_z,
        -sh_second * along_x,
        sh_third[0] * along_x * along_y,
        sh_third[1] * along_y * along_z,
        sh_third[2] * (2.0 * square_z - square_x - square_y),
        sh_third[3] * along_x * along_z,
        sh_third[4] * (square_x - square_y),
        sh_fourth[0] * along_y * (3.0 * square_x - square_y),
        sh_fourth[1] * along_x * along_y * along_z,
        sh_fourth[2] * along_y * (4.0 * square_z - square_x - square_y),
        sh_fourth[3] * along_z * (2.0 * square_z - 3.0 * square_x - 3.0 * square_y),
        sh_fourth[4] * along_x * (4.0 * square_z - square_x - square_y),
        sh_fourth[5] * along_z * (square_x - square_y),
        sh_fourth[6] * along_x * (square_x - 3.0 * square_y),
    ]


def footprint(params, frame, half_width, half_height):
    rot = [frame[0:3], frame[3:6], frame[6:9]]
    shift, back = frame[9:12], frame[12:15]
    x, y, z = params[0], params[1], params[2]
    viewed = [rot[k][0] * x + rot[k][1] * y + rot[k][2] * z + shift[k] for k in range(3)]
    inverse_depth = 1.0 / viewed[2]
    screen_u = focal_length * viewed[0] * inverse_depth + half_width
    screen_v = focal_length * viewed[1] * inverse_depth + half_height
    scales = [jnp.exp(params[3 + k]) for k in range(3)]
    size = params[6] * params[6] + params[7] * params[7] + params[8] * params[8] + params[9] * params[9]
    unit = 1.0 / jnp.sqrt(size)
    w, i, j, k = [params[6 + n] * unit for n in range(4)]
    turn = [
        [1.0 - 2.0 * (j * j + k * k), 2.0 * (i * j - w * k), 2.0 * (i * k + w * j)],
        [2.0 * (i * j + w * k), 1.0 - 2.0 * (i * i + k * k), 2.0 * (j * k - w * i)],
        [2.0 * (i * k - w * j), 2.0 * (j * k + w * i), 1.0 - 2.0 * (i * i + j * j)],
    ]
    near = focal_length * inverse_depth
    slant_x = -near * viewed[0] * inverse_depth
    slant_y = -near * viewed[1] * inverse_depth
    mapping = [
        [near * rot[0][n] + slant_x * rot[2][n] for n in range(3)],
        [near * rot[1][n] + slant_y * rot[2][n] for n in range(3)],
    ]
    half = [
        [
            (mapping[m][0] * turn[0][n] + mapping[m][1] * turn[1][n] + mapping[m][2] * turn[2][n])
            * scales[n]
            for n in range(3)
        ]
        for m in range(2)
    ]

    def inner(p, q):
        return p[0] * q[0] + p[1] * q[1] + p[2] * q[2]

    cover_a = inner(half[0], half[0]) + blur_floor
    cover_b = inner(half[0], half[1])
    cover_c = inner(half[1], half[1]) + blur_floor
    towards = [x + back[0], y + back[1], z + back[2]]
    inverse_length = 1.0 / jnp.sqrt(inner(towards, towards))
    harmonics = sh_terms(*[t * inverse_length for t in towards])
    colours = []
    for channel in range(3):
        running = 0.5 + sh_first * params[11 + 16 * channel]
        for term in range(1, 16):
            running = running + harmonics[term - 1] * params[11 + 16 * channel + term]
        colours.append(jnp.maximum(running, 0.0))
    return (screen_u, screen_v, cover_a, cover_b, cover_c, *colours)


def conic_of(cover_a, cover_b, cover_c):
    inverse = 1.0 / (cover_a * cover_c - cover_b * cover_b)
    return cover_c * inverse, -cover_b * inverse, cover_a * inverse


def project(params, frame, half_width, half_height):
    u, w, cover_a, cover_b, cover_c, *colours = footprint(params, frame, half_width, half_height)
    return [u, w, *conic_of(cover_a, cover_b, cover_c), jax.nn.sigmoid(params[10]), *colours]


def turned(tiles):
    swapped = jnp.swapaxes(jnp.stack(tiles, axis=0), 0, 1)
    return [swapped[n] for n in range(8)]


def lane_pick(values, lanes):
    numbers = lax.GatherDimensionNumbers(
        offset_dims=(),
        collapsed_slice_dims=(1,),
        start_index_map=(1,),
        operand_batching_dims=(0,),
        start_indices_batching_dims=(0,),
    )
    return lax.gather(
        values, lanes[:, :, None], numbers, (1, 1), mode=lax.GatherScatterMode.PROMISE_IN_BOUNDS
    )


def pick_eight(source_ref, wanted):
    count, blocks = source_ref.shape[:2]
    high, low = wanted >> 7, wanted & 127
    held = [jnp.zeros((8, LANES), jnp.float32)] * count
    for block in range(blocks):
        hit = high == block
        for row in range(count):
            source = jnp.broadcast_to(source_ref[row, block : block + 1, :], (8, LANES))
            held[row] = jnp.where(hit, lane_pick(source, low), held[row])
    return held


def pick(source_ref, wanted_ref, picked_ref):
    def body(g, _):
        at = pl.ds(pl.multiple_of(g * 8, 8), 8)
        for row, value in enumerate(pick_eight(source_ref, wanted_ref[at, :])):
            picked_ref[row, at, :] = value
        return 0

    lax.fori_loop(0, wanted_ref.shape[0] // 8, body, 0)


def lane_block():
    return lax.broadcasted_iota(jnp.int32, (8, LANES), 1) >> 5


def block_turn(vectors):
    block = lane_block()
    out = []
    for j in range(4):
        made = None
        for i in range(4):
            shift = ((i - j) * 32) % LANES
            moved = pltpu.roll(vectors[i], shift, 1) if shift else vectors[i]
            made = moved if made is None else jnp.where(block == i, moved, made)
        out.append(made)
    return out


def device_rows(g, d):
    return pl.ds(32 * g + d, 8, stride=4)


def pack(picked_ref, message_ref):
    nothing = jnp.zeros((8, LANES), jnp.float32)
    for g in range(4):
        for a in range(3):
            rows = [
                picked_ref[4 * a + b, 8 * g : 8 * g + 8, :] if 4 * a + b < 9 else nothing
                for b in range(4)
            ]
            for d, made in enumerate(block_turn(rows)):
                message_ref[device_rows(g, d), a, :] = made


def unpack(message_ref, buffer_ref):
    for g in range(4):
        for a in range(3):
            rows = [message_ref[device_rows(g, d), a, :] for d in range(4)]
            for b, made in enumerate(block_turn(rows)):
                if 4 * a + b < 9:
                    buffer_ref[4 * a + b, 8 * g : 8 * g + 8, :] = made


def greet():
    me, devices = lax.axis_index("dev"), lax.axis_size("dev")
    barrier = pltpu.get_barrier_semaphore()

    def body(j, _):
        pl.semaphore_signal(
            barrier, inc=1, device_id=(lax.rem(me + j, devices),), device_id_type=pl.DeviceIdType.MESH
        )
        return 0

    lax.fori_loop(1, devices, body, 0)


def greeted():
    pl.semaphore_wait(pltpu.get_barrier_semaphore(), lax.axis_size("dev") - 1)


def deliver(message_ref, landing_ref, sent, landed, meanwhile=None):
    me, devices = lax.axis_index("dev"), lax.axis_size("dev")

    def remote(source, target, device):
        return pltpu.make_async_remote_copy(
            src_ref=source,
            dst_ref=target,
            send_sem=sent.at[0],
            recv_sem=landed.at[0],
            device_id=(device,),
            device_id_type=pl.DeviceIdType.MESH,
        )

    def body(j, _):
        other = lax.rem(me + j, devices)
        remote(message_ref.at[other], landing_ref.at[me], other).start()
        return 0

    lax.fori_loop(1, devices, body, 0)
    own = pltpu.make_async_copy(message_ref.at[me], landing_ref.at[me], sent.at[1])
    own.start()
    if meanwhile is not None:
        meanwhile()
    own.wait()
    several = pl.ds(0, devices - 1)
    remote(message_ref.at[several], landing_ref.at[several], lax.rem(me + 1, devices)).wait()


def project_all(view, camera_ref, params_ref, params_held, splats_ref, loaded, half):
    chunks = params_ref.shape[1] // CHUNK
    loads = [
        pltpu.make_async_copy(
            params_ref.at[:, CHUNK * k : CHUNK * (k + 1)], params_held.at[k], loaded.at[k]
        )
        for k in range(chunks)
    ]
    for load in loads:
        load.start()
    greet()
    frame = camera_frame(camera_ref, view)
    for k in range(chunks):
        loads[k].wait()
        rows = []
        for g in range(8):
            rows += turned([param_tile(params_held, k, g, c) for c in range(8)])
        splats = project(rows, frame, *half)
        for n in range(9):
            splats_ref[n, 8 * k : 8 * k + 8, :] = splats[n]


def param_tile(params_held, k, g, c):
    at = slice(LANES * c, LANES * (c + 1))
    if g < 7:
        return params_held[k, 8 * g : 8 * g + 8, at]
    return jnp.concatenate([params_held[k, 56:59, at], jnp.zeros((5, LANES), jnp.float32)], axis=0)


def list_order(lists_ref, turn_ref, order_ref):
    turn_ref[...] = jnp.transpose(jnp.concatenate([lists_ref[...]] * 4, axis=0))
    block = lax.broadcasted_iota(jnp.int32, (32, LANES), 1) >> 5
    made = None
    for part in range(4):
        value = turn_ref[pl.ds(part, 32, stride=4), :]
        made = value if made is None else jnp.where(block == part, value, made)
    order_ref[...] = made


def goal_order(targets_ref, goals_ref):
    for c in range(3):
        left, right = targets_ref[c, :, 0:128], targets_ref[c, :, 128:256]
        stacked = jnp.concatenate(
            [left, pltpu.roll(left, 64, 1), right, pltpu.roll(right, 64, 1)], axis=0
        )
        goals_ref[c] = jnp.transpose(stacked)[0:64, :]


def inverse_of(ids_ref, blocks):
    lane = lax.broadcasted_iota(jnp.int32, (blocks, LANES), 1)
    row_id = lax.broadcasted_iota(jnp.int32, (blocks, LANES), 0)
    low_id = lax.broadcasted_iota(jnp.int32, (LANES, LANES), 0)
    lane_digit = (lane + 1).astype(jnp.float32)

    def body(j, total):
        ids = ids_ref[pl.ds(j, 1), :]
        hit = row_id == (ids >> 7)
        digit = jnp.full((blocks, LANES), j, jnp.int32).astype(jnp.float32)
        left = jnp.concatenate(
            [jnp.where(hit, lane_digit, 0.0), jnp.where(hit, digit, 0.0)], axis=0
        ).astype(jnp.bfloat16)
        right = jnp.where(low_id == (ids & 127), 1.0, 0.0).astype(jnp.bfloat16)
        return total + lax.dot_general(
            left, right, (((1,), (1,)), ((), ())), preferred_element_type=jnp.float32
        )

    total = lax.fori_loop(0, ids_ref.shape[0], body, jnp.zeros((2 * blocks, LANES), jnp.float32), unroll=4)
    return (total[blocks:] * 128.0 + total[:blocks]).astype(jnp.int32) - 1


def entry_rows(picked_ref, rows_ref):
    block = lane_block()
    scale = {2: -0.5 * LOG2E, 3: -LOG2E, 4: -0.5 * LOG2E}
    for row in range(9):
        for g in range(4):
            value = picked_ref[row, 8 * g : 8 * g + 8, :]
            if row in scale:
                value = value * scale[row]
            moved = [value] + [pltpu.roll(value, 32 * k, 1) for k in range(1, 4)]
            for part in range(4):
                made = moved[(0 - part) % 4]
                for b in range(1, 4):
                    made = jnp.where(block == b, moved[(b - part) % 4], made)
                rows_ref[4 * row + part, 8 * g : 8 * g + 8, :] = made


def pixel_places(tiles_ref):
    lane = lax.broadcasted_iota(jnp.int32, (8, LANES), 1)
    sub = lax.broadcasted_iota(jnp.int32, (8, LANES), 0)
    tiles = jnp.broadcast_to(jnp.concatenate([tiles_ref[...]] * 4, axis=1), (8, LANES))
    column = (tiles & (TILES_X - 1)) * 16 + sub
    row = (tiles >> 7) * 16 + (lane >> 5) * 4
    across = [column.astype(jnp.float32) + (0.5 + 8 * p) for p in range(2)]
    down = [row.astype(jnp.float32) + (0.5 + q) for q in range(4)]
    return across, down


def splat_at(rows_ref, j, part):
    return [
        jnp.broadcast_to(rows_ref[4 * row + part, pl.ds(j, 1), :], (8, LANES)) for row in range(9)
    ]


def composite(rows_ref, across, down, keep):
    def body(j, carry):
        clear, light = list(carry[:8]), [list(carry[8 + 8 * c : 16 + 8 * c]) for c in range(3)]
        for part in range(4):
            u, w, a, b, c2, o, *colour = splat_at(rows_ref, j, part)
            dx = [u - x for x in across]
            dy = [w - y for y in down]
            ax = [a * d for d in dx]
            by = [b * d for d in dy]
            cy = [c2 * d * d for d in dy]
            for v in range(8):
                q, p = v // 2, v % 2
                alpha = o * jnp.exp2((ax[p] + by[q]) * dx[p] + cy[q])
                weight = clear[v] * alpha
                if keep is not None:
                    keep[0][j, part * 8 + v] = alpha
                    keep[1][j, part * 8 + v] = weight
                clear[v] = clear[v] - weight
                for c in range(3):
                    light[c][v] = light[c][v] + colour[c] * weight
        return (*clear, *light[0], *light[1], *light[2])

    start = tuple([jnp.ones((8, LANES), jnp.float32)] * 8 + [jnp.zeros((8, LANES), jnp.float32)] * 24)
    done = lax.fori_loop(0, LIST_LEN // 4, body, start)
    return [done[8 + 8 * c : 16 + 8 * c] for c in range(3)]


def train_kernel(
    camera_ref, params_ref, send_ref, lists_ref, tiles_ref, targets_ref, returned_ref, from_send_ref,
    params_held, splats_ref, buffer_ref, picked_ref, rows_ref, alpha_ref, weight_ref, sums_ref,
    miss_ref, message_ref, landing_ref, turn_ref, order_ref, from_list_ref, goals_ref,
    loaded, sent, landed, sent_back, landed_back, *, half,
):
    project_all(0, camera_ref, params_ref, params_held, splats_ref, loaded, half)
    pick(splats_ref, send_ref, picked_ref)
    pack(picked_ref, message_ref.at[0])
    greeted()

    def before_landing():
        list_order(lists_ref, turn_ref, order_ref)
        goal_order(targets_ref, goals_ref)
        from_list_ref[...] = inverse_of(order_ref, 32)

    deliver(message_ref.at[0], landing_ref, sent, landed, before_landing)
    unpack(landing_ref, buffer_ref)
    pick(buffer_ref, order_ref, picked_ref)
    entry_rows(picked_ref, rows_ref)
    across, down = pixel_places(tiles_ref)
    light = composite(rows_ref, across, down, (alpha_ref, weight_ref))
    for c in range(3):
        for v in range(8):
            miss_ref[8 * c + v] = light[c][v] - goals_ref[c, 8 * v : 8 * v + 8, :]

    def body(step, behind):
        j = LIST_LEN // 4 - 1 - step
        behind = list(behind)
        for part in (3, 2, 1, 0):
            u, w, _, _, _, _, *colour = splat_at(rows_ref, j, part)
            dx = [u - x for x in across]
            dy = [w - y for y in down]
            pull = []
            tint = [None] * 3
            for v in range(8):
                alpha = alpha_ref[j, part * 8 + v]
                weight = weight_ref[j, part * 8 + v]
                miss = [miss_ref[8 * c + v] for c in range(3)]
                ahead = colour[0] * miss[0] + colour[1] * miss[1] + colour[2] * miss[2] - behind[v]
                pull.append(weight * ahead)
                behind[v] = behind[v] + alpha * ahead
                for c in range(3):
                    term = weight * miss[c]
                    tint[c] = term if tint[c] is None else tint[c] + term
            row_pull = [pull[2 * q] + pull[2 * q + 1] for q in range(4)]
            row_down = [row_pull[q] * dy[q] for q in range(4)]
            col_pull = [pull[p] + pull[2 + p] + pull[4 + p] + pull[6 + p] for p in range(2)]
            col_down = [
                pull[p] * dy[0] + pull[2 + p] * dy[1] + pull[4 + p] * dy[2] + pull[6 + p] * dy[3]
                for p in range(2)
            ]
            col_across = [col_pull[p] * dx[p] for p in range(2)]
            sums = [
                col_across[0] + col_across[1],
                row_down[0] + row_down[1] + row_down[2] + row_down[3],
                col_across[0] * dx[0] + col_across[1] * dx[1],
                col_down[0] * dx[0] + col_down[1] * dx[1],
                row_down[0] * dy[0] + row_down[1] * dy[1] + row_down[2] * dy[2] + row_down[3] * dy[3],
                col_pull[0] + col_pull[1],
                *tint,
            ]
            for n in range(9):
                sums_ref[4 * n + part, pl.ds(j, 1), :] = jnp.sum(sums[n], axis=0, keepdims=True)
        return tuple(behind)

    lax.fori_loop(0, LIST_LEN // 4, body, tuple([jnp.zeros((8, LANES), jnp.float32)] * 8))

    block = lane_block()
    for g in range(4):
        moment = []
        for n in range(9):
            made = None
            for part in range(4):
                value = sums_ref[4 * n + part, 8 * g : 8 * g + 8, :]
                value = value + pltpu.roll(value, 64, 1)
                value = value + pltpu.roll(value, 32, 1)
                made = value if made is None else jnp.where(block == part, value, made)
            moment.append(made)
        a, b, c2 = [picked_ref[n, 8 * g : 8 * g + 8, :] for n in (2, 3, 4)]
        grads = [
            -(a * moment[0] + b * moment[1]),
            -(c2 * moment[1] + b * moment[0]),
            -0.5 * moment[2],
            -moment[3],
            -0.5 * moment[4],
            *moment[5:],
        ]
        for n in range(9):
            buffer_ref[n, 8 * g : 8 * g + 8, :] = grads[n]
    pick(buffer_ref, from_list_ref, picked_ref)
    pack(picked_ref, message_ref.at[1])

    def before_return():
        from_send_ref[...] = inverse_of(send_ref, from_send_ref.shape[0])

    deliver(message_ref.at[1], returned_ref, sent_back, landed_back, before_return)


def update_kernel(
    camera_ref, rates_ref, back_ref, inverse_ref, params_ref, first_ref, second_ref,
    new_params_ref, new_first_ref, new_second_ref,
    buffer_ref, frame_ref, *, half,
):
    step = pl.program_id(0)

    @pl.when(step == 0)
    def _():
        unpack(back_ref, buffer_ref)
        for n, entry in enumerate(camera_frame(camera_ref, 0)):
            frame_ref[n] = entry

    slot_grads = pick_eight(buffer_ref, inverse_ref[...])
    rows = []
    for g in range(8):
        rows += turned([params_ref[8 * g : 8 * g + 8, LANES * c : LANES * (c + 1)] for c in range(8)])
    frame = [frame_ref[n] for n in range(15)]
    used = rows[:10] + [None] + rows[11:59]

    def view_first(*leaves):
        return footprint(list(leaves[:10]) + [None] + list(leaves[10:]), frame, *half)

    made, pullback = jax.vjp(view_first, *(used[:10] + used[11:]))
    ka, kb, kc = conic_of(*made[2:5])
    ga, gb, gc = slot_grads[2], 0.5 * slot_grads[3], slot_grads[4]
    left = [[ka * ga + kb * gb, ka * gb + kb * gc], [kb * ga + kc * gb, kb * gb + kc * gc]]
    cover_grads = (
        -(left[0][0] * ka + left[0][1] * kb),
        -2.0 * (left[0][0] * kb + left[0][1] * kc),
        -(left[1][0] * kb + left[1][1] * kc),
    )
    grads = list(pullback((slot_grads[0], slot_grads[1], *cover_grads, *slot_grads[6:])))
    opacity_grad = slot_grads[5] * (1.0 - jax.nn.sigmoid(rows[10]))
    grads = grads[:10] + [opacity_grad] + grads[10:] + [jnp.zeros((8, LANES), jnp.float32)] * 5
    for g in range(8):
        columns = turned(grads[8 * g : 8 * g + 8])
        rate = rates_ref[8 * g : 8 * g + 8, :]
        for c in range(8):
            at = (slice(8 * g, 8 * g + 8), slice(LANES * c, LANES * (c + 1)))
            gradient = columns[c]
            first = 0.9 * first_ref[at] + 0.1 * gradient
            second = 0.999 * second_ref[at] + 0.001 * gradient * gradient
            value = params_ref[at] - rate * (first * (1.0 / bias_first)) / (
                jnp.sqrt(second * (1.0 / bias_second)) + adam_epsilon
            )
            new_first_ref[at] = first
            new_second_ref[at] = second
            new_params_ref[at] = value


def render_kernel(
    camera_ref, params_ref, send_ref, lists_ref, tiles_ref, image_ref,
    params_held, splats_ref, buffer_ref, picked_ref, rows_ref, message_ref, landing_ref,
    turn_ref, order_ref, loaded, sent, landed, *, half,
):
    project_all(1, camera_ref, params_ref, params_held, splats_ref, loaded, half)
    pick(splats_ref, send_ref, picked_ref)
    pack(picked_ref, message_ref)
    greeted()
    deliver(
        message_ref, landing_ref, sent, landed, lambda: list_order(lists_ref, turn_ref, order_ref)
    )
    unpack(landing_ref, buffer_ref)
    pick(buffer_ref, order_ref, picked_ref)
    entry_rows(picked_ref, rows_ref)
    across, down = pixel_places(tiles_ref)
    light = composite(rows_ref, across, down, None)
    for c in range(3):
        flat = jnp.concatenate(list(light[c]), axis=0)
        upright = jnp.transpose(jnp.concatenate([flat, flat], axis=0))
        pieces = [upright[32 * b : 32 * b + 32, :] for b in range(4)]
        low = lax.broadcasted_iota(jnp.int32, (32, LANES), 1) < 64
        image_ref[c, :, 0:128] = jnp.where(low, pieces[0], pieces[1])
        image_ref[c, :, 128:256] = jnp.where(low, pieces[2], pieces[3])


def vmem(shape):
    return pltpu.VMEM(shape, jnp.float32)


def whole():
    return pl.BlockSpec(memory_space=pltpu.VMEM)


def scalars():
    return pl.BlockSpec(memory_space=pltpu.SMEM)


def f32(*shape):
    return jax.ShapeDtypeStruct(shape, jnp.float32)


def shards(
    gauss_params, adam_first, adam_second, camera, send_first, send_second,
    lists_first, lists_second, tiles_first, tiles_second, targets,
):
    local = gauss_params.shape[1]
    steps, blocks = local // CHUNK, local // LANES
    devices = lax.axis_size("dev")
    half = (TILES_X * 8.0, lists_first.shape[0] * devices // TILES_X * 8.0)
    megabyte = 1024 * 1024
    streamed = pltpu.CompilerParams(vmem_limit_bytes=62 * megabyte)

    def linked(number):
        return pltpu.CompilerParams(
            vmem_limit_bytes=60 * megabyte, collective_id=number, has_side_effects=True
        )

    slots_first, slots_second = send_first.reshape(32, LANES), send_second.reshape(32, LANES)
    packet = (devices, 3, LANES)
    links = [pltpu.SemaphoreType.DMA((2,)), pltpu.SemaphoreType.DMA((1,))]
    loading = pltpu.SemaphoreType.DMA((steps,))
    held = [vmem((steps, 59, CHUNK)), vmem((9, blocks, LANES)), vmem((9, 32, LANES)), vmem((9, 32, LANES))]
    anywhere = pl.BlockSpec(memory_space=pl.ANY)

    def integers(*shape):
        return pltpu.VMEM(shape, jnp.int32)

    returned, from_send = pl.pallas_call(
        functools.partial(train_kernel, half=half),
        out_shape=(f32(*packet), jax.ShapeDtypeStruct((blocks, LANES), jnp.int32)),
        in_specs=[scalars(), anywhere, whole(), whole(), whole(), whole()],
        out_specs=(whole(), whole()),
        scratch_shapes=[
            *held, vmem((36, 32, LANES)), vmem((32, 32, 8, LANES)), vmem((32, 32, 8, LANES)),
            vmem((36, 32, LANES)), vmem((24, 8, LANES)), vmem((2, *packet)), vmem(packet),
            integers(LANES, LANES), integers(32, LANES), integers(32, LANES), vmem((3, 64, LANES)),
            loading, *links, *links,
        ],
        compiler_params=linked(1),
        name="train",
    )(camera, gauss_params, slots_first, lists_first, tiles_first[None], jnp.transpose(targets, (1, 0, 2)))
    block = pl.BlockSpec((64, CHUNK), lambda i: (0, i))
    new_params, new_first, new_second = pl.pallas_call(
        functools.partial(update_kernel, half=half),
        grid=(steps,),
        out_shape=(f32(59, local), f32(59, local), f32(59, local)),
        in_specs=[
            scalars(),
            pl.BlockSpec((64, LANES), lambda i: (0, 0)),
            pl.BlockSpec(packet, lambda i: (0, 0, 0)),
            pl.BlockSpec((8, LANES), lambda i: (i, 0)),
            block, block, block,
        ],
        out_specs=(block, block, block),
        scratch_shapes=[vmem((9, 32, LANES)), vmem((15, 8, LANES))],
        compiler_params=streamed,
        name="update",
    )(camera, jnp.asarray(rate_values()), returned, from_send, gauss_params, adam_first, adam_second)
    image = pl.pallas_call(
        functools.partial(render_kernel, half=half),
        out_shape=f32(3, TILE_DEV, 256),
        in_specs=[scalars(), anywhere, whole(), whole(), whole()],
        out_specs=whole(),
        scratch_shapes=[
            *held, vmem((36, 32, LANES)), vmem(packet), vmem(packet),
            integers(LANES, LANES), integers(32, LANES), loading, *links,
        ],
        compiler_params=linked(2),
        name="render",
    )(camera, new_params, slots_second, lists_second, tiles_second[None])
    return (new_params, new_first, new_second, jnp.transpose(image, (1, 0, 2)))


def solution(mesh):
    split = P(None, "dev")
    rows = P("dev", None)
    return jax.shard_map(
        shards,
        mesh=mesh,
        in_specs=(split, split, split, P(), rows, rows, rows, rows, P("dev"), P("dev"), P("dev", None, None)),
        out_specs=(split, split, split, P("dev", None, None)),
        check_vma=False,
    )
```

```python
import functools

import jax
import jax.numpy as jnp
import numpy as np
from jax import lax
from jax.experimental import pallas as pl
from jax.experimental.pallas import tpu as pltpu
from jax.sharding import PartitionSpec as P

LANES = 128
TILES_X = 128
TILE_DEV = 32
LIST_LEN = 128
CHUNK = 1024
LOG2E = 1.4426950408889634

focal_length = 1000.0
blur_floor = 0.3
adam_epsilon = 1e-08
bias_first = 1.0 - 0.9**20
bias_second = 1.0 - 0.999**20
sh_first = 0.28209479177387814
sh_second = 0.4886025119029199
sh_third = (
    1.0925484305920792,
    -1.0925484305920792,
    0.31539156525252005,
    -1.0925484305920792,
    0.5462742152960396,
)
sh_fourth = (
    -0.5900435899266435,
    2.890611442640554,
    -0.4570457994644658,
    0.3731763325901154,
    -0.4570457994644658,
    1.445305721320277,
    -0.5900435899266435,
)


def rate_values():
    values = np.full((64,), 0.000125)
    values[0:3] = 0.00016
    values[3:6] = 0.005
    values[6:10] = 0.001
    values[10] = 0.05
    values[11] = 0.0025
    values[27] = 0.0025
    values[43] = 0.0025
    return np.broadcast_to(values[:, None], (64, LANES)).astype(np.float32)


def small_turn(angle):
    square = angle * angle
    cosine = 1.0 + square * (
        -1 / 2 + square * (1 / 24 + square * (-1 / 720 + square * (1 / 40320 - square / 3628800)))
    )
    sine = angle * (
        1.0 + square * (-1 / 6 + square * (1 / 120 + square * (-1 / 5040 + square / 362880)))
    )
    return cosine, sine


def camera_frame(camera_ref, view):
    def full(k):
        return jnp.full((8, LANES), camera_ref[view, k], jnp.float32)

    (ca, sa), (cb, sb), (cc, sc) = [small_turn(full(k)) for k in range(3)]
    rot = [
        [cc * cb, cc * (sb * sa) - sc * ca, cc * (sb * ca) + sc * sa],
        [sc * cb, sc * (sb * sa) + cc * ca, sc * (sb * ca) - cc * sa],
        [-sb, cb * sa, cb * ca],
    ]
    shift = [full(3), full(4), full(5)]
    back = [rot[0][k] * shift[0] + rot[1][k] * shift[1] + rot[2][k] * shift[2] for k in range(3)]
    return [rot[0][0], rot[0][1], rot[0][2], rot[1][0], rot[1][1], rot[1][2],
            rot[2][0], rot[2][1], rot[2][2]] + shift + back


def sh_terms(along_x, along_y, along_z):
    square_x, square_y, square_z = (along_x * along_x, along_y * along_y, along_z * along_z)
    return [
        -sh_second * along_y,
        sh_second * along_z,
        -sh_second * along_x,
        sh_third[0] * along_x * along_y,
        sh_third[1] * along_y * along_z,
        sh_third[2] * (2.0 * square_z - square_x - square_y),
        sh_third[3] * along_x * along_z,
        sh_third[4] * (square_x - square_y),
        sh_fourth[0] * along_y * (3.0 * square_x - square_y),
        sh_fourth[1] * along_x * along_y * along_z,
        sh_fourth[2] * along_y * (4.0 * square_z - square_x - square_y),
        sh_fourth[3] * along_z * (2.0 * square_z - 3.0 * square_x - 3.0 * square_y),
        sh_fourth[4] * along_x * (4.0 * square_z - square_x - square_y),
        sh_fourth[5] * along_z * (square_x - square_y),
        sh_fourth[6] * along_x * (square_x - 3.0 * square_y),
    ]


def footprint(params, frame, half_width, half_height):
    rot = [frame[0:3], frame[3:6], frame[6:9]]
    shift, back = frame[9:12], frame[12:15]
    x, y, z = params[0], params[1], params[2]
    viewed = [rot[k][0] * x + rot[k][1] * y + rot[k][2] * z + shift[k] for k in range(3)]
    inverse_depth = 1.0 / viewed[2]
    screen_u = focal_length * viewed[0] * inverse_depth + half_width
    screen_v = focal_length * viewed[1] * inverse_depth + half_height
    scales = [jnp.exp(params[3 + k]) for k in range(3)]
    size = params[6] * params[6] + params[7] * params[7] + params[8] * params[8] + params[9] * params[9]
    unit = 1.0 / jnp.sqrt(size)
    w, i, j, k = [params[6 + n] * unit for n in range(4)]
    turn = [
        [1.0 - 2.0 * (j * j + k * k), 2.0 * (i * j - w * k), 2.0 * (i * k + w * j)],
        [2.0 * (i * j + w * k), 1.0 - 2.0 * (i * i + k * k), 2.0 * (j * k - w * i)],
        [2.0 * (i * k - w * j), 2.0 * (j * k + w * i), 1.0 - 2.0 * (i * i + j * j)],
    ]
    near = focal_length * inverse_depth
    slant_x = -near * viewed[0] * inverse_depth
    slant_y = -near * viewed[1] * inverse_depth
    mapping = [
        [near * rot[0][n] + slant_x * rot[2][n] for n in range(3)],
        [near * rot[1][n] + slant_y * rot[2][n] for n in range(3)],
    ]
    half = [
        [
            (mapping[m][0] * turn[0][n] + mapping[m][1] * turn[1][n] + mapping[m][2] * turn[2][n])
            * scales[n]
            for n in range(3)
        ]
        for m in range(2)
    ]

    def inner(p, q):
        return p[0] * q[0] + p[1] * q[1] + p[2] * q[2]

    cover_a = inner(half[0], half[0]) + blur_floor
    cover_b = inner(half[0], half[1])
    cover_c = inner(half[1], half[1]) + blur_floor
    towards = [x + back[0], y + back[1], z + back[2]]
    inverse_length = 1.0 / jnp.sqrt(inner(towards, towards))
    harmonics = sh_terms(*[t * inverse_length for t in towards])
    colours = []
    for channel in range(3):
        running = 0.5 + sh_first * params[11 + 16 * channel]
        for term in range(1, 16):
            running = running + harmonics[term - 1] * params[11 + 16 * channel + term]
        colours.append(jnp.maximum(running, 0.0))
    return (screen_u, screen_v, cover_a, cover_b, cover_c, *colours)


def conic_of(cover_a, cover_b, cover_c):
    inverse = 1.0 / (cover_a * cover_c - cover_b * cover_b)
    return cover_c * inverse, -cover_b * inverse, cover_a * inverse


def project(params, frame, half_width, half_height):
    u, w, cover_a, cover_b, cover_c, *colours = footprint(params, frame, half_width, half_height)
    return [u, w, *conic_of(cover_a, cover_b, cover_c), jax.nn.sigmoid(params[10]), *colours]


def turned(tiles):
    swapped = jnp.swapaxes(jnp.stack(tiles, axis=0), 0, 1)
    return [swapped[n] for n in range(8)]


def lane_pick(values, lanes):
    numbers = lax.GatherDimensionNumbers(
        offset_dims=(),
        collapsed_slice_dims=(1,),
        start_index_map=(1,),
        operand_batching_dims=(0,),
        start_indices_batching_dims=(0,),
    )
    return lax.gather(
        values, lanes[:, :, None], numbers, (1, 1), mode=lax.GatherScatterMode.PROMISE_IN_BOUNDS
    )


def pick_eight(source_ref, wanted):
    count, blocks = source_ref.shape[:2]
    high, low = wanted >> 7, wanted & 127
    held = [jnp.zeros((8, LANES), jnp.float32)] * count
    for block in range(blocks):
        hit = high == block
        for row in range(count):
            source = jnp.broadcast_to(source_ref[row, block : block + 1, :], (8, LANES))
            held[row] = jnp.where(hit, lane_pick(source, low), held[row])
    return held


def pick(source_ref, wanted_ref, picked_ref):
    def body(g, _):
        at = pl.ds(pl.multiple_of(g * 8, 8), 8)
        for row, value in enumerate(pick_eight(source_ref, wanted_ref[at, :])):
            picked_ref[row, at, :] = value
        return 0

    lax.fori_loop(0, wanted_ref.shape[0] // 8, body, 0)


def lane_block():
    return lax.broadcasted_iota(jnp.int32, (8, LANES), 1) >> 5


def block_turn(vectors):
    block = lane_block()
    out = []
    for j in range(4):
        made = None
        for i in range(4):
            shift = ((i - j) * 32) % LANES
            moved = pltpu.roll(vectors[i], shift, 1) if shift else vectors[i]
            made = moved if made is None else jnp.where(block == i, moved, made)
        out.append(made)
    return out


def device_rows(g, d):
    return pl.ds(32 * g + d, 8, stride=4)


def pack_group(values, message_ref, g):
    nothing = jnp.zeros((8, LANES), jnp.float32)
    for a in range(3):
        rows = [values[4 * a + b] if 4 * a + b < 9 else nothing for b in range(4)]
        for d, made in enumerate(block_turn(rows)):
            message_ref[device_rows(g, d), a, :] = made


def unpack(message_ref, buffer_ref):
    for g in range(4):
        for a in range(3):
            rows = [message_ref[device_rows(g, d), a, :] for d in range(4)]
            for b, made in enumerate(block_turn(rows)):
                if 4 * a + b < 9:
                    buffer_ref[4 * a + b, 8 * g : 8 * g + 8, :] = made


def greet():
    me, devices = lax.axis_index("dev"), lax.axis_size("dev")
    barrier = pltpu.get_barrier_semaphore()

    def body(j, _):
        pl.semaphore_signal(
            barrier, inc=1, device_id=(lax.rem(me + j, devices),), device_id_type=pl.DeviceIdType.MESH
        )
        return 0

    lax.fori_loop(1, devices, body, 0)


def greeted():
    pl.semaphore_wait(pltpu.get_barrier_semaphore(), lax.axis_size("dev") - 1)


def deliver(
    source_ref, wanted_ref, message_ref, landing_ref, sent, landed, ready, meanwhile
):
    me, devices = lax.axis_index("dev"), lax.axis_size("dev")
    share = devices // 4
    home, place = lax.div(me, share), lax.rem(me, share)

    def remote(source, target, device):
        return pltpu.make_async_remote_copy(
            src_ref=source,
            dst_ref=target,
            send_sem=sent.at[0],
            recv_sem=landed.at[0],
            device_id=(device,),
            device_id_type=pl.DeviceIdType.MESH,
        )

    for ahead in (2, 1, 3, 0):
        g = lax.rem(home + ahead, 4)
        at = pl.ds(pl.multiple_of(g * 8, 8), 8)
        pack_group(pick_eight(source_ref, wanted_ref[at, :]), message_ref, g)
        if ahead == 2 and ready is not None:
            ready()

        def body(i, _):
            other = g * share + lax.rem(place + i, share)
            remote(message_ref.at[other], landing_ref.at[me], other).start()
            return 0

        if ahead:
            lax.fori_loop(share // 2, share + share // 2, body, 0)
        else:
            lax.fori_loop(1, share, body, 0)
    own = pltpu.make_async_copy(message_ref.at[me], landing_ref.at[me], sent.at[1])
    own.start()
    meanwhile()
    own.wait()
    several = pl.ds(0, devices - 1)
    remote(message_ref.at[several], landing_ref.at[several], lax.rem(me + 1, devices)).wait()


def project_all(view, camera_ref, params_ref, params_held, splats_ref, loaded, half):
    chunks = params_ref.shape[1] // CHUNK
    loads = [
        pltpu.make_async_copy(
            params_ref.at[:, CHUNK * k : CHUNK * (k + 1)], params_held.at[k], loaded.at[k]
        )
        for k in range(chunks)
    ]
    for load in loads:
        load.start()
    greet()
    frame = camera_frame(camera_ref, view)
    for k in range(chunks):
        loads[k].wait()
        rows = []
        for g in range(8):
            rows += turned([param_tile(params_held, k, g, c) for c in range(8)])
        splats = project(rows, frame, *half)
        for n in range(9):
            splats_ref[n, 8 * k : 8 * k + 8, :] = splats[n]


def param_tile(params_held, k, g, c):
    at = slice(LANES * c, LANES * (c + 1))
    if g < 7:
        return params_held[k, 8 * g : 8 * g + 8, at]
    return jnp.concatenate([params_held[k, 56:59, at], jnp.zeros((5, LANES), jnp.float32)], axis=0)


def list_order(lists_ref, turn_ref, order_ref):
    turn_ref[...] = jnp.transpose(jnp.concatenate([lists_ref[...]] * 4, axis=0))
    block = lax.broadcasted_iota(jnp.int32, (32, LANES), 1) >> 5
    made = None
    for part in range(4):
        value = turn_ref[pl.ds(part, 32, stride=4), :]
        made = value if made is None else jnp.where(block == part, value, made)
    order_ref[...] = made


def goal_order(targets_ref, goals_ref):
    for c in range(3):
        left, right = targets_ref[c, :, 0:128], targets_ref[c, :, 128:256]
        stacked = jnp.concatenate(
            [left, pltpu.roll(left, 64, 1), right, pltpu.roll(right, 64, 1)], axis=0
        )
        goals_ref[c] = jnp.transpose(stacked)[0:64, :]


def inverse_of(ids_ref, blocks):
    lane = lax.broadcasted_iota(jnp.int32, (blocks, LANES), 1)
    row_id = lax.broadcasted_iota(jnp.int32, (blocks, LANES), 0)
    low_id = lax.broadcasted_iota(jnp.int32, (LANES, LANES), 0)
    lane_digit = (lane + 1).astype(jnp.float32)

    def body(j, total):
        ids = ids_ref[pl.ds(j, 1), :]
        hit = row_id == (ids >> 7)
        digit = jnp.full((blocks, LANES), j, jnp.int32).astype(jnp.float32)
        left = jnp.concatenate(
            [jnp.where(hit, lane_digit, 0.0), jnp.where(hit, digit, 0.0)], axis=0
        ).astype(jnp.bfloat16)
        right = jnp.where(low_id == (ids & 127), 1.0, 0.0).astype(jnp.bfloat16)
        return total + lax.dot_general(
            left, right, (((1,), (1,)), ((), ())), preferred_element_type=jnp.float32
        )

    total = lax.fori_loop(0, ids_ref.shape[0], body, jnp.zeros((2 * blocks, LANES), jnp.float32), unroll=4)
    return (total[blocks:] * 128.0 + total[:blocks]).astype(jnp.int32) - 1


def entry_rows(picked_ref, rows_ref):
    block = lane_block()
    scale = {2: -0.5 * LOG2E, 3: -LOG2E, 4: -0.5 * LOG2E}
    for row in range(9):
        for g in range(4):
            value = picked_ref[row, 8 * g : 8 * g + 8, :]
            if row in scale:
                value = value * scale[row]
            moved = [value] + [pltpu.roll(value, 32 * k, 1) for k in range(1, 4)]
            for part in range(4):
                made = moved[(0 - part) % 4]
                for b in range(1, 4):
                    made = jnp.where(block == b, moved[(b - part) % 4], made)
                rows_ref[4 * row + part, 8 * g : 8 * g + 8, :] = made


def pixel_places(tiles_ref):
    lane = lax.broadcasted_iota(jnp.int32, (8, LANES), 1)
    sub = lax.broadcasted_iota(jnp.int32, (8, LANES), 0)
    tiles = jnp.broadcast_to(jnp.concatenate([tiles_ref[...]] * 4, axis=1), (8, LANES))
    column = (tiles & (TILES_X - 1)) * 16 + sub
    row = (tiles >> 7) * 16 + (lane >> 5) * 4
    across = [column.astype(jnp.float32) + (0.5 + 8 * p) for p in range(2)]
    down = [row.astype(jnp.float32) + (0.5 + q) for q in range(4)]
    return across, down


def splat_at(rows_ref, j, part):
    return [
        jnp.broadcast_to(rows_ref[4 * row + part, pl.ds(j, 1), :], (8, LANES)) for row in range(9)
    ]


def composite(rows_ref, across, down, keep):
    def body(j, carry):
        clear, light = list(carry[:8]), [list(carry[8 + 8 * c : 16 + 8 * c]) for c in range(3)]
        for part in range(4):
            u, w, a, b, c2, o, *colour = splat_at(rows_ref, j, part)
            dx = [u - x for x in across]
            dy = [w - y for y in down]
            ax = [a * d for d in dx]
            by = [b * d for d in dy]
            cy = [c2 * d * d for d in dy]
            for v in range(8):
                q, p = v // 2, v % 2
                alpha = o * jnp.exp2((ax[p] + by[q]) * dx[p] + cy[q])
                weight = clear[v] * alpha
                if keep is not None:
                    keep[0][j, part * 8 + v] = alpha
                    keep[1][j, part * 8 + v] = weight
                clear[v] = clear[v] - weight
                for c in range(3):
                    light[c][v] = light[c][v] + colour[c] * weight
        return (*clear, *light[0], *light[1], *light[2])

    start = tuple([jnp.ones((8, LANES), jnp.float32)] * 8 + [jnp.zeros((8, LANES), jnp.float32)] * 24)
    done = lax.fori_loop(0, LIST_LEN // 4, body, start)
    return [done[8 + 8 * c : 16 + 8 * c] for c in range(3)]


def train_kernel(
    camera_ref, params_ref, send_ref, lists_ref, tiles_ref, targets_ref, returned_ref, from_send_ref,
    params_held, splats_ref, buffer_ref, picked_ref, rows_ref, alpha_ref, weight_ref, sums_ref,
    miss_ref, message_ref, landing_ref, turn_ref, order_ref, from_list_ref, goals_ref,
    loaded, sent, landed, sent_back, landed_back, *, half,
):
    project_all(0, camera_ref, params_ref, params_held, splats_ref, loaded, half)
    def before_landing():
        list_order(lists_ref, turn_ref, order_ref)
        goal_order(targets_ref, goals_ref)
        from_list_ref[...] = inverse_of(order_ref, 32)

    deliver(
        splats_ref, send_ref, message_ref.at[0], landing_ref, sent, landed, greeted, before_landing
    )
    unpack(landing_ref, buffer_ref)
    pick(buffer_ref, order_ref, picked_ref)
    entry_rows(picked_ref, rows_ref)
    across, down = pixel_places(tiles_ref)
    light = composite(rows_ref, across, down, (alpha_ref, weight_ref))
    for c in range(3):
        for v in range(8):
            miss_ref[8 * c + v] = light[c][v] - goals_ref[c, 8 * v : 8 * v + 8, :]

    def body(step, behind):
        j = LIST_LEN // 4 - 1 - step
        behind = list(behind)
        for part in (3, 2, 1, 0):
            u, w, _, _, _, _, *colour = splat_at(rows_ref, j, part)
            dx = [u - x for x in across]
            dy = [w - y for y in down]
            pull = []
            tint = [None] * 3
            for v in range(8):
                alpha = alpha_ref[j, part * 8 + v]
                weight = weight_ref[j, part * 8 + v]
                miss = [miss_ref[8 * c + v] for c in range(3)]
                ahead = colour[0] * miss[0] + colour[1] * miss[1] + colour[2] * miss[2] - behind[v]
                pull.append(weight * ahead)
                behind[v] = behind[v] + alpha * ahead
                for c in range(3):
                    term = weight * miss[c]
                    tint[c] = term if tint[c] is None else tint[c] + term
            row_pull = [pull[2 * q] + pull[2 * q + 1] for q in range(4)]
            row_down = [row_pull[q] * dy[q] for q in range(4)]
            col_pull = [pull[p] + pull[2 + p] + pull[4 + p] + pull[6 + p] for p in range(2)]
            col_down = [
                pull[p] * dy[0] + pull[2 + p] * dy[1] + pull[4 + p] * dy[2] + pull[6 + p] * dy[3]
                for p in range(2)
            ]
            col_across = [col_pull[p] * dx[p] for p in range(2)]
            sums = [
                col_across[0] + col_across[1],
                row_down[0] + row_down[1] + row_down[2] + row_down[3],
                col_across[0] * dx[0] + col_across[1] * dx[1],
                col_down[0] * dx[0] + col_down[1] * dx[1],
                row_down[0] * dy[0] + row_down[1] * dy[1] + row_down[2] * dy[2] + row_down[3] * dy[3],
                col_pull[0] + col_pull[1],
                *tint,
            ]
            for n in range(9):
                sums_ref[4 * n + part, pl.ds(j, 1), :] = jnp.sum(sums[n], axis=0, keepdims=True)
        return tuple(behind)

    lax.fori_loop(0, LIST_LEN // 4, body, tuple([jnp.zeros((8, LANES), jnp.float32)] * 8))

    block = lane_block()
    for g in range(4):
        moment = []
        for n in range(9):
            made = None
            for part in range(4):
                value = sums_ref[4 * n + part, 8 * g : 8 * g + 8, :]
                value = value + pltpu.roll(value, 64, 1)
                value = value + pltpu.roll(value, 32, 1)
                made = value if made is None else jnp.where(block == part, value, made)
            moment.append(made)
        a, b, c2 = [picked_ref[n, 8 * g : 8 * g + 8, :] for n in (2, 3, 4)]
        grads = [
            -(a * moment[0] + b * moment[1]),
            -(c2 * moment[1] + b * moment[0]),
            -0.5 * moment[2],
            -moment[3],
            -0.5 * moment[4],
            *moment[5:],
        ]
        for n in range(9):
            buffer_ref[n, 8 * g : 8 * g + 8, :] = grads[n]

    def before_return():
        from_send_ref[...] = inverse_of(send_ref, from_send_ref.shape[0])

    deliver(
        buffer_ref, from_list_ref, message_ref.at[1], returned_ref, sent_back, landed_back,
        None, before_return,
    )


def update_kernel(
    camera_ref, rates_ref, back_ref, inverse_ref, params_ref, first_ref, second_ref,
    new_params_ref, new_first_ref, new_second_ref,
    buffer_ref, frame_ref, *, half,
):
    step = pl.program_id(0)

    @pl.when(step == 0)
    def _():
        unpack(back_ref, buffer_ref)
        for n, entry in enumerate(camera_frame(camera_ref, 0)):
            frame_ref[n] = entry

    slot_grads = pick_eight(buffer_ref, inverse_ref[...])
    rows = []
    for g in range(8):
        rows += turned([params_ref[8 * g : 8 * g + 8, LANES * c : LANES * (c + 1)] for c in range(8)])
    frame = [frame_ref[n] for n in range(15)]
    used = rows[:10] + [None] + rows[11:59]

    def view_first(*leaves):
        return footprint(list(leaves[:10]) + [None] + list(leaves[10:]), frame, *half)

    made, pullback = jax.vjp(view_first, *(used[:10] + used[11:]))
    ka, kb, kc = conic_of(*made[2:5])
    ga, gb, gc = slot_grads[2], 0.5 * slot_grads[3], slot_grads[4]
    left = [[ka * ga + kb * gb, ka * gb + kb * gc], [kb * ga + kc * gb, kb * gb + kc * gc]]
    cover_grads = (
        -(left[0][0] * ka + left[0][1] * kb),
        -2.0 * (left[0][0] * kb + left[0][1] * kc),
        -(left[1][0] * kb + left[1][1] * kc),
    )
    grads = list(pullback((slot_grads[0], slot_grads[1], *cover_grads, *slot_grads[6:])))
    opacity_grad = slot_grads[5] * (1.0 - jax.nn.sigmoid(rows[10]))
    grads = grads[:10] + [opacity_grad] + grads[10:] + [jnp.zeros((8, LANES), jnp.float32)] * 5
    for g in range(8):
        columns = turned(grads[8 * g : 8 * g + 8])
        rate = rates_ref[8 * g : 8 * g + 8, :]
        for c in range(8):
            at = (slice(8 * g, 8 * g + 8), slice(LANES * c, LANES * (c + 1)))
            gradient = columns[c]
            first = 0.9 * first_ref[at] + 0.1 * gradient
            second = 0.999 * second_ref[at] + 0.001 * gradient * gradient
            value = params_ref[at] - rate * (first * (1.0 / bias_first)) / (
                jnp.sqrt(second * (1.0 / bias_second)) + adam_epsilon
            )
            new_first_ref[at] = first
            new_second_ref[at] = second
            new_params_ref[at] = value


def render_kernel(
    camera_ref, params_ref, send_ref, lists_ref, tiles_ref, image_ref,
    params_held, splats_ref, buffer_ref, picked_ref, rows_ref, message_ref, landing_ref,
    turn_ref, order_ref, loaded, sent, landed, *, half,
):
    project_all(1, camera_ref, params_ref, params_held, splats_ref, loaded, half)
    deliver(
        splats_ref, send_ref, message_ref, landing_ref, sent, landed, greeted,
        lambda: list_order(lists_ref, turn_ref, order_ref),
    )
    unpack(landing_ref, buffer_ref)
    pick(buffer_ref, order_ref, picked_ref)
    entry_rows(picked_ref, rows_ref)
    across, down = pixel_places(tiles_ref)
    light = composite(rows_ref, across, down, None)
    for c in range(3):
        flat = jnp.concatenate(list(light[c]), axis=0)
        upright = jnp.transpose(jnp.concatenate([flat, flat], axis=0))
        pieces = [upright[32 * b : 32 * b + 32, :] for b in range(4)]
        low = lax.broadcasted_iota(jnp.int32, (32, LANES), 1) < 64
        image_ref[c, :, 0:128] = jnp.where(low, pieces[0], pieces[1])
        image_ref[c, :, 128:256] = jnp.where(low, pieces[2], pieces[3])


def vmem(shape):
    return pltpu.VMEM(shape, jnp.float32)


def whole():
    return pl.BlockSpec(memory_space=pltpu.VMEM)


def scalars():
    return pl.BlockSpec(memory_space=pltpu.SMEM)


def f32(*shape):
    return jax.ShapeDtypeStruct(shape, jnp.float32)


def shards(
    gauss_params, adam_first, adam_second, camera, send_first, send_second,
    lists_first, lists_second, tiles_first, tiles_second, targets,
):
    local = gauss_params.shape[1]
    steps, blocks = local // CHUNK, local // LANES
    devices = lax.axis_size("dev")
    half = (TILES_X * 8.0, lists_first.shape[0] * devices // TILES_X * 8.0)
    megabyte = 1024 * 1024
    streamed = pltpu.CompilerParams(vmem_limit_bytes=62 * megabyte)

    def linked(number):
        return pltpu.CompilerParams(
            vmem_limit_bytes=(60 if number == 1 else 52) * megabyte,
            collective_id=number,
            has_side_effects=True,
        )

    slots_first, slots_second = send_first.reshape(32, LANES), send_second.reshape(32, LANES)
    packet = (devices, 3, LANES)
    links = [pltpu.SemaphoreType.DMA((2,)), pltpu.SemaphoreType.DMA((1,))]
    loading = pltpu.SemaphoreType.DMA((steps,))
    held = [vmem((steps, 59, CHUNK)), vmem((9, blocks, LANES)), vmem((9, 32, LANES)), vmem((9, 32, LANES))]
    outside = pl.BlockSpec(memory_space=pltpu.HBM)

    def integers(*shape):
        return pltpu.VMEM(shape, jnp.int32)

    returned, from_send = pl.pallas_call(
        functools.partial(train_kernel, half=half),
        out_shape=(f32(*packet), jax.ShapeDtypeStruct((blocks, LANES), jnp.int32)),
        in_specs=[scalars(), outside, whole(), whole(), whole(), whole()],
        out_specs=(whole(), whole()),
        scratch_shapes=[
            *held, vmem((36, 32, LANES)), vmem((32, 32, 8, LANES)), vmem((32, 32, 8, LANES)),
            vmem((36, 32, LANES)), vmem((24, 8, LANES)), vmem((2, *packet)), vmem(packet),
            integers(LANES, LANES), integers(32, LANES), integers(32, LANES), vmem((3, 64, LANES)),
            loading, *links, *links,
        ],
        compiler_params=linked(1),
        name="train",
    )(camera, gauss_params, slots_first, lists_first, tiles_first[None], jnp.transpose(targets, (1, 0, 2)))
    block = pl.BlockSpec((64, CHUNK), lambda i: (0, i))
    new_params, new_first, new_second = pl.pallas_call(
        functools.partial(update_kernel, half=half),
        grid=(steps,),
        out_shape=(f32(59, local), f32(59, local), f32(59, local)),
        in_specs=[
            scalars(),
            pl.BlockSpec((64, LANES), lambda i: (0, 0)),
            pl.BlockSpec(packet, lambda i: (0, 0, 0)),
            pl.BlockSpec((8, LANES), lambda i: (i, 0)),
            block, block, block,
        ],
        out_specs=(block, block, block),
        scratch_shapes=[vmem((9, 32, LANES)), vmem((15, 8, LANES))],
        compiler_params=streamed,
        name="update",
    )(camera, jnp.asarray(rate_values()), returned, from_send, gauss_params, adam_first, adam_second)
    image = pl.pallas_call(
        functools.partial(render_kernel, half=half),
        out_shape=f32(3, TILE_DEV, 256),
        in_specs=[scalars(), outside, whole(), whole(), whole()],
        out_specs=whole(),
        scratch_shapes=[
            *held, vmem((36, 32, LANES)), vmem(packet), vmem(packet),
            integers(LANES, LANES), integers(32, LANES), loading, *links,
        ],
        compiler_params=linked(2),
        name="render",
    )(camera, new_params, slots_second, lists_second, tiles_second[None])
    return (new_params, new_first, new_second, jnp.transpose(image, (1, 0, 2)))


def solution(mesh):
    split = P(None, "dev")
    rows = P("dev", None)
    return jax.shard_map(
        shards,
        mesh=mesh,
        in_specs=(split, split, split, P(), rows, rows, rows, rows, P("dev"), P("dev"), P("dev", None, None)),
        out_specs=(split, split, split, P("dev", None, None)),
        check_vma=False,
    )
```

```python
import functools

import jax
import jax.numpy as jnp
import numpy as np
from jax import lax
from jax.experimental import pallas as pl
from jax.experimental.pallas import tpu as pltpu
from jax.sharding import PartitionSpec as P

LANES = 128
TILES_X = 128
TILE_DEV = 32
LIST_LEN = 128
CHUNK = 1024
LOG2E = 1.4426950408889634

focal_length = 1000.0
blur_floor = 0.3
adam_epsilon = 1e-08
bias_first = 1.0 - 0.9**20
bias_second = 1.0 - 0.999**20
sh_first = 0.28209479177387814
sh_second = 0.4886025119029199
sh_third = (
    1.0925484305920792,
    -1.0925484305920792,
    0.31539156525252005,
    -1.0925484305920792,
    0.5462742152960396,
)
sh_fourth = (
    -0.5900435899266435,
    2.890611442640554,
    -0.4570457994644658,
    0.3731763325901154,
    -0.4570457994644658,
    1.445305721320277,
    -0.5900435899266435,
)


def rate_values():
    values = np.full((64,), 0.000125)
    values[0:3] = 0.00016
    values[3:6] = 0.005
    values[6:10] = 0.001
    values[10] = 0.05
    values[11] = 0.0025
    values[27] = 0.0025
    values[43] = 0.0025
    return np.broadcast_to(values[:, None], (64, LANES)).astype(np.float32)


def small_turn(angle):
    square = angle * angle
    cosine = 1.0 + square * (
        -1 / 2 + square * (1 / 24 + square * (-1 / 720 + square * (1 / 40320 - square / 3628800)))
    )
    sine = angle * (
        1.0 + square * (-1 / 6 + square * (1 / 120 + square * (-1 / 5040 + square / 362880)))
    )
    return cosine, sine


def camera_frame(camera_ref, view):
    def full(k):
        return jnp.full((8, LANES), camera_ref[view, k], jnp.float32)

    (ca, sa), (cb, sb), (cc, sc) = [small_turn(full(k)) for k in range(3)]
    rot = [
        [cc * cb, cc * (sb * sa) - sc * ca, cc * (sb * ca) + sc * sa],
        [sc * cb, sc * (sb * sa) + cc * ca, sc * (sb * ca) - cc * sa],
        [-sb, cb * sa, cb * ca],
    ]
    shift = [full(3), full(4), full(5)]
    back = [rot[0][k] * shift[0] + rot[1][k] * shift[1] + rot[2][k] * shift[2] for k in range(3)]
    return [rot[0][0], rot[0][1], rot[0][2], rot[1][0], rot[1][1], rot[1][2],
            rot[2][0], rot[2][1], rot[2][2]] + shift + back


def sh_terms(along_x, along_y, along_z):
    square_x, square_y, square_z = (along_x * along_x, along_y * along_y, along_z * along_z)
    return [
        -sh_second * along_y,
        sh_second * along_z,
        -sh_second * along_x,
        sh_third[0] * along_x * along_y,
        sh_third[1] * along_y * along_z,
        sh_third[2] * (2.0 * square_z - square_x - square_y),
        sh_third[3] * along_x * along_z,
        sh_third[4] * (square_x - square_y),
        sh_fourth[0] * along_y * (3.0 * square_x - square_y),
        sh_fourth[1] * along_x * along_y * along_z,
        sh_fourth[2] * along_y * (4.0 * square_z - square_x - square_y),
        sh_fourth[3] * along_z * (2.0 * square_z - 3.0 * square_x - 3.0 * square_y),
        sh_fourth[4] * along_x * (4.0 * square_z - square_x - square_y),
        sh_fourth[5] * along_z * (square_x - square_y),
        sh_fourth[6] * along_x * (square_x - 3.0 * square_y),
    ]


def footprint(params, frame, half_width, half_height):
    rot = [frame[0:3], frame[3:6], frame[6:9]]
    shift, back = frame[9:12], frame[12:15]
    x, y, z = params[0], params[1], params[2]
    viewed = [rot[k][0] * x + rot[k][1] * y + rot[k][2] * z + shift[k] for k in range(3)]
    inverse_depth = 1.0 / viewed[2]
    screen_u = focal_length * viewed[0] * inverse_depth + half_width
    screen_v = focal_length * viewed[1] * inverse_depth + half_height
    scales = [jnp.exp(params[3 + k]) for k in range(3)]
    size = params[6] * params[6] + params[7] * params[7] + params[8] * params[8] + params[9] * params[9]
    unit = 1.0 / jnp.sqrt(size)
    w, i, j, k = [params[6 + n] * unit for n in range(4)]
    turn = [
        [1.0 - 2.0 * (j * j + k * k), 2.0 * (i * j - w * k), 2.0 * (i * k + w * j)],
        [2.0 * (i * j + w * k), 1.0 - 2.0 * (i * i + k * k), 2.0 * (j * k - w * i)],
        [2.0 * (i * k - w * j), 2.0 * (j * k + w * i), 1.0 - 2.0 * (i * i + j * j)],
    ]
    near = focal_length * inverse_depth
    slant_x = -near * viewed[0] * inverse_depth
    slant_y = -near * viewed[1] * inverse_depth
    mapping = [
        [near * rot[0][n] + slant_x * rot[2][n] for n in range(3)],
        [near * rot[1][n] + slant_y * rot[2][n] for n in range(3)],
    ]
    half = [
        [
            (mapping[m][0] * turn[0][n] + mapping[m][1] * turn[1][n] + mapping[m][2] * turn[2][n])
            * scales[n]
            for n in range(3)
        ]
        for m in range(2)
    ]

    def inner(p, q):
        return p[0] * q[0] + p[1] * q[1] + p[2] * q[2]

    cover_a = inner(half[0], half[0]) + blur_floor
    cover_b = inner(half[0], half[1])
    cover_c = inner(half[1], half[1]) + blur_floor
    towards = [x + back[0], y + back[1], z + back[2]]
    inverse_length = 1.0 / jnp.sqrt(inner(towards, towards))
    harmonics = sh_terms(*[t * inverse_length for t in towards])
    colours = []
    for channel in range(3):
        running = 0.5 + sh_first * params[11 + 16 * channel]
        for term in range(1, 16):
            running = running + harmonics[term - 1] * params[11 + 16 * channel + term]
        colours.append(jnp.maximum(running, 0.0))
    return (screen_u, screen_v, cover_a, cover_b, cover_c, *colours)


def conic_of(cover_a, cover_b, cover_c):
    inverse = 1.0 / (cover_a * cover_c - cover_b * cover_b)
    return cover_c * inverse, -cover_b * inverse, cover_a * inverse


def project(params, frame, half_width, half_height):
    u, w, cover_a, cover_b, cover_c, *colours = footprint(params, frame, half_width, half_height)
    return [u, w, *conic_of(cover_a, cover_b, cover_c), jax.nn.sigmoid(params[10]), *colours]


def turned(tiles):
    swapped = jnp.swapaxes(jnp.stack(tiles, axis=0), 0, 1)
    return [swapped[n] for n in range(8)]


def lane_pick(values, lanes):
    numbers = lax.GatherDimensionNumbers(
        offset_dims=(),
        collapsed_slice_dims=(1,),
        start_index_map=(1,),
        operand_batching_dims=(0,),
        start_indices_batching_dims=(0,),
    )
    return lax.gather(
        values, lanes[:, :, None], numbers, (1, 1), mode=lax.GatherScatterMode.PROMISE_IN_BOUNDS
    )


def pick_eight(source_ref, wanted):
    count, blocks = source_ref.shape[:2]
    high, low = wanted >> 7, wanted & 127
    held = [jnp.zeros((8, LANES), jnp.float32)] * count
    for block in range(blocks):
        hit = high == block
        for row in range(count):
            source = jnp.broadcast_to(source_ref[row, block : block + 1, :], (8, LANES))
            held[row] = jnp.where(hit, lane_pick(source, low), held[row])
    return held


def pick(source_ref, wanted_ref, picked_ref):
    def body(g, _):
        at = pl.ds(pl.multiple_of(g * 8, 8), 8)
        for row, value in enumerate(pick_eight(source_ref, wanted_ref[at, :])):
            picked_ref[row, at, :] = value
        return 0

    lax.fori_loop(0, wanted_ref.shape[0] // 8, body, 0)


def lane_block():
    return lax.broadcasted_iota(jnp.int32, (8, LANES), 1) >> 5


def block_turn(vectors):
    block = lane_block()
    out = []
    for j in range(4):
        made = None
        for i in range(4):
            shift = ((i - j) * 32) % LANES
            moved = pltpu.roll(vectors[i], shift, 1) if shift else vectors[i]
            made = moved if made is None else jnp.where(block == i, moved, made)
        out.append(made)
    return out


def device_rows(g, d):
    return pl.ds(32 * g + d, 8, stride=4)


def pack_group(values, message_ref, g):
    nothing = jnp.zeros((8, LANES), jnp.float32)
    for a in range(3):
        rows = [values[4 * a + b] if 4 * a + b < 9 else nothing for b in range(4)]
        for d, made in enumerate(block_turn(rows)):
            message_ref[device_rows(g, d), a, :] = made


def unpack(message_ref, buffer_ref):
    for g in range(4):
        for a in range(3):
            rows = [message_ref[device_rows(g, d), a, :] for d in range(4)]
            for b, made in enumerate(block_turn(rows)):
                if 4 * a + b < 9:
                    buffer_ref[4 * a + b, 8 * g : 8 * g + 8, :] = made


def greet():
    me, devices = lax.axis_index("dev"), lax.axis_size("dev")
    barrier = pltpu.get_barrier_semaphore()

    def body(j, _):
        pl.semaphore_signal(
            barrier, inc=1, device_id=(lax.rem(me + j, devices),), device_id_type=pl.DeviceIdType.MESH
        )
        return 0

    lax.fori_loop(1, devices, body, 0)


def greeted():
    pl.semaphore_wait(pltpu.get_barrier_semaphore(), lax.axis_size("dev") - 1)


def deliver(
    source_ref, wanted_ref, message_ref, landing_ref, sent, landed, ready, meanwhile
):
    me, devices = lax.axis_index("dev"), lax.axis_size("dev")
    share = devices // 4
    home, place = lax.div(me, share), lax.rem(me, share)

    def remote(source, target, device):
        return pltpu.make_async_remote_copy(
            src_ref=source,
            dst_ref=target,
            send_sem=sent.at[0],
            recv_sem=landed.at[0],
            device_id=(device,),
            device_id_type=pl.DeviceIdType.MESH,
        )

    for ahead in (2, 1, 3, 0):
        g = lax.rem(home + ahead, 4)
        at = pl.ds(pl.multiple_of(g * 8, 8), 8)
        pack_group(pick_eight(source_ref, wanted_ref[at, :]), message_ref, g)
        if ahead == 2 and ready is not None:
            ready()

        def body(i, _):
            other = g * share + lax.rem(place + i, share)
            remote(message_ref.at[other], landing_ref.at[me], other).start()
            return 0

        if ahead:
            lax.fori_loop(share // 2, share + share // 2, body, 0)
        else:
            lax.fori_loop(1, share, body, 0)
    own = pltpu.make_async_copy(message_ref.at[me], landing_ref.at[me], sent.at[1])
    own.start()
    meanwhile()
    own.wait()
    several = pl.ds(0, devices - 1)
    remote(message_ref.at[several], landing_ref.at[several], lax.rem(me + 1, devices)).wait()


def project_all(view, camera_ref, params_ref, params_held, splats_ref, loaded, half):
    chunks = params_ref.shape[1] // CHUNK
    loads = [
        pltpu.make_async_copy(
            params_ref.at[:, CHUNK * k : CHUNK * (k + 1)], params_held.at[k], loaded.at[k]
        )
        for k in range(chunks)
    ]
    for load in loads:
        load.start()
    greet()
    frame = camera_frame(camera_ref, view)
    for k in range(chunks):
        loads[k].wait()
        rows = []
        for g in range(8):
            rows += turned([param_tile(params_held, k, g, c) for c in range(8)])
        splats = project(rows, frame, *half)
        for n in range(9):
            splats_ref[n, 8 * k : 8 * k + 8, :] = splats[n]


def param_tile(params_held, k, g, c):
    at = slice(LANES * c, LANES * (c + 1))
    if g < 7:
        return params_held[k, 8 * g : 8 * g + 8, at]
    return jnp.concatenate([params_held[k, 56:59, at], jnp.zeros((5, LANES), jnp.float32)], axis=0)


def list_order(lists_ref, turn_ref, order_ref):
    turn_ref[...] = jnp.transpose(jnp.concatenate([lists_ref[...]] * 4, axis=0))
    block = lax.broadcasted_iota(jnp.int32, (32, LANES), 1) >> 5
    made = None
    for part in range(4):
        value = turn_ref[pl.ds(part, 32, stride=4), :]
        made = value if made is None else jnp.where(block == part, value, made)
    order_ref[...] = made


def goal_order(targets_ref, goals_ref):
    for c in range(3):
        left, right = targets_ref[c, :, 0:128], targets_ref[c, :, 128:256]
        stacked = jnp.concatenate(
            [left, pltpu.roll(left, 64, 1), right, pltpu.roll(right, 64, 1)], axis=0
        )
        goals_ref[c] = jnp.transpose(stacked)[0:64, :]


def inverse_of(ids_ref, blocks):
    lane = lax.broadcasted_iota(jnp.int32, (blocks, LANES), 1)
    row_id = lax.broadcasted_iota(jnp.int32, (blocks, LANES), 0)
    low_id = lax.broadcasted_iota(jnp.int32, (LANES, LANES), 0)
    lane_digit = (lane + 1).astype(jnp.float32)

    def body(j, total):
        ids = ids_ref[pl.ds(j, 1), :]
        hit = row_id == (ids >> 7)
        digit = jnp.full((blocks, LANES), j, jnp.int32).astype(jnp.float32)
        left = jnp.concatenate(
            [jnp.where(hit, lane_digit, 0.0), jnp.where(hit, digit, 0.0)], axis=0
        ).astype(jnp.bfloat16)
        right = jnp.where(low_id == (ids & 127), 1.0, 0.0).astype(jnp.bfloat16)
        return total + lax.dot_general(
            left, right, (((1,), (1,)), ((), ())), preferred_element_type=jnp.float32
        )

    total = lax.fori_loop(0, ids_ref.shape[0], body, jnp.zeros((2 * blocks, LANES), jnp.float32), unroll=4)
    return (total[blocks:] * 128.0 + total[:blocks]).astype(jnp.int32) - 1


def entry_rows(picked_ref, rows_ref):
    block = lane_block()
    scale = {2: -0.5 * LOG2E, 3: -LOG2E, 4: -0.5 * LOG2E}
    for row in range(9):
        for g in range(4):
            value = picked_ref[row, 8 * g : 8 * g + 8, :]
            if row in scale:
                value = value * scale[row]
            moved = [value] + [pltpu.roll(value, 32 * k, 1) for k in range(1, 4)]
            for part in range(4):
                made = moved[(0 - part) % 4]
                for b in range(1, 4):
                    made = jnp.where(block == b, moved[(b - part) % 4], made)
                rows_ref[4 * row + part, 8 * g : 8 * g + 8, :] = made


def pixel_places(tiles_ref):
    lane = lax.broadcasted_iota(jnp.int32, (8, LANES), 1)
    sub = lax.broadcasted_iota(jnp.int32, (8, LANES), 0)
    tiles = jnp.broadcast_to(jnp.concatenate([tiles_ref[...]] * 4, axis=1), (8, LANES))
    column = (tiles & (TILES_X - 1)) * 16 + sub
    row = (tiles >> 7) * 16 + (lane >> 5) * 4
    across = [column.astype(jnp.float32) + (0.5 + 8 * p) for p in range(2)]
    down = [row.astype(jnp.float32) + (0.5 + q) for q in range(4)]
    return across, down


def splat_at(rows_ref, j, part):
    return [
        jnp.broadcast_to(rows_ref[4 * row + part, pl.ds(j, 1), :], (8, LANES)) for row in range(9)
    ]


def composite(rows_ref, across, down, keep):
    def body(j, carry):
        clear, light = list(carry[:8]), [list(carry[8 + 8 * c : 16 + 8 * c]) for c in range(3)]
        for part in range(4):
            u, w, a, b, c2, o, *colour = splat_at(rows_ref, j, part)
            dx = [u - x for x in across]
            dy = [w - y for y in down]
            ax = [a * d for d in dx]
            by = [b * d for d in dy]
            cy = [c2 * d * d for d in dy]
            for v in range(8):
                q, p = v // 2, v % 2
                alpha = o * jnp.exp2((ax[p] + by[q]) * dx[p] + cy[q])
                weight = clear[v] * alpha
                if keep is not None:
                    keep[0][j, part * 8 + v] = alpha
                    keep[1][j, part * 8 + v] = weight
                clear[v] = clear[v] - weight
                for c in range(3):
                    light[c][v] = light[c][v] + colour[c] * weight
        return (*clear, *light[0], *light[1], *light[2])

    start = tuple([jnp.ones((8, LANES), jnp.float32)] * 8 + [jnp.zeros((8, LANES), jnp.float32)] * 24)
    done = lax.fori_loop(0, LIST_LEN // 4, body, start)
    return [done[8 + 8 * c : 16 + 8 * c] for c in range(3)]


def train_kernel(
    camera_ref, params_ref, send_ref, lists_ref, tiles_ref, targets_ref, returned_ref, from_send_ref,
    params_held, splats_ref, buffer_ref, picked_ref, rows_ref, alpha_ref, weight_ref, sums_ref,
    miss_ref, message_ref, landing_ref, turn_ref, order_ref, from_list_ref, goals_ref,
    loaded, sent, landed, sent_back, landed_back, *, half,
):
    project_all(0, camera_ref, params_ref, params_held, splats_ref, loaded, half)
    def before_landing():
        list_order(lists_ref, turn_ref, order_ref)
        goal_order(targets_ref, goals_ref)
        from_list_ref[...] = inverse_of(order_ref, 32)

    deliver(
        splats_ref, send_ref, message_ref.at[0], landing_ref, sent, landed, greeted, before_landing
    )
    unpack(landing_ref, buffer_ref)
    pick(buffer_ref, order_ref, picked_ref)
    entry_rows(picked_ref, rows_ref)
    across, down = pixel_places(tiles_ref)
    light = composite(rows_ref, across, down, (alpha_ref, weight_ref))
    for c in range(3):
        for v in range(8):
            miss_ref[8 * c + v] = light[c][v] - goals_ref[c, 8 * v : 8 * v + 8, :]

    def body(step, behind):
        j = LIST_LEN // 4 - 1 - step
        behind = list(behind)
        for part in (3, 2, 1, 0):
            u, w, _, _, _, _, *colour = splat_at(rows_ref, j, part)
            dx = [u - x for x in across]
            dy = [w - y for y in down]
            pull = []
            tint = [None] * 3
            for v in range(8):
                alpha = alpha_ref[j, part * 8 + v]
                weight = weight_ref[j, part * 8 + v]
                miss = [miss_ref[8 * c + v] for c in range(3)]
                ahead = colour[0] * miss[0] + colour[1] * miss[1] + colour[2] * miss[2] - behind[v]
                pull.append(weight * ahead)
                behind[v] = behind[v] + alpha * ahead
                for c in range(3):
                    term = weight * miss[c]
                    tint[c] = term if tint[c] is None else tint[c] + term
            row_pull = [pull[2 * q] + pull[2 * q + 1] for q in range(4)]
            row_down = [row_pull[q] * dy[q] for q in range(4)]
            col_pull = [pull[p] + pull[2 + p] + pull[4 + p] + pull[6 + p] for p in range(2)]
            col_down = [
                pull[p] * dy[0] + pull[2 + p] * dy[1] + pull[4 + p] * dy[2] + pull[6 + p] * dy[3]
                for p in range(2)
            ]
            col_across = [col_pull[p] * dx[p] for p in range(2)]
            sums = [
                col_across[0] + col_across[1],
                row_down[0] + row_down[1] + row_down[2] + row_down[3],
                col_across[0] * dx[0] + col_across[1] * dx[1],
                col_down[0] * dx[0] + col_down[1] * dx[1],
                row_down[0] * dy[0] + row_down[1] * dy[1] + row_down[2] * dy[2] + row_down[3] * dy[3],
                col_pull[0] + col_pull[1],
                *tint,
            ]
            for n in range(9):
                sums_ref[4 * n + part, pl.ds(j, 1), :] = jnp.sum(sums[n], axis=0, keepdims=True)
        return tuple(behind)

    lax.fori_loop(0, LIST_LEN // 4, body, tuple([jnp.zeros((8, LANES), jnp.float32)] * 8))

    block = lane_block()
    for g in range(4):
        moment = []
        for n in range(9):
            made = None
            for part in range(4):
                value = sums_ref[4 * n + part, 8 * g : 8 * g + 8, :]
                value = value + pltpu.roll(value, 64, 1)
                value = value + pltpu.roll(value, 32, 1)
                made = value if made is None else jnp.where(block == part, value, made)
            moment.append(made)
        a, b, c2 = [picked_ref[n, 8 * g : 8 * g + 8, :] for n in (2, 3, 4)]
        grads = [
            -(a * moment[0] + b * moment[1]),
            -(c2 * moment[1] + b * moment[0]),
            -0.5 * moment[2],
            -moment[3],
            -0.5 * moment[4],
            *moment[5:],
        ]
        for n in range(9):
            buffer_ref[n, 8 * g : 8 * g + 8, :] = grads[n]

    def before_return():
        from_send_ref[...] = inverse_of(send_ref, from_send_ref.shape[0])

    deliver(
        buffer_ref, from_list_ref, message_ref.at[1], returned_ref, sent_back, landed_back,
        None, before_return,
    )


def update_kernel(
    camera_ref, rates_ref, back_ref, inverse_ref, params_ref, first_ref, second_ref,
    new_params_ref, new_first_ref, new_second_ref,
    buffer_ref, frame_ref, *, half,
):
    step = pl.program_id(0)

    @pl.when(step == 0)
    def _():
        unpack(back_ref, buffer_ref)
        for n, entry in enumerate(camera_frame(camera_ref, 0)):
            frame_ref[n] = entry

    for h in range(params_ref.shape[1] // CHUNK):
        left_edge = CHUNK * h
        slot_grads = pick_eight(buffer_ref, inverse_ref[8 * h : 8 * h + 8, :])
        rows = []
        for g in range(8):
            rows += turned([params_ref[8 * g : 8 * g + 8, left_edge + LANES * c : left_edge + LANES * (c + 1)] for c in range(8)])
        frame = [frame_ref[n] for n in range(15)]
        used = rows[:10] + [None] + rows[11:59]

        def view_first(*leaves):
            return footprint(list(leaves[:10]) + [None] + list(leaves[10:]), frame, *half)

        made, pullback = jax.vjp(view_first, *(used[:10] + used[11:]))
        ka, kb, kc = conic_of(*made[2:5])
        ga, gb, gc = slot_grads[2], 0.5 * slot_grads[3], slot_grads[4]
        left = [[ka * ga + kb * gb, ka * gb + kb * gc], [kb * ga + kc * gb, kb * gb + kc * gc]]
        cover_grads = (
            -(left[0][0] * ka + left[0][1] * kb),
            -2.0 * (left[0][0] * kb + left[0][1] * kc),
            -(left[1][0] * kb + left[1][1] * kc),
        )
        grads = list(pullback((slot_grads[0], slot_grads[1], *cover_grads, *slot_grads[6:])))
        opacity_grad = slot_grads[5] * (1.0 - jax.nn.sigmoid(rows[10]))
        grads = grads[:10] + [opacity_grad] + grads[10:] + [jnp.zeros((8, LANES), jnp.float32)] * 5
        for g in range(8):
            columns = turned(grads[8 * g : 8 * g + 8])
            rate = rates_ref[8 * g : 8 * g + 8, :]
            for c in range(8):
                at = (slice(8 * g, 8 * g + 8), slice(left_edge + LANES * c, left_edge + LANES * (c + 1)))
                gradient = columns[c]
                first = 0.9 * first_ref[at] + 0.1 * gradient
                second = 0.999 * second_ref[at] + 0.001 * gradient * gradient
                value = params_ref[at] - rate * (first * (1.0 / bias_first)) / (
                    jnp.sqrt(second * (1.0 / bias_second)) + adam_epsilon
                )
                new_first_ref[at] = first
                new_second_ref[at] = second
                new_params_ref[at] = value


def render_kernel(
    camera_ref, params_ref, send_ref, lists_ref, tiles_ref, image_ref,
    params_held, splats_ref, buffer_ref, picked_ref, rows_ref, message_ref, landing_ref,
    turn_ref, order_ref, loaded, sent, landed, *, half,
):
    project_all(1, camera_ref, params_ref, params_held, splats_ref, loaded, half)
    deliver(
        splats_ref, send_ref, message_ref, landing_ref, sent, landed, greeted,
        lambda: list_order(lists_ref, turn_ref, order_ref),
    )
    unpack(landing_ref, buffer_ref)
    pick(buffer_ref, order_ref, picked_ref)
    entry_rows(picked_ref, rows_ref)
    across, down = pixel_places(tiles_ref)
    light = composite(rows_ref, across, down, None)
    for c in range(3):
        flat = jnp.concatenate(list(light[c]), axis=0)
        upright = jnp.transpose(jnp.concatenate([flat, flat], axis=0))
        pieces = [upright[32 * b : 32 * b + 32, :] for b in range(4)]
        low = lax.broadcasted_iota(jnp.int32, (32, LANES), 1) < 64
        image_ref[c, :, 0:128] = jnp.where(low, pieces[0], pieces[1])
        image_ref[c, :, 128:256] = jnp.where(low, pieces[2], pieces[3])


def vmem(shape):
    return pltpu.VMEM(shape, jnp.float32)


def whole():
    return pl.BlockSpec(memory_space=pltpu.VMEM)


def scalars():
    return pl.BlockSpec(memory_space=pltpu.SMEM)


def f32(*shape):
    return jax.ShapeDtypeStruct(shape, jnp.float32)


def shards(
    gauss_params, adam_first, adam_second, camera, send_first, send_second,
    lists_first, lists_second, tiles_first, tiles_second, targets,
):
    local = gauss_params.shape[1]
    steps, blocks = local // CHUNK, local // LANES
    devices = lax.axis_size("dev")
    half = (TILES_X * 8.0, lists_first.shape[0] * devices // TILES_X * 8.0)
    megabyte = 1024 * 1024
    streamed = pltpu.CompilerParams(vmem_limit_bytes=62 * megabyte)

    def linked(number):
        return pltpu.CompilerParams(
            vmem_limit_bytes=(60 if number == 1 else 52) * megabyte,
            collective_id=number,
            has_side_effects=True,
        )

    slots_first, slots_second = send_first.reshape(32, LANES), send_second.reshape(32, LANES)
    packet = (devices, 3, LANES)
    links = [pltpu.SemaphoreType.DMA((2,)), pltpu.SemaphoreType.DMA((1,))]
    loading = pltpu.SemaphoreType.DMA((steps,))
    held = [vmem((steps, 59, CHUNK)), vmem((9, blocks, LANES)), vmem((9, 32, LANES)), vmem((9, 32, LANES))]
    outside = pl.BlockSpec(memory_space=pltpu.HBM)

    def integers(*shape):
        return pltpu.VMEM(shape, jnp.int32)

    returned, from_send = pl.pallas_call(
        functools.partial(train_kernel, half=half),
        out_shape=(f32(*packet), jax.ShapeDtypeStruct((blocks, LANES), jnp.int32)),
        in_specs=[scalars(), outside, whole(), whole(), whole(), whole()],
        out_specs=(whole(), whole()),
        scratch_shapes=[
            *held, vmem((36, 32, LANES)), vmem((32, 32, 8, LANES)), vmem((32, 32, 8, LANES)),
            vmem((36, 32, LANES)), vmem((24, 8, LANES)), vmem((2, *packet)), vmem(packet),
            integers(LANES, LANES), integers(32, LANES), integers(32, LANES), vmem((3, 64, LANES)),
            loading, *links, *links,
        ],
        compiler_params=linked(1),
        name="train",
    )(camera, gauss_params, slots_first, lists_first, tiles_first[None], jnp.transpose(targets, (1, 0, 2)))
    wide = 2
    block = pl.BlockSpec((64, wide * CHUNK), lambda i: (0, i))
    new_params, new_first, new_second = pl.pallas_call(
        functools.partial(update_kernel, half=half),
        grid=(steps // wide,),
        out_shape=(f32(59, local), f32(59, local), f32(59, local)),
        in_specs=[
            scalars(),
            pl.BlockSpec((64, LANES), lambda i: (0, 0)),
            pl.BlockSpec(packet, lambda i: (0, 0, 0)),
            pl.BlockSpec((8 * wide, LANES), lambda i: (i, 0)),
            block, block, block,
        ],
        out_specs=(block, block, block),
        scratch_shapes=[vmem((9, 32, LANES)), vmem((15, 8, LANES))],
        compiler_params=streamed,
        name="update",
    )(camera, jnp.asarray(rate_values()), returned, from_send, gauss_params, adam_first, adam_second)
    image = pl.pallas_call(
        functools.partial(render_kernel, half=half),
        out_shape=f32(3, TILE_DEV, 256),
        in_specs=[scalars(), outside, whole(), whole(), whole()],
        out_specs=whole(),
        scratch_shapes=[
            *held, vmem((36, 32, LANES)), vmem(packet), vmem(packet),
            integers(LANES, LANES), integers(32, LANES), loading, *links,
        ],
        compiler_params=linked(2),
        name="render",
    )(camera, new_params, slots_second, lists_second, tiles_second[None])
    return (new_params, new_first, new_second, jnp.transpose(image, (1, 0, 2)))


def solution(mesh):
    split = P(None, "dev")
    rows = P("dev", None)
    return jax.shard_map(
        shards,
        mesh=mesh,
        in_specs=(split, split, split, P(), rows, rows, rows, rows, P("dev"), P("dev"), P("dev", None, None)),
        out_specs=(split, split, split, P("dev", None, None)),
        check_vma=False,
    )
```

```python
import functools

import jax
import jax.numpy as jnp
import numpy as np
from jax import lax
from jax.experimental import pallas as pl
from jax.experimental.pallas import tpu as pltpu
from jax.sharding import PartitionSpec as P

LANES = 128
TILES_X = 128
TILE_DEV = 32
LIST_LEN = 128
CHUNK = 1024
LOG2E = 1.4426950408889634

focal_length = 1000.0
blur_floor = 0.3
adam_epsilon = 1e-08
bias_first = 1.0 - 0.9**20
bias_second = 1.0 - 0.999**20
sh_first = 0.28209479177387814
sh_second = 0.4886025119029199
sh_third = (
    1.0925484305920792,
    -1.0925484305920792,
    0.31539156525252005,
    -1.0925484305920792,
    0.5462742152960396,
)
sh_fourth = (
    -0.5900435899266435,
    2.890611442640554,
    -0.4570457994644658,
    0.3731763325901154,
    -0.4570457994644658,
    1.445305721320277,
    -0.5900435899266435,
)


def rate_values():
    values = np.full((64,), 0.000125)
    values[0:3] = 0.00016
    values[3:6] = 0.005
    values[6:10] = 0.001
    values[10] = 0.05
    values[11] = 0.0025
    values[27] = 0.0025
    values[43] = 0.0025
    return np.broadcast_to(values[:, None], (64, LANES)).astype(np.float32)


def small_turn(angle):
    square = angle * angle
    cosine = 1.0 + square * (
        -1 / 2 + square * (1 / 24 + square * (-1 / 720 + square * (1 / 40320 - square / 3628800)))
    )
    sine = angle * (
        1.0 + square * (-1 / 6 + square * (1 / 120 + square * (-1 / 5040 + square / 362880)))
    )
    return cosine, sine


def camera_frame(camera_ref, view):
    def full(k):
        return jnp.full((8, LANES), camera_ref[view, k], jnp.float32)

    (ca, sa), (cb, sb), (cc, sc) = [small_turn(full(k)) for k in range(3)]
    rot = [
        [cc * cb, cc * (sb * sa) - sc * ca, cc * (sb * ca) + sc * sa],
        [sc * cb, sc * (sb * sa) + cc * ca, sc * (sb * ca) - cc * sa],
        [-sb, cb * sa, cb * ca],
    ]
    shift = [full(3), full(4), full(5)]
    back = [rot[0][k] * shift[0] + rot[1][k] * shift[1] + rot[2][k] * shift[2] for k in range(3)]
    return [rot[0][0], rot[0][1], rot[0][2], rot[1][0], rot[1][1], rot[1][2],
            rot[2][0], rot[2][1], rot[2][2]] + shift + back


def sh_terms(along_x, along_y, along_z):
    square_x, square_y, square_z = (along_x * along_x, along_y * along_y, along_z * along_z)
    return [
        -sh_second * along_y,
        sh_second * along_z,
        -sh_second * along_x,
        sh_third[0] * along_x * along_y,
        sh_third[1] * along_y * along_z,
        sh_third[2] * (2.0 * square_z - square_x - square_y),
        sh_third[3] * along_x * along_z,
        sh_third[4] * (square_x - square_y),
        sh_fourth[0] * along_y * (3.0 * square_x - square_y),
        sh_fourth[1] * along_x * along_y * along_z,
        sh_fourth[2] * along_y * (4.0 * square_z - square_x - square_y),
        sh_fourth[3] * along_z * (2.0 * square_z - 3.0 * square_x - 3.0 * square_y),
        sh_fourth[4] * along_x * (4.0 * square_z - square_x - square_y),
        sh_fourth[5] * along_z * (square_x - square_y),
        sh_fourth[6] * along_x * (square_x - 3.0 * square_y),
    ]


def footprint(params, frame, half_width, half_height):
    rot = [frame[0:3], frame[3:6], frame[6:9]]
    shift, back = frame[9:12], frame[12:15]
    x, y, z = params[0], params[1], params[2]
    viewed = [rot[k][0] * x + rot[k][1] * y + rot[k][2] * z + shift[k] for k in range(3)]
    inverse_depth = 1.0 / viewed[2]
    screen_u = focal_length * viewed[0] * inverse_depth + half_width
    screen_v = focal_length * viewed[1] * inverse_depth + half_height
    scales = [jnp.exp(params[3 + k]) for k in range(3)]
    size = params[6] * params[6] + params[7] * params[7] + params[8] * params[8] + params[9] * params[9]
    unit = 1.0 / jnp.sqrt(size)
    w, i, j, k = [params[6 + n] * unit for n in range(4)]
    turn = [
        [1.0 - 2.0 * (j * j + k * k), 2.0 * (i * j - w * k), 2.0 * (i * k + w * j)],
        [2.0 * (i * j + w * k), 1.0 - 2.0 * (i * i + k * k), 2.0 * (j * k - w * i)],
        [2.0 * (i * k - w * j), 2.0 * (j * k + w * i), 1.0 - 2.0 * (i * i + j * j)],
    ]
    near = focal_length * inverse_depth
    slant_x = -near * viewed[0] * inverse_depth
    slant_y = -near * viewed[1] * inverse_depth
    mapping = [
        [near * rot[0][n] + slant_x * rot[2][n] for n in range(3)],
        [near * rot[1][n] + slant_y * rot[2][n] for n in range(3)],
    ]
    half = [
        [
            (mapping[m][0] * turn[0][n] + mapping[m][1] * turn[1][n] + mapping[m][2] * turn[2][n])
            * scales[n]
            for n in range(3)
        ]
        for m in range(2)
    ]

    def inner(p, q):
        return p[0] * q[0] + p[1] * q[1] + p[2] * q[2]

    cover_a = inner(half[0], half[0]) + blur_floor
    cover_b = inner(half[0], half[1])
    cover_c = inner(half[1], half[1]) + blur_floor
    towards = [x + back[0], y + back[1], z + back[2]]
    inverse_length = 1.0 / jnp.sqrt(inner(towards, towards))
    harmonics = sh_terms(*[t * inverse_length for t in towards])
    colours = []
    for channel in range(3):
        running = 0.5 + sh_first * params[11 + 16 * channel]
        for term in range(1, 16):
            running = running + harmonics[term - 1] * params[11 + 16 * channel + term]
        colours.append(jnp.maximum(running, 0.0))
    return (screen_u, screen_v, cover_a, cover_b, cover_c, *colours)


def conic_of(cover_a, cover_b, cover_c):
    inverse = 1.0 / (cover_a * cover_c - cover_b * cover_b)
    return cover_c * inverse, -cover_b * inverse, cover_a * inverse


def project(params, frame, half_width, half_height):
    u, w, cover_a, cover_b, cover_c, *colours = footprint(params, frame, half_width, half_height)
    return [u, w, *conic_of(cover_a, cover_b, cover_c), jax.nn.sigmoid(params[10]), *colours]


def turned(tiles):
    swapped = jnp.swapaxes(jnp.stack(tiles, axis=0), 0, 1)
    return [swapped[n] for n in range(8)]


def lane_pick(values, lanes):
    numbers = lax.GatherDimensionNumbers(
        offset_dims=(),
        collapsed_slice_dims=(1,),
        start_index_map=(1,),
        operand_batching_dims=(0,),
        start_indices_batching_dims=(0,),
    )
    return lax.gather(
        values, lanes[:, :, None], numbers, (1, 1), mode=lax.GatherScatterMode.PROMISE_IN_BOUNDS
    )


def pick_eight(source_ref, wanted):
    count, blocks = source_ref.shape[:2]
    high, low = wanted >> 7, wanted & 127
    held = [jnp.zeros((8, LANES), jnp.float32)] * count
    for block in range(blocks):
        hit = high == block
        for row in range(count):
            source = jnp.broadcast_to(source_ref[row, block : block + 1, :], (8, LANES))
            held[row] = jnp.where(hit, lane_pick(source, low), held[row])
    return held


def split_rows(source_ref, parts_ref):
    half = source_ref.shape[1] // 2
    for row in range(4):
        rest = jnp.concatenate([source_ref[5 + row, :half], source_ref[5 + row, half:]], axis=1)
        for part in range(3):
            rounded = rest.astype(jnp.bfloat16)
            start = (part * 4 + row) * half
            parts_ref[start : start + half, :] = rounded
            rest = rest - rounded.astype(jnp.float32)


def pick_eight_split(source_ref, parts_ref, wanted):
    blocks = source_ref.shape[1]
    half = blocks // 2
    high, low = wanted >> 7, wanted & 127
    column = ((wanted >> (7 + half.bit_length() - 1)) << 7) | low
    line = high & (half - 1)
    line_id = lax.broadcasted_iota(jnp.int32, (half, 2 * LANES), 0)
    column_id = lax.broadcasted_iota(jnp.int32, (2 * LANES, 2 * LANES), 0)
    found = [[] for _ in range(4)]
    for pair in range(4):

        def joined(values):
            return jnp.concatenate(
                [values[2 * pair : 2 * pair + 1], values[2 * pair + 1 : 2 * pair + 2]], axis=1
            )

        choose = jnp.where(column_id == joined(column), 1.0, 0.0).astype(jnp.bfloat16)
        hit = line_id == joined(line)
        part = jnp.dot(parts_ref[...], choose, preferred_element_type=jnp.float32)
        size = 4 * half
        value = part[:size] + part[size : 2 * size] + part[2 * size :]
        for row in range(4):
            one = jnp.where(hit, value[row * half : (row + 1) * half], 0.0)
            one = jnp.sum(one, axis=0, keepdims=True)
            found[row] += [one[:, :LANES], one[:, LANES:]]
    held = [jnp.zeros((8, LANES), jnp.float32)] * 5
    for block in range(blocks):
        here = high == block
        for row in range(5):
            source = jnp.broadcast_to(source_ref[row, block : block + 1, :], (8, LANES))
            held[row] = jnp.where(here, lane_pick(source, low), held[row])
    return held + [jnp.concatenate(rows, axis=0) for rows in found]


def pick(source_ref, wanted_ref, picked_ref):
    def body(g, _):
        at = pl.ds(pl.multiple_of(g * 8, 8), 8)
        for row, value in enumerate(pick_eight(source_ref, wanted_ref[at, :])):
            picked_ref[row, at, :] = value
        return 0

    lax.fori_loop(0, wanted_ref.shape[0] // 8, body, 0)


def lane_block():
    return lax.broadcasted_iota(jnp.int32, (8, LANES), 1) >> 5


def block_turn(vectors):
    block = lane_block()
    out = []
    for j in range(4):
        made = None
        for i in range(4):
            shift = ((i - j) * 32) % LANES
            moved = pltpu.roll(vectors[i], shift, 1) if shift else vectors[i]
            made = moved if made is None else jnp.where(block == i, moved, made)
        out.append(made)
    return out


def device_rows(g, d):
    return pl.ds(32 * g + d, 8, stride=4)


def pack_group(values, message_ref, g):
    nothing = jnp.zeros((8, LANES), jnp.float32)
    for a in range(3):
        rows = [values[4 * a + b] if 4 * a + b < 9 else nothing for b in range(4)]
        for d, made in enumerate(block_turn(rows)):
            message_ref[device_rows(g, d), a, :] = made


def unpack(message_ref, buffer_ref):
    for g in range(4):
        for a in range(3):
            rows = [message_ref[device_rows(g, d), a, :] for d in range(4)]
            for b, made in enumerate(block_turn(rows)):
                if 4 * a + b < 9:
                    buffer_ref[4 * a + b, 8 * g : 8 * g + 8, :] = made


def greet():
    me, devices = lax.axis_index("dev"), lax.axis_size("dev")
    barrier = pltpu.get_barrier_semaphore()

    def body(j, _):
        pl.semaphore_signal(
            barrier, inc=1, device_id=(lax.rem(me + j, devices),), device_id_type=pl.DeviceIdType.MESH
        )
        return 0

    lax.fori_loop(1, devices, body, 0)


def greeted():
    pl.semaphore_wait(pltpu.get_barrier_semaphore(), lax.axis_size("dev") - 1)


def deliver(
    source_ref, parts_ref, wanted_ref, message_ref, landing_ref, sent, landed, ready, meanwhile
):
    me, devices = lax.axis_index("dev"), lax.axis_size("dev")
    share = devices // 4
    home, place = lax.div(me, share), lax.rem(me, share)

    def remote(source, target, device):
        return pltpu.make_async_remote_copy(
            src_ref=source,
            dst_ref=target,
            send_sem=sent.at[0],
            recv_sem=landed.at[0],
            device_id=(device,),
            device_id_type=pl.DeviceIdType.MESH,
        )

    if parts_ref is not None:
        split_rows(source_ref, parts_ref)
    for ahead in (2, 1, 3, 0):
        g = lax.rem(home + ahead, 4)
        at = pl.ds(pl.multiple_of(g * 8, 8), 8)
        if parts_ref is None:
            values = pick_eight(source_ref, wanted_ref[at, :])
        else:
            values = pick_eight_split(source_ref, parts_ref, wanted_ref[at, :])
        pack_group(values, message_ref, g)
        if ahead == 2 and ready is not None:
            ready()

        def body(i, _):
            other = g * share + lax.rem(place + i, share)
            remote(message_ref.at[other], landing_ref.at[me], other).start()
            return 0

        if ahead:
            lax.fori_loop(share // 2, share + share // 2, body, 0)
        else:
            lax.fori_loop(1, share, body, 0)
    own = pltpu.make_async_copy(message_ref.at[me], landing_ref.at[me], sent.at[1])
    own.start()
    meanwhile()
    own.wait()
    several = pl.ds(0, devices - 1)
    remote(message_ref.at[several], landing_ref.at[several], lax.rem(me + 1, devices)).wait()


def project_all(view, camera_ref, params_ref, params_held, splats_ref, loaded, half):
    chunks = params_ref.shape[1] // CHUNK
    loads = [
        pltpu.make_async_copy(
            params_ref.at[:, CHUNK * k : CHUNK * (k + 1)], params_held.at[k], loaded.at[k]
        )
        for k in range(chunks)
    ]
    for load in loads:
        load.start()
    greet()
    frame = camera_frame(camera_ref, view)
    for k in range(chunks):
        loads[k].wait()
        rows = []
        for g in range(8):
            rows += turned([param_tile(params_held, k, g, c) for c in range(8)])
        splats = project(rows, frame, *half)
        for n in range(9):
            splats_ref[n, 8 * k : 8 * k + 8, :] = splats[n]


def param_tile(params_held, k, g, c):
    at = slice(LANES * c, LANES * (c + 1))
    if g < 7:
        return params_held[k, 8 * g : 8 * g + 8, at]
    return jnp.concatenate([params_held[k, 56:59, at], jnp.zeros((5, LANES), jnp.float32)], axis=0)


def list_order(lists_ref, turn_ref, order_ref):
    turn_ref[...] = jnp.transpose(jnp.concatenate([lists_ref[...]] * 4, axis=0))
    block = lax.broadcasted_iota(jnp.int32, (32, LANES), 1) >> 5
    made = None
    for part in range(4):
        value = turn_ref[pl.ds(part, 32, stride=4), :]
        made = value if made is None else jnp.where(block == part, value, made)
    order_ref[...] = made


def goal_order(targets_ref, goals_ref):
    for c in range(3):
        left, right = targets_ref[c, :, 0:128], targets_ref[c, :, 128:256]
        stacked = jnp.concatenate(
            [left, pltpu.roll(left, 64, 1), right, pltpu.roll(right, 64, 1)], axis=0
        )
        goals_ref[c] = jnp.transpose(stacked)[0:64, :]


def inverse_of(ids_ref, blocks):
    lane = lax.broadcasted_iota(jnp.int32, (blocks, LANES), 1)
    row_id = lax.broadcasted_iota(jnp.int32, (blocks, LANES), 0)
    low_id = lax.broadcasted_iota(jnp.int32, (LANES, LANES), 0)
    lane_digit = (lane + 1).astype(jnp.float32)

    def body(j, total):
        ids = ids_ref[pl.ds(j, 1), :]
        hit = row_id == (ids >> 7)
        digit = jnp.full((blocks, LANES), j, jnp.int32).astype(jnp.float32)
        left = jnp.concatenate(
            [jnp.where(hit, lane_digit, 0.0), jnp.where(hit, digit, 0.0)], axis=0
        ).astype(jnp.bfloat16)
        right = jnp.where(low_id == (ids & 127), 1.0, 0.0).astype(jnp.bfloat16)
        return total + lax.dot_general(
            left, right, (((1,), (1,)), ((), ())), preferred_element_type=jnp.float32
        )

    total = lax.fori_loop(0, ids_ref.shape[0], body, jnp.zeros((2 * blocks, LANES), jnp.float32), unroll=4)
    return (total[blocks:] * 128.0 + total[:blocks]).astype(jnp.int32) - 1


def entry_rows(picked_ref, rows_ref):
    block = lane_block()
    scale = {2: -0.5 * LOG2E, 3: -LOG2E, 4: -0.5 * LOG2E}
    for row in range(9):
        for g in range(4):
            value = picked_ref[row, 8 * g : 8 * g + 8, :]
            if row in scale:
                value = value * scale[row]
            moved = [value] + [pltpu.roll(value, 32 * k, 1) for k in range(1, 4)]
            for part in range(4):
                made = moved[(0 - part) % 4]
                for b in range(1, 4):
                    made = jnp.where(block == b, moved[(b - part) % 4], made)
                rows_ref[4 * row + part, 8 * g : 8 * g + 8, :] = made


def pixel_places(tiles_ref):
    lane = lax.broadcasted_iota(jnp.int32, (8, LANES), 1)
    sub = lax.broadcasted_iota(jnp.int32, (8, LANES), 0)
    tiles = jnp.broadcast_to(jnp.concatenate([tiles_ref[...]] * 4, axis=1), (8, LANES))
    column = (tiles & (TILES_X - 1)) * 16 + sub
    row = (tiles >> 7) * 16 + (lane >> 5) * 4
    across = [column.astype(jnp.float32) + (0.5 + 8 * p) for p in range(2)]
    down = [row.astype(jnp.float32) + (0.5 + q) for q in range(4)]
    return across, down


def splat_at(rows_ref, j, part):
    return [
        jnp.broadcast_to(rows_ref[4 * row + part, pl.ds(j, 1), :], (8, LANES)) for row in range(9)
    ]


def composite(rows_ref, across, down, keep):
    def body(j, carry):
        clear, light = list(carry[:8]), [list(carry[8 + 8 * c : 16 + 8 * c]) for c in range(3)]
        for part in range(4):
            u, w, a, b, c2, o, *colour = splat_at(rows_ref, j, part)
            dx = [u - x for x in across]
            dy = [w - y for y in down]
            ax = [a * d for d in dx]
            by = [b * d for d in dy]
            cy = [c2 * d * d for d in dy]
            for v in range(8):
                q, p = v // 2, v % 2
                alpha = o * jnp.exp2((ax[p] + by[q]) * dx[p] + cy[q])
                weight = clear[v] * alpha
                if keep is not None:
                    keep[0][j, part * 8 + v] = alpha
                    keep[1][j, part * 8 + v] = weight
                clear[v] = clear[v] - weight
                for c in range(3):
                    light[c][v] = light[c][v] + colour[c] * weight
        return (*clear, *light[0], *light[1], *light[2])

    start = tuple([jnp.ones((8, LANES), jnp.float32)] * 8 + [jnp.zeros((8, LANES), jnp.float32)] * 24)
    done = lax.fori_loop(0, LIST_LEN // 4, body, start)
    return [done[8 + 8 * c : 16 + 8 * c] for c in range(3)]


def train_kernel(
    camera_ref, params_ref, send_ref, lists_ref, tiles_ref, targets_ref, returned_ref, from_send_ref,
    params_held, splats_ref, parts_ref, buffer_ref, picked_ref, rows_ref, alpha_ref, weight_ref, sums_ref,
    miss_ref, message_ref, landing_ref, turn_ref, order_ref, from_list_ref, goals_ref,
    loaded, sent, landed, sent_back, landed_back, *, half,
):
    project_all(0, camera_ref, params_ref, params_held, splats_ref, loaded, half)
    def before_landing():
        list_order(lists_ref, turn_ref, order_ref)
        goal_order(targets_ref, goals_ref)
        from_list_ref[...] = inverse_of(order_ref, 32)

    deliver(
        splats_ref, parts_ref, send_ref, message_ref.at[0], landing_ref, sent, landed,
        greeted, before_landing,
    )
    unpack(landing_ref, buffer_ref)
    pick(buffer_ref, order_ref, picked_ref)
    entry_rows(picked_ref, rows_ref)
    across, down = pixel_places(tiles_ref)
    light = composite(rows_ref, across, down, (alpha_ref, weight_ref))
    for c in range(3):
        for v in range(8):
            miss_ref[8 * c + v] = light[c][v] - goals_ref[c, 8 * v : 8 * v + 8, :]

    def body(step, behind):
        j = LIST_LEN // 4 - 1 - step
        behind = list(behind)
        for part in (3, 2, 1, 0):
            u, w, _, _, _, _, *colour = splat_at(rows_ref, j, part)
            dx = [u - x for x in across]
            dy = [w - y for y in down]
            pull = []
            tint = [None] * 3
            for v in range(8):
                alpha = alpha_ref[j, part * 8 + v]
                weight = weight_ref[j, part * 8 + v]
                miss = [miss_ref[8 * c + v] for c in range(3)]
                ahead = colour[0] * miss[0] + colour[1] * miss[1] + colour[2] * miss[2] - behind[v]
                pull.append(weight * ahead)
                behind[v] = behind[v] + alpha * ahead
                for c in range(3):
                    term = weight * miss[c]
                    tint[c] = term if tint[c] is None else tint[c] + term
            row_pull = [pull[2 * q] + pull[2 * q + 1] for q in range(4)]
            row_down = [row_pull[q] * dy[q] for q in range(4)]
            col_pull = [pull[p] + pull[2 + p] + pull[4 + p] + pull[6 + p] for p in range(2)]
            col_down = [
                pull[p] * dy[0] + pull[2 + p] * dy[1] + pull[4 + p] * dy[2] + pull[6 + p] * dy[3]
                for p in range(2)
            ]
            col_across = [col_pull[p] * dx[p] for p in range(2)]
            sums = [
                col_across[0] + col_across[1],
                row_down[0] + row_down[1] + row_down[2] + row_down[3],
                col_across[0] * dx[0] + col_across[1] * dx[1],
                col_down[0] * dx[0] + col_down[1] * dx[1],
                row_down[0] * dy[0] + row_down[1] * dy[1] + row_down[2] * dy[2] + row_down[3] * dy[3],
                col_pull[0] + col_pull[1],
                *tint,
            ]
            for n in range(9):
                sums_ref[4 * n + part, pl.ds(j, 1), :] = jnp.sum(sums[n], axis=0, keepdims=True)
        return tuple(behind)

    lax.fori_loop(0, LIST_LEN // 4, body, tuple([jnp.zeros((8, LANES), jnp.float32)] * 8))

    block = lane_block()
    for g in range(4):
        moment = []
        for n in range(9):
            made = None
            for part in range(4):
                value = sums_ref[4 * n + part, 8 * g : 8 * g + 8, :]
                value = value + pltpu.roll(value, 64, 1)
                value = value + pltpu.roll(value, 32, 1)
                made = value if made is None else jnp.where(block == part, value, made)
            moment.append(made)
        a, b, c2 = [picked_ref[n, 8 * g : 8 * g + 8, :] for n in (2, 3, 4)]
        grads = [
            -(a * moment[0] + b * moment[1]),
            -(c2 * moment[1] + b * moment[0]),
            -0.5 * moment[2],
            -moment[3],
            -0.5 * moment[4],
            *moment[5:],
        ]
        for n in range(9):
            buffer_ref[n, 8 * g : 8 * g + 8, :] = grads[n]

    def before_return():
        from_send_ref[...] = inverse_of(send_ref, from_send_ref.shape[0])

    deliver(
        buffer_ref, None, from_list_ref, message_ref.at[1], returned_ref, sent_back, landed_back,
        None, before_return,
    )


def update_kernel(
    camera_ref, rates_ref, back_ref, inverse_ref, params_ref, first_ref, second_ref,
    new_params_ref, new_first_ref, new_second_ref,
    buffer_ref, frame_ref, *, half,
):
    step = pl.program_id(0)

    @pl.when(step == 0)
    def _():
        unpack(back_ref, buffer_ref)
        for n, entry in enumerate(camera_frame(camera_ref, 0)):
            frame_ref[n] = entry

    for h in range(params_ref.shape[1] // CHUNK):
        left_edge = CHUNK * h
        slot_grads = pick_eight(buffer_ref, inverse_ref[8 * h : 8 * h + 8, :])
        rows = []
        for g in range(8):
            rows += turned([params_ref[8 * g : 8 * g + 8, left_edge + LANES * c : left_edge + LANES * (c + 1)] for c in range(8)])
        frame = [frame_ref[n] for n in range(15)]
        used = rows[:10] + [None] + rows[11:59]

        def view_first(*leaves):
            return footprint(list(leaves[:10]) + [None] + list(leaves[10:]), frame, *half)

        made, pullback = jax.vjp(view_first, *(used[:10] + used[11:]))
        ka, kb, kc = conic_of(*made[2:5])
        ga, gb, gc = slot_grads[2], 0.5 * slot_grads[3], slot_grads[4]
        left = [[ka * ga + kb * gb, ka * gb + kb * gc], [kb * ga + kc * gb, kb * gb + kc * gc]]
        cover_grads = (
            -(left[0][0] * ka + left[0][1] * kb),
            -2.0 * (left[0][0] * kb + left[0][1] * kc),
            -(left[1][0] * kb + left[1][1] * kc),
        )
        grads = list(pullback((slot_grads[0], slot_grads[1], *cover_grads, *slot_grads[6:])))
        opacity_grad = slot_grads[5] * (1.0 - jax.nn.sigmoid(rows[10]))
        grads = grads[:10] + [opacity_grad] + grads[10:] + [jnp.zeros((8, LANES), jnp.float32)] * 5
        for g in range(8):
            columns = turned(grads[8 * g : 8 * g + 8])
            rate = rates_ref[8 * g : 8 * g + 8, :]
            for c in range(8):
                at = (slice(8 * g, 8 * g + 8), slice(left_edge + LANES * c, left_edge + LANES * (c + 1)))
                gradient = columns[c]
                first = 0.9 * first_ref[at] + 0.1 * gradient
                second = 0.999 * second_ref[at] + 0.001 * gradient * gradient
                value = params_ref[at] - rate * (first * (1.0 / bias_first)) / (
                    jnp.sqrt(second * (1.0 / bias_second)) + adam_epsilon
                )
                new_first_ref[at] = first
                new_second_ref[at] = second
                new_params_ref[at] = value


def render_kernel(
    camera_ref, params_ref, send_ref, lists_ref, tiles_ref, image_ref,
    params_held, splats_ref, parts_ref, buffer_ref, picked_ref, rows_ref, message_ref, landing_ref,
    turn_ref, order_ref, loaded, sent, landed, *, half,
):
    project_all(1, camera_ref, params_ref, params_held, splats_ref, loaded, half)
    deliver(
        splats_ref, parts_ref, send_ref, message_ref, landing_ref, sent, landed, greeted,
        lambda: list_order(lists_ref, turn_ref, order_ref),
    )
    unpack(landing_ref, buffer_ref)
    pick(buffer_ref, order_ref, picked_ref)
    entry_rows(picked_ref, rows_ref)
    across, down = pixel_places(tiles_ref)
    light = composite(rows_ref, across, down, None)
    for c in range(3):
        flat = jnp.concatenate(list(light[c]), axis=0)
        upright = jnp.transpose(jnp.concatenate([flat, flat], axis=0))
        pieces = [upright[32 * b : 32 * b + 32, :] for b in range(4)]
        low = lax.broadcasted_iota(jnp.int32, (32, LANES), 1) < 64
        image_ref[c, :, 0:128] = jnp.where(low, pieces[0], pieces[1])
        image_ref[c, :, 128:256] = jnp.where(low, pieces[2], pieces[3])


def vmem(shape):
    return pltpu.VMEM(shape, jnp.float32)


def whole():
    return pl.BlockSpec(memory_space=pltpu.VMEM)


def scalars():
    return pl.BlockSpec(memory_space=pltpu.SMEM)


def f32(*shape):
    return jax.ShapeDtypeStruct(shape, jnp.float32)


def shards(
    gauss_params, adam_first, adam_second, camera, send_first, send_second,
    lists_first, lists_second, tiles_first, tiles_second, targets,
):
    local = gauss_params.shape[1]
    steps, blocks = local // CHUNK, local // LANES
    devices = lax.axis_size("dev")
    half = (TILES_X * 8.0, lists_first.shape[0] * devices // TILES_X * 8.0)
    megabyte = 1024 * 1024
    streamed = pltpu.CompilerParams(vmem_limit_bytes=62 * megabyte)

    def linked(number):
        return pltpu.CompilerParams(
            vmem_limit_bytes=(60 if number == 1 else 52) * megabyte,
            collective_id=number,
            has_side_effects=True,
        )

    slots_first, slots_second = send_first.reshape(32, LANES), send_second.reshape(32, LANES)
    packet = (devices, 3, LANES)
    links = [pltpu.SemaphoreType.DMA((2,)), pltpu.SemaphoreType.DMA((1,))]
    loading = pltpu.SemaphoreType.DMA((steps,))
    held = [
        vmem((steps, 59, CHUNK)), vmem((9, blocks, LANES)),
        pltpu.VMEM((6 * blocks, 2 * LANES), jnp.bfloat16), vmem((9, 32, LANES)), vmem((9, 32, LANES)),
    ]
    outside = pl.BlockSpec(memory_space=pltpu.HBM)

    def integers(*shape):
        return pltpu.VMEM(shape, jnp.int32)

    returned, from_send = pl.pallas_call(
        functools.partial(train_kernel, half=half),
        out_shape=(f32(*packet), jax.ShapeDtypeStruct((blocks, LANES), jnp.int32)),
        in_specs=[scalars(), outside, whole(), whole(), whole(), whole()],
        out_specs=(whole(), whole()),
        scratch_shapes=[
            *held, vmem((36, 32, LANES)), vmem((32, 32, 8, LANES)), vmem((32, 32, 8, LANES)),
            vmem((36, 32, LANES)), vmem((24, 8, LANES)), vmem((2, *packet)), vmem(packet),
            integers(LANES, LANES), integers(32, LANES), integers(32, LANES), vmem((3, 64, LANES)),
            loading, *links, *links,
        ],
        compiler_params=linked(1),
        name="train",
    )(camera, gauss_params, slots_first, lists_first, tiles_first[None], jnp.transpose(targets, (1, 0, 2)))
    wide = 2
    block = pl.BlockSpec((64, wide * CHUNK), lambda i: (0, i))
    new_params, new_first, new_second = pl.pallas_call(
        functools.partial(update_kernel, half=half),
        grid=(steps // wide,),
        out_shape=(f32(59, local), f32(59, local), f32(59, local)),
        in_specs=[
            scalars(),
            pl.BlockSpec((64, LANES), lambda i: (0, 0)),
            pl.BlockSpec(packet, lambda i: (0, 0, 0)),
            pl.BlockSpec((8 * wide, LANES), lambda i: (i, 0)),
            block, block, block,
        ],
        out_specs=(block, block, block),
        scratch_shapes=[vmem((9, 32, LANES)), vmem((15, 8, LANES))],
        compiler_params=streamed,
        name="update",
    )(camera, jnp.asarray(rate_values()), returned, from_send, gauss_params, adam_first, adam_second)
    image = pl.pallas_call(
        functools.partial(render_kernel, half=half),
        out_shape=f32(3, TILE_DEV, 256),
        in_specs=[scalars(), outside, whole(), whole(), whole()],
        out_specs=whole(),
        scratch_shapes=[
            *held, vmem((36, 32, LANES)), vmem(packet), vmem(packet),
            integers(LANES, LANES), integers(32, LANES), loading, *links,
        ],
        compiler_params=linked(2),
        name="render",
    )(camera, new_params, slots_second, lists_second, tiles_second[None])
    return (new_params, new_first, new_second, jnp.transpose(image, (1, 0, 2)))


def solution(mesh):
    split = P(None, "dev")
    rows = P("dev", None)
    return jax.shard_map(
        shards,
        mesh=mesh,
        in_specs=(split, split, split, P(), rows, rows, rows, rows, P("dev"), P("dev"), P("dev", None, None)),
        out_specs=(split, split, split, P("dev", None, None)),
        check_vma=False,
    )
```
